32 devices in a mesh: space: 8 (over z, x), mem: 4 (over y, core).
Axes of the slice: x: 2, y: 2, z: 4, core: 2. Of those that a mesh axis runs over, the one named last changes fastest.
Arguments:
- state: float32 [64, 3, 128, 256], P('mem', None, 'space'), may hold values from -6 to 6
- depth: float32 [128, 256], P('space'), may hold values from 0.5 to 2
- obs_cells: int32 [4, 512, 128], P(None, 'space'), may hold values from 0 to 4095, as said below
- obs_weights: float32 [4, 512, 128], P(None, 'space'), may hold values from 0 to 0.5
- owner_map: int32 [512, 1], P('space'), may hold values from 0 to 7; in each aligned block of 64 rows (0 to 63, 64 to 127, ...) at most 16 rows name the same one
- obs_values: float32 [8, 8, 16, 128], P('space'), may hold values from -8 to 8
- obs_precision: float32 [8, 8, 16, 128], P('space'), may hold values from 0.5 to 6
Outputs:
- analysis: float32 [64, 3, 128, 256], P('mem', None, 'space')
The draws below stay inside these ranges and needn't reach their ends.
Inputs may be any that keep to these rules, and one draw needn't show every extreme that they name: The cells of block b lie in the rows of space device b // 64; obs_cells is the offset within those rows. `owner_map`: among the 64 blocks of one space device no owner is named more than 16 times, and in some device one owner is named exactly 16 times.
All inputs are finite; a program needn't handle non-finite values.
Results may differ from the reference program's by a relative error of at most 0.00012.
Values sent between devices are 32-bit elements; how exact they have to be, the bound alone decides.
No kernel may reach another device: no remote copies, remote signals or barrier semaphores. Data moves between devices by JAX's collectives and lax.ppermute only.
A program may use at most 64 MiB of HBM per device.

```python
import math
import jax
import jax.numpy as jnp
import numpy as np
from jax import lax

M = 64
CX = 16
NY = 256
STEPS = 2
OBS_BLK = 128
SRC_BLK = 64
PAIR_CAP = 16
NX = 128
BLOCKS = 512
N_SPACE = 8


def draw_obs_cells(key, part):
    strip = CX * NY
    offsets = jax.random.randint(key, (4, BLOCKS, OBS_BLK), 0, strip)
    offsets = offsets.at[0, 0, 0].set(0)
    offsets = offsets.at[3, BLOCKS - 1, OBS_BLK - 1].set(strip - 1)
    return offsets.astype(jnp.int32)


def draw_obs_precision(key, part):
    shape = (N_SPACE, N_SPACE, PAIR_CAP, OBS_BLK)
    source = jnp.arange(N_SPACE, dtype=jnp.float32)[None, :, None, None] / max(N_SPACE - 1, 1)
    base = jnp.exp(jax.random.uniform(key, shape, jnp.float32, math.log(0.5), math.log(2.0)))
    ramp = 1.0 + 2.0 * source
    return (base * ramp).astype(jnp.float32)


def level_of(own_key, extent, split, low, top_value):
    def one(position, shards_of):
        draws = jax.random.uniform(jax.random.fold_in(jax.random.fold_in(own_key, 6), position), (shards_of,), jnp.float32, low / len(split), top_value / len(split))
        return jnp.repeat(jnp.exp(draws), extent[position] // shards_of).reshape((-1,) + (1,) * (len(extent) - position - 1))

    factor_of = one(*split[0])
    for cut in split[1:]:
        factor_of = factor_of * one(*cut)
    return factor_of


def assign_block(stream_key, own, number, rows, amount, top, limit, slope):
    sequence = jax.random.permutation(stream_key, amount)
    packed, ordinary = load_shares(amount, rows * top, limit, slope, True), load_shares(amount, rows * top, limit, slope, False)
    places = jnp.arange(amount)

    def named(lengths, rotation):
        used = int((lengths > 0).sum())
        fixed = max(1, used // 4)
        moved = fixed + (places - fixed + rotation * (used - fixed)) % max(1, amount - fixed)
        return jnp.zeros((amount,), jnp.int32).at[sequence[jnp.where(places < fixed, places, moved)]].set(jnp.asarray(lengths, jnp.int32))

    lengths = jnp.where(number % 4 == 0, named(packed, number // 4), named(ordinary, number - number // 4 - 1))
    mixed = jax.random.permutation(jax.random.fold_in(own, 3), amount)
    source_of, taker = mixed[0:amount // 2 * 2:2], mixed[1:amount // 2 * 2:2]
    margin = jnp.minimum(lengths[source_of] - 1, limit - lengths[taker]) // 2
    margin = jnp.where((source_of == sequence[0]) | (taker == sequence[0]) | (lengths[taker] == 0), 0, jnp.maximum(margin, 0))
    moved = jax.random.randint(jax.random.fold_in(own, 4), (amount // 2,), 0, 1 << 20) % (margin + 1)
    lengths = lengths.at[source_of].add(-moved).at[taker].add(moved)
    labels = jnp.searchsorted(jnp.cumsum(lengths), jnp.arange(rows * top), side="right").astype(jnp.int32)
    grid = labels.reshape(top, rows).T
    grid = grid[jax.random.permutation(jax.random.fold_in(own, 1), rows)]
    rotation = jax.random.randint(jax.random.fold_in(own, 2), (rows, 1), 0, top)
    return jnp.take_along_axis(grid, (jnp.arange(top)[None, :] + rotation) % top, axis=1)


def load_shares(number_of, total, reach, lean, full):
    portions = [(1 << 20) // math.isqrt(grade ** lean) + 1 for grade in range(1, number_of + 1)]
    largest = reach if full else min(reach, max(-(-total // number_of), total * portions[0] // sum(portions)))
    least = 1 if total - largest >= number_of - 1 else 0
    holding, spare = [largest] + [least] * (number_of - 1), total - largest - least * (number_of - 1)
    while spare > 0:
        free = [i for i in range(1, number_of) if holding[i] < largest] or [i for i in range(1, number_of) if holding[i] < reach]
        mass, left = sum([portions[i] for i in free]), spare
        for i in free:
            more = min(reach - holding[i], max(1, left * portions[i] // mass), spare)
            holding[i] = holding[i] + more
            spare = spare - more
    return np.array(holding)


def centred(own_key, extent, width, most, shards=(), kind=jnp.bfloat16):
    drawn = width * jax.random.normal(own_key, extent, jnp.float32)
    if shards:
        drawn = drawn * level_of(own_key, extent, shards, -0.22, 0.18)
    return jnp.clip(drawn, -most, most).astype(kind)


def setup_inputs(seed: int = 0) -> dict:
    key_list = jax.random.split(jax.random.key(seed), 8)
    state = centred(key_list[0], (M, 3, NX, NY), 1.0, 6.0, ((0, 4), (2, 8)), jnp.float32)
    depth = jnp.clip(jnp.exp(math.log(2.0) - 1.3862944 * jax.random.uniform(key_list[1], (NX, NY), jnp.float32) ** level_of(key_list[1], (NX, NY), ((0, 8),), -0.2, 0.2)), 0.5, 2.0)
    obs_cells = draw_obs_cells(jax.random.fold_in(key_list[7], 71), 0)
    obs_weights = jnp.clip(0.5 * jax.random.uniform(key_list[3], (4, BLOCKS, OBS_BLK), jnp.float32) ** level_of(key_list[3], (4, BLOCKS, OBS_BLK), ((1, 8),), -0.2, 0.2), 0.0, 0.5)
    owner_map_keys = jax.random.split(jax.random.fold_in(key_list[4], 1), BLOCKS // SRC_BLK)
    owner_map_turns = jax.random.permutation(jax.random.fold_in(key_list[4], 3), BLOCKS // SRC_BLK)
    owner_map = jax.vmap(lambda own, number: assign_block(jax.random.fold_in(key_list[4], 2), own, number, SRC_BLK, N_SPACE, 1, PAIR_CAP, 2))(owner_map_keys, owner_map_turns).reshape((BLOCKS, 1))
    obs_values = centred(key_list[5], (N_SPACE, N_SPACE, PAIR_CAP, OBS_BLK), 1.5, 8.0, ((0, 8),), jnp.float32)
    obs_precision = draw_obs_precision(jax.random.fold_in(key_list[7], 71), 0)
    return {"state": state, "depth": depth, "obs_cells": obs_cells, "obs_weights": obs_weights, "owner_map": owner_map, "obs_values": obs_values, "obs_precision": obs_precision}


mass_rate = 0.2
wave_rate = 0.2
turn_rate = 0.1

def diff_rows(field):
    widths = [(0, 0)] * (field.ndim - 2) + [(1, 1), (0, 0)]
    padded = jnp.pad(field, widths)
    return padded[..., 2:, :] - padded[..., :-2, :]

def diff_cols(field):
    return jnp.roll(field, -1, axis=-1) - jnp.roll(field, 1, axis=-1)

def advance(fluid_elevation, zonal_wind, meridional_wind, depth, inside):
    fluid_elevation = (fluid_elevation - mass_rate * (diff_rows(depth * zonal_wind) + diff_cols(depth * meridional_wind))) * inside
    east_new = (zonal_wind - wave_rate * diff_rows(fluid_elevation) + turn_rate * meridional_wind) * inside
    north_new = (meridional_wind - wave_rate * diff_cols(fluid_elevation) - turn_rate * zonal_wind) * inside
    return (fluid_elevation, east_new, north_new)

def gram_terms(values, seen, weight, scale):
    middle = lax.optimization_barrier(jnp.mean(values, axis=0))
    factor = weight * scale
    scaled = (values - middle[None]) * factor[None]
    depart = (seen - middle) * factor
    gram = jnp.einsum('mrk,nrk->mn', scaled, scaled, precision=lax.Precision.HIGHEST)
    proj = jnp.einsum('mrk,rk->m', scaled, depart, precision=lax.Precision.HIGHEST)
    return (gram, proj)

def make_mixing(lower, proj, members):
    eye = jnp.eye(members, dtype=jnp.float32)
    first = lax.linalg.triangular_solve(lower, proj[:, None], left_side=True, lower=True)
    mean_weights = lax.linalg.triangular_solve(lower, first, left_side=True, lower=True, transpose_a=True)[:, 0]
    inverse_lower = lax.linalg.triangular_solve(lower, eye, left_side=True, lower=True)
    spread = math.sqrt(members - 1) * inverse_lower.T
    coef = mean_weights[:, None] + spread
    return coef + (1.0 - lax.optimization_barrier(jnp.sum(coef, axis=0)))[None, :] / members

def block_slots(owners):
    same = (owners[:, :, None] == owners[:, None, :]).astype(jnp.int32)
    order = jnp.arange(owners.shape[1], dtype=jnp.int32)
    earlier = (order[:, None] < order[None, :]).astype(jnp.int32)
    return lax.optimization_barrier(jnp.sum(same * earlier[None], axis=1))

def reference(state, depth, obs_cells, obs_weights, owner_map, obs_values, obs_precision):
    fluid_elevation, zonal_wind, meridional_wind = (state[:, 0], state[:, 1], state[:, 2])
    for step in range(STEPS):
        fluid_elevation, zonal_wind, meridional_wind = advance(fluid_elevation, zonal_wind, meridional_wind, depth, jnp.float32(1.0))
    prior_fields = jnp.stack([fluid_elevation, zonal_wind, meridional_wind], axis=1)
    flat = fluid_elevation.reshape(M, NX * NY)
    source = jnp.arange(BLOCKS, dtype=jnp.int32) // SRC_BLK
    cells = (obs_cells + (source * (CX * NY))[None, :, None]).astype(jnp.int32)

    def predict(row):
        return lax.optimization_barrier(jnp.sum(obs_weights * row[cells], axis=0))
    predicted = lax.map(predict, flat)
    owners = owner_map[:, 0]
    slots = block_slots(owners.reshape(N_SPACE, SRC_BLK)).reshape(BLOCKS)
    seen = obs_values[owners, source, slots]
    weight = obs_precision[owners, source, slots]
    scale = math.sqrt((M - 1) / (BLOCKS * OBS_BLK))
    gram, proj = gram_terms(predicted, seen, weight, scale)
    system = (M - 1) * jnp.eye(M, dtype=jnp.float32) + gram
    lower = jnp.linalg.cholesky(system)
    transform_weights = make_mixing(lower, proj, M)
    return jnp.einsum('gv,gpbo->vpbo', transform_weights, prior_fields, precision=lax.Precision.HIGHEST)
```

```python
import functools
import math

import jax
import jax.numpy as jnp
from jax import lax
from jax.experimental import pallas as pl
from jax.experimental.pallas import tpu as pltpu
from jax.sharding import PartitionSpec as P

STEPS = 2
RIM = 2 * STEPS

mass_rate = 0.2
wave_rate = 0.2
turn_rate = 0.1

VMEM = pl.BlockSpec(memory_space=pltpu.VMEM)
SMEM = pl.BlockSpec(memory_space=pltpu.SMEM)
F32 = jnp.float32
BF16 = jnp.bfloat16


def diff_cols(field):
    width = field.shape[-1]
    return pltpu.roll(field, width - 1, 1) - pltpu.roll(field, 1, 1)


def forecast_kernel(inside, state, above, below, depth, height_out, wind_out, h, u, v, flux):
    members, _, rows, cols = state.shape
    total = rows + 2 * RIM
    deep = [above[3 * members, t : t + 1] for t in range(RIM)]
    deep += [depth[t : t + 1] for t in range(rows)]
    deep += [below[3 * members, t : t + 1] for t in range(RIM)]
    deep = [jnp.broadcast_to(d, (members, cols)) for d in deep]

    for field, dst in enumerate((h, u, v)):
        for t in range(RIM):
            dst[t] = above[field * members : (field + 1) * members, t, :]
            dst[RIM + rows + t] = below[field * members : (field + 1) * members, t, :]
        for t in range(rows):
            dst[RIM + t] = state[:, field, t, :]

    for step in range(STEPS):
        low, high = 2 * step, total - 2 * step
        for e in range(low, high):
            flux[e] = deep[e] * u[e]
        for e in range(low + 1, high - 1):
            new = h[e] - mass_rate * (flux[e + 1] - flux[e - 1] + diff_cols(deep[e] * v[e]))
            if e < RIM:
                new = new * inside[0]
            elif e >= RIM + rows:
                new = new * inside[1]
            h[e] = new
        for e in range(low + 2, high - 2):
            east, north, mid = u[e], v[e], h[e]
            u[e] = east - wave_rate * (h[e + 1] - h[e - 1]) + turn_rate * north
            v[e] = north - wave_rate * diff_cols(mid) - turn_rate * east
    for t in range(rows):
        height_out[t] = h[RIM + t]
        wind_out[0, t] = u[RIM + t]
        wind_out[1, t] = v[RIM + t]


def forecast(inside, state, above, below, depth):
    members, _, rows, cols = state.shape
    total = rows + 2 * RIM
    return pl.pallas_call(
        forecast_kernel,
        out_shape=(
            jax.ShapeDtypeStruct((rows, members, cols), F32),
            jax.ShapeDtypeStruct((2, rows, members, cols), F32),
        ),
        in_specs=[SMEM, VMEM, VMEM, VMEM, VMEM],
        out_specs=(VMEM, VMEM),
        scratch_shapes=[pltpu.VMEM((total, members, cols), F32)] * 4,
        compiler_params=pltpu.CompilerParams(vmem_limit_bytes=32 * 1024 * 1024),
        name="forecast",
    )(inside, state, above, below, depth)


def gram_kernel(scale, count_mem, place, owners, *refs):
    pieces = refs[:count_mem]
    cells, weights, got, out, split, seen, factor, lined, used = refs[count_mem:]
    rows, members, cols = pieces[0].shape
    total = members * count_mem
    points, blocks, width = cells.shape
    all_blocks = owners.shape[0]
    slots = got.shape[1] // 2
    quarter = place[0]

    for owner in range(got.shape[0]):
        used[owner] = 0

    def dispatch(b, carry):
        owner = owners[b]
        slot = used[owner]
        used[owner] = slot + 1
        local = b - quarter * blocks

        @pl.when((local >= 0) & (local < blocks))
        def _():
            seen[pl.ds(local, 1)] = got[owner, pl.ds(slot, 1)]
            factor[pl.ds(local, 1)] = got[owner, pl.ds(slot + slots, 1)] * scale

        return carry

    lax.fori_loop(0, all_blocks, dispatch, 0)

    for k, piece in enumerate(pieces):
        who = lax.bitwise_xor(quarter, k)
        for r in range(rows):
            x = piece[r]
            high = x.astype(BF16)
            low = (x - high.astype(F32)).astype(BF16)
            at = pl.ds(pl.multiple_of(r * total + who * members, members), members)
            split[at, 0:cols] = high
            split[at, cols : 2 * cols] = low

    lined[total : 2 * total] = jnp.zeros((total, blocks * width), F32)

    def block(b, carry):
        result = None
        for half in range(points // 2):
            cell = jnp.concatenate(
                [cells[2 * half, pl.ds(b, 1), :], cells[2 * half + 1, pl.ds(b, 1), :]], axis=1
            )
            share = jnp.concatenate(
                [weights[2 * half, pl.ds(b, 1), :], weights[2 * half + 1, pl.ds(b, 1), :]], axis=1
            )
            row = cell // cols
            col = jnp.broadcast_to(cell - row * cols, (cols, 2 * width))
            here = lax.broadcasted_iota(jnp.int32, (cols, 2 * width), 0) == col
            pick = jnp.where(here, 1.0, 0.0).astype(BF16)
            lines = jnp.dot(
                split[...], jnp.concatenate([pick, pick], axis=0), preferred_element_type=F32
            )
            for r in range(rows):
                term = lines[r * total : (r + 1) * total] * jnp.where(row == r, share, 0.0)
                term = term[:, :width] + term[:, width:]
                result = term if result is None else result + term
        middle = jnp.sum(result, axis=0, keepdims=True) * (1.0 / total)
        much = factor[pl.ds(b, 1)]
        at = pl.ds(pl.multiple_of(b * width, width), width)
        lined[0:total, at] = (result - middle) * much
        lined[total : total + 1, at] = (seen[pl.ds(b, 1)] - middle) * much
        return carry

    lax.fori_loop(0, blocks, block, 0, unroll=2)

    x = lined[...]
    gram = lax.dot_general(
        x, x, (((1,), (1,)), ((), ())), precision=lax.Precision.HIGHEST, preferred_element_type=F32
    )
    packed = pack_gram(gram, total)
    for d in range(out.shape[0]):
        out[d] = packed


def pack_gram(gram, total):
    half, quarter = total // 2, total // 4
    span = 2 * total
    top, low = gram[0:half], gram[half:total]
    lane = lax.broadcasted_iota(jnp.int32, (half, span), 1)
    line = lax.broadcasted_iota(jnp.int32, (half, span), 0)
    both = jnp.where(lane <= line, top, pltpu.roll(low, span - half, 1))
    wide = jnp.where(lane < half, both, pltpu.roll(low, half, 1))
    lane_q = lane[0:quarter]
    body = jnp.where(lane_q < total, wide[0:quarter], pltpu.roll(wide[quarter:half], total, 1))
    diag = jnp.sum(jnp.where(lane == line + half, low, 0.0), axis=0, keepdims=True)
    lane_1 = lane[0:8]
    tail = jnp.where(
        lane_1 < total, gram[total : total + 8], pltpu.roll(jnp.broadcast_to(diag, (8, span)), half, 1)
    )
    return jnp.concatenate([body, tail], axis=0)


def unpack_gram(packed, total):
    half, quarter = total // 2, total // 4
    span = 2 * total
    body, tail = packed[0:quarter], packed[quarter : quarter + 1]
    wide = jnp.concatenate([body, pltpu.roll(body, total, 1)], axis=0)
    low = pltpu.roll(wide, span - half, 1)
    lane = lax.broadcasted_iota(jnp.int32, (half, span), 1)
    line = lax.broadcasted_iota(jnp.int32, (half, span), 0)
    first = lane < half
    stacked = jnp.concatenate(
        [jnp.where(first, wide, 0.0), jnp.where(first, low, 0.0), jnp.zeros((total, span), F32)], axis=0
    )
    turned = stacked.T[0:half]
    top = jnp.where(first & (lane <= line), wide, turned)
    diag = pltpu.roll(jnp.broadcast_to(tail, (half, span)), span - half, 1)
    corner = jnp.where(lane > line, wide, turned)
    corner = pltpu.roll(jnp.where(first, corner, 0.0), half, 1)
    corner = jnp.where(lane == line + half, diag, corner)
    bottom = jnp.where(first, low, corner)
    return jnp.concatenate([top, bottom], axis=0), tail


def analysis_kernel(count_mem, place, sums, *refs):
    heights = refs[:count_mem]
    winds = refs[count_mem : 2 * count_mem]
    out, lower, stack = refs[2 * count_mem :]
    rows, members, cols = heights[0].shape
    total = members * count_mem
    span = 2 * total
    quarter = place[0]

    packed = sums[0]
    for d in range(1, sums.shape[0]):
        packed = packed + sums[d]
    system, proj = unpack_gram(packed, total)
    lane = lax.broadcasted_iota(jnp.int32, (total, span), 1)
    line = lax.broadcasted_iota(jnp.int32, (total, span), 0)
    work = jnp.where(
        lane < total,
        system + jnp.where(lane == line, float(total - 1), 0.0),
        jnp.where(lane == line + total, 1.0, 0.0),
    )
    tiles = [work[8 * g : 8 * g + 8] for g in range(total // 8)]
    below = lax.broadcasted_iota(jnp.int32, (8, span), 0)
    for k in range(total):
        g, s = k // 8, k % 8
        pivot = jnp.broadcast_to(tiles[g][s : s + 1], (8, span))
        scaled = pivot / jnp.broadcast_to(pivot[:, k : k + 1], (8, span))
        for t in range(g, total // 8):
            if t == g and s == 7:
                continue
            column = jnp.broadcast_to(tiles[t][:, k : k + 1], (8, span))
            if t == g:
                column = jnp.where(below > s, column, 0.0)
            tiles[t] = tiles[t] - column * scaled
    work = jnp.concatenate(tiles, axis=0)
    diag = jnp.sum(jnp.where(lane == line, work, 0.0), axis=1, keepdims=True)
    inverse = jnp.where(lane < total, pltpu.roll(work, total, 1), 0.0) / jnp.sqrt(diag)
    first = jnp.sum(jnp.where(lane < total, inverse * proj, 0.0), axis=1, keepdims=True)
    mean_weights = jnp.sum(inverse * first, axis=0, keepdims=True)
    lower[...] = inverse
    mine = lower[pl.ds(pl.multiple_of(quarter * members, members), members)]
    coef = mean_weights + math.sqrt(total - 1) * mine
    short = lane[0:members]
    coef = jnp.where(short < total, coef, 0.0)
    mixing = coef + (1.0 - jnp.sum(coef, axis=1, keepdims=True)) * (1.0 / total)
    mixing = mixing[:, 0:total]
    high = mixing.astype(BF16)
    low = (mixing - high.astype(F32)).astype(BF16)
    left = jnp.concatenate([high, high, low], axis=1)

    for field in range(3):
        for r in range(rows):
            for k in range(count_mem):
                who = lax.bitwise_xor(quarter, k)
                x = heights[k][r] if field == 0 else winds[k][field - 1, r]
                upper = x.astype(BF16)
                rest = (x - upper.astype(F32)).astype(BF16)
                at = pl.multiple_of(who * members, members)
                stack[r % 2, pl.ds(at, members), :] = upper
                stack[r % 2, pl.ds(at + total, members), :] = rest
                stack[r % 2, pl.ds(at + 2 * total, members), :] = upper
            out[:, field, r, :] = jnp.dot(left, stack[r % 2], preferred_element_type=F32)


def swap(x, axis, bit):
    count = lax.axis_size(axis)
    return lax.ppermute(x, axis, [(i, i ^ bit) for i in range(count)])


def local(state, depth, obs_cells, obs_weights, owner_map, obs_values, obs_precision):
    members, fields, rows, cols = state.shape
    count = lax.axis_size("space")
    count_mem = lax.axis_size("mem")
    place = lax.axis_index("space")
    quarter = lax.axis_index("mem").astype(jnp.int32).reshape(1)
    total = members * count_mem
    blocks, width = obs_cells.shape[1:]
    share = blocks // count_mem
    scale = math.sqrt((total - 1) / (count * blocks * width))

    def rim(at):
        strip = lax.slice_in_dim(state, at, at + RIM, axis=2)
        strip = strip.transpose(1, 0, 2, 3).reshape(fields * members, RIM, cols)
        return jnp.concatenate([strip, depth[None, at : at + RIM]], axis=0)

    ends = count - 1
    above = lax.ppermute(rim(rows - RIM), "space", [(i, i + 1) for i in range(ends)])
    below = lax.ppermute(rim(0), "space", [(i + 1, i) for i in range(ends)])
    inside = jnp.stack([place > 0, place < ends]).astype(F32)
    held = jnp.concatenate([obs_values[0], obs_precision[0]], axis=1)
    got = lax.all_to_all(held, "space", split_axis=0, concat_axis=0, tiled=True)

    height, wind = forecast(inside, state, above, below, depth)
    bits = [1 << i for i in range(count_mem.bit_length() - 1)]
    heights = {0: height}
    winds = {0: wind}
    for bit in reversed(bits):
        for k in list(heights):
            heights[k ^ bit] = swap(heights[k], "mem", bit)
        for k in list(winds):
            winds[k ^ bit] = swap(winds[k], "mem", bit)
    heights = [heights[k] for k in range(count_mem)]
    winds = [winds[k] for k in range(count_mem)]

    spread = total // 4 + 8
    devices = count * count_mem
    sent = pl.pallas_call(
        functools.partial(gram_kernel, scale, count_mem),
        out_shape=jax.ShapeDtypeStruct((devices, spread, 2 * total), F32),
        grid_spec=pltpu.PrefetchScalarGridSpec(
            num_scalar_prefetch=2,
            grid=(1,),
            in_specs=[pl.BlockSpec((rows, members, cols), lambda i, q, o: (0, 0, 0))] * count_mem
            + [pl.BlockSpec((obs_cells.shape[0], share, width), lambda i, q, o: (0, q[0], 0))] * 2
            + [pl.BlockSpec(got.shape, lambda i, q, o: (0, 0, 0))],
            out_specs=pl.BlockSpec((devices, spread, 2 * total), lambda i, q, o: (0, 0, 0)),
            scratch_shapes=[
                pltpu.VMEM((rows * total, 2 * cols), BF16),
                pltpu.VMEM((share, width), F32),
                pltpu.VMEM((share, width), F32),
                pltpu.VMEM((2 * total, share * width), F32),
                pltpu.SMEM((count,), jnp.int32),
            ],
        ),
        compiler_params=pltpu.CompilerParams(vmem_limit_bytes=48 * 1024 * 1024),
        name="gram",
    )(quarter, owner_map[:, 0], *heights, obs_cells, obs_weights, got)
    sums = lax.all_to_all(sent, ("space", "mem"), split_axis=0, concat_axis=0, tiled=True)

    return pl.pallas_call(
        functools.partial(analysis_kernel, count_mem),
        out_shape=jax.ShapeDtypeStruct(state.shape, F32),
        in_specs=[SMEM, VMEM] + [VMEM] * (2 * count_mem),
        out_specs=VMEM,
        scratch_shapes=[
            pltpu.VMEM((total, 2 * total), F32),
            pltpu.VMEM((2, 3 * total, cols), BF16),
        ],
        compiler_params=pltpu.CompilerParams(vmem_limit_bytes=48 * 1024 * 1024),
        name="analysis",
    )(quarter, sums, *heights, *winds)


def solution(mesh):
    return jax.shard_map(
        local,
        mesh=mesh,
        in_specs=(
            P("mem", None, "space", None),
            P("space", None),
            P(None, "space", None),
            P(None, "space", None),
            P("space", None),
            P("space", None, None, None),
            P("space", None, None, None),
        ),
        out_specs=P("mem", None, "space", None),
        check_vma=False,
    )
```

```python
import functools
import math

import jax
import jax.numpy as jnp
from jax import lax
from jax.experimental import pallas as pl
from jax.experimental.pallas import tpu as pltpu
from jax.sharding import PartitionSpec as P

mass_rate = 0.2
wave_rate = 0.2
turn_rate = 0.1

VMEM = pl.BlockSpec(memory_space=pltpu.VMEM)
SMEM = pl.BlockSpec(memory_space=pltpu.SMEM)
F32 = jnp.float32
BF16 = jnp.bfloat16


def diff_cols(field):
    width = field.shape[-1]
    return pltpu.roll(field, width - 1, 1) - pltpu.roll(field, 1, 1)


def edge_kernel(peers, state, depth, values, precision, above, below, *held):
    members, _, rows, cols = state.shape
    width = values.shape[-1]
    for out, sign, at in ((above, 1.0, range(4)), (below, -1.0, range(rows - 1, rows - 5, -1))):
        deep = [jnp.broadcast_to(depth[t : t + 1], (members, cols)) for t in at]
        h = [state[:, 0, t, :] for t in at]
        u = [state[:, 1, t, :] for t in at]
        v = [state[:, 2, t, :] for t in at]
        flux = [d * e for d, e in zip(deep, u)]
        first = h[0] - mass_rate * (sign * flux[1] + diff_cols(deep[0] * v[0]))
        second, third = (
            h[i] - mass_rate * (sign * (flux[i + 1] - flux[i - 1]) + diff_cols(deep[i] * v[i]))
            for i in (1, 2)
        )
        east = u[0] - wave_rate * sign * second + turn_rate * v[0]
        east_next = u[1] - wave_rate * sign * third + turn_rate * v[1]
        north = v[0] - turn_rate * u[0] - wave_rate * diff_cols(first)
        twice = first - mass_rate * (
            sign * deep[1] * (east_next + sign * wave_rate * first) + diff_cols(deep[0] * north)
        )
        for i, part in enumerate((flux[0], first, east, twice)):
            out[i * members : (i + 1) * members] = part
        out[4 * members : 4 * members + 8] = jnp.concatenate(
            [deep[0][0:1], deep[1][0:1], jnp.zeros((6, cols), F32)], axis=0
        )
    for j, out in enumerate(held):
        peer = lax.bitwise_xor(lax.axis_index("space"), peers * lax.axis_index("mem") + j)
        out[:, 0:width] = values[0, peer]
        out[:, width : 2 * width] = precision[0, peer]


def edges(peers, state, depth, values, precision):
    members, _, _, cols = state.shape
    rim = jax.ShapeDtypeStruct((4 * members + 8, cols), F32)
    held = jax.ShapeDtypeStruct((values.shape[2], cols), F32)
    return pl.pallas_call(
        functools.partial(edge_kernel, peers),
        out_shape=(rim, rim) + (held,) * peers,
        in_specs=[VMEM] * 4,
        out_specs=(VMEM,) * (2 + peers),
        name="edges",
    )(state, depth, values, precision)


def forecast_kernel(last, state, depth, above, below, *refs):
    held = refs[:-6]
    height_out, wind_out, h, u, v, flux = refs[-6:]
    members, _, rows, cols = state.shape
    slots = held[0].shape[0]
    deep = [jnp.broadcast_to(depth[t : t + 1], (members, cols)) for t in range(rows)]
    sides = []
    place = lax.axis_index("space")
    for ref, sign, edge, inside in (
        (above, -1.0, 0, place > 0),
        (below, 1.0, rows - 1, place < last),
    ):
        parts = [ref[i * members : (i + 1) * members] for i in range(4)]
        deeps = [
            jnp.broadcast_to(ref[4 * members + i : 4 * members + i + 1], (members, cols))
            for i in range(2)
        ]
        sides.append((parts, deeps, sign, edge, inside.astype(F32)))

    def outer(edge):
        return 0 if edge == 0 else rows + 1

    for t in range(rows):
        h[t + 1] = state[:, 0, t, :]
        u[t] = state[:, 1, t, :]
        v[t] = state[:, 2, t, :]
        flux[t + 1] = deep[t] * u[t]
    deltas = []
    for (first_flux, _, _, _), _, sign, edge, _ in sides:
        deltas.append(sign * mass_rate * flux[edge + 1])
        flux[outer(edge)] = first_flux

    def new_heights():
        for t in range(rows):
            h[t + 1] = h[t + 1] - mass_rate * (flux[t + 2] - flux[t] + diff_cols(deep[t] * v[t]))

    def new_winds(put):
        for t in range(rows):
            east, north = u[t], v[t]
            put(
                t,
                east - wave_rate * (h[t + 2] - h[t]) + turn_rate * north,
                north - wave_rate * diff_cols(h[t + 1]) - turn_rate * east,
            )

    def keep(t, east, north):
        u[t], v[t] = east, north
        flux[t + 1] = deep[t] * east

    def emit(t, east, north):
        wind_out[0, t] = east
        wind_out[1, t] = north

    new_heights()
    for delta, ((_, first, east, _), deeps, sign, edge, inside) in zip(deltas, sides):
        h[outer(edge)] = (first + delta) * inside
        flux[outer(edge)] = deeps[0] * (east + sign * wave_rate * h[edge + 1])
    new_winds(keep)
    rims = []
    for delta, ((_, _, _, twice), deeps, sign, edge, inside) in zip(deltas, sides):
        turned = wave_rate * diff_cols(deeps[0] * diff_cols(delta))
        change = wave_rate * deeps[1] * delta - sign * flux[edge + 1] - turned
        rims.append((edge, (twice + delta - mass_rate * change) * inside))
    new_heights()
    for edge, rim in rims:
        h[outer(edge)] = rim
    new_winds(emit)
    for t in range(rows):
        height_out[t] = h[t + 1]
    for j, piece in enumerate(held):
        at = j * slots
        height_out[rows + at // members, at % members : at % members + slots, :] = piece[...]


def forecast(last, state, depth, above, below, held):
    members, _, rows, cols = state.shape
    extra = -(-len(held) * held[0].shape[0] // members)
    return pl.pallas_call(
        functools.partial(forecast_kernel, last),
        out_shape=(
            jax.ShapeDtypeStruct((rows + extra, members, cols), F32),
            jax.ShapeDtypeStruct((2, rows, members, cols), F32),
        ),
        in_specs=[VMEM] * (4 + len(held)),
        out_specs=(VMEM, VMEM),
        scratch_shapes=[
            pltpu.VMEM((rows + 2, members, cols), F32),
            pltpu.VMEM((rows, members, cols), F32),
            pltpu.VMEM((rows, members, cols), F32),
            pltpu.VMEM((rows + 2, members, cols), F32),
        ],
        compiler_params=pltpu.CompilerParams(vmem_limit_bytes=32 * 1024 * 1024),
        name="forecast",
    )(state, depth, above, below, *held)


def interpolate(pieces, cells, weights, split, put):
    rows = split.shape[0] // (len(pieces) * pieces[0].shape[1])
    _, members, cols = pieces[0].shape
    total = members * len(pieces)
    points, blocks, width = cells.shape
    quarter = lax.axis_index("mem")
    blocks = blocks // lax.axis_size("mem")
    for k, piece in enumerate(pieces):
        who = lax.bitwise_xor(lax.rem(quarter, len(pieces)), k)
        for r in range(rows):
            x = piece[r]
            high = x.astype(BF16)
            low = (x - high.astype(F32)).astype(BF16)
            at = pl.ds(pl.multiple_of(r * total + who * members, members), members)
            split[at, 0:cols] = high
            split[at, cols : 2 * cols] = low

    def block(b, carry):
        result = None
        line = pl.ds(quarter * blocks + b, 1)
        for half in range(points // 2):
            cell = jnp.concatenate(
                [cells[2 * half, line, :], cells[2 * half + 1, line, :]], axis=1
            )
            share = jnp.concatenate(
                [weights[2 * half, line, :], weights[2 * half + 1, line, :]], axis=1
            )
            row = cell // cols
            col = jnp.broadcast_to(cell - row * cols, (cols, 2 * width))
            here = lax.broadcasted_iota(jnp.int32, (cols, 2 * width), 0) == col
            pick = jnp.where(here, 1.0, 0.0).astype(BF16)
            lines = jnp.dot(
                split[...], jnp.concatenate([pick, pick], axis=0), preferred_element_type=F32
            )
            for r in range(rows):
                term = lines[r * total : (r + 1) * total] * jnp.where(row == r, share, 0.0)
                term = term[:, :width] + term[:, width:]
                result = term if result is None else result + term
        put(b, result)
        return carry

    lax.fori_loop(0, blocks, block, 0, unroll=2)


def predict_kernel(count, *refs):
    pieces = refs[:count]
    cells, weights, out, split = refs[count:]

    def put(b, result):
        out[b] = result

    interpolate(pieces, cells, weights, split, put)


def gram_kernel(scale, count, count_mem, owners, *refs):
    pieces = refs[:count_mem]
    early = refs[count_mem : count_mem + count_mem // count - 1]
    cells, weights, out, split, got, seen, factor, lined, used = refs[-9:]
    _, members, cols = pieces[0].shape
    total = members * count_mem
    part = members * count
    rows = split.shape[0] // part
    all_blocks = owners.shape[0]
    blocks, width = all_blocks // count_mem, cells.shape[2]
    slots = got.shape[1]
    peers = got.shape[0] // count_mem
    space, quarter = lax.axis_index("space"), lax.axis_index("mem")

    for owner in range(got.shape[0]):
        used[owner] = 0
    for k, piece in enumerate(pieces):
        who = lax.bitwise_xor(quarter, k)
        for j in range(peers):
            at = j * slots
            got[who * peers + j] = piece[
                rows + at // members, at % members : at % members + slots, :
            ]

    def dispatch(b, carry):
        owner = owners[b]
        slot = used[owner]
        used[owner] = slot + 1
        at = b - quarter * blocks

        @pl.when((at >= 0) & (at < blocks))
        def _():
            line = got[lax.bitwise_xor(owner, space), pl.ds(slot, 1)]
            seen[pl.ds(at, 1)] = line[:, 0:width]
            factor[pl.ds(at, 1)] = line[:, width : 2 * width] * scale

        return carry

    lax.fori_loop(0, all_blocks, dispatch, 0)

    mine = quarter // count
    groups = count_mem // count
    for g in range(groups - 1):
        base = pl.multiple_of(lax.bitwise_xor(mine, g) * part, part)
        for b in range(blocks):
            lined[pl.ds(base, part), b * width : (b + 1) * width] = early[g][b]
    final = pl.multiple_of(lax.bitwise_xor(mine, groups - 1) * part, part)

    def put(b, result):
        at = pl.ds(pl.multiple_of(b * width, width), width)
        lined[pl.ds(final, part), at] = result

    interpolate(pieces[count_mem - count :], cells, weights, split, put)
    lined[total : 2 * total] = jnp.zeros((total, blocks * width), F32)
    for b in range(blocks):
        at = pl.ds(b * width, width)
        values = lined[0:total, at]
        much = factor[b : b + 1]
        middle = jnp.sum(values, axis=0, keepdims=True) * (1.0 / total)
        lined[0:total, at] = (values - middle) * much
        lined[total : total + 1, at] = (seen[b : b + 1] - middle) * much

    x = lined[...]
    gram = lax.dot_general(
        x, x, (((1,), (1,)), ((), ())), precision=lax.Precision.HIGHEST, preferred_element_type=F32
    )
    packed = pack_gram(gram, total)
    spread = out.shape[1]
    for d in range(out.shape[0]):
        for r in range(spread):
            out[d, r] = packed[r : r + 1]


def pack_gram(gram, total):
    half, quarter = total // 2, total // 4
    span = 2 * total
    top, low = gram[0:half], gram[half:total]
    lane = lax.broadcasted_iota(jnp.int32, (half, span), 1)
    line = lax.broadcasted_iota(jnp.int32, (half, span), 0)
    both = jnp.where(lane <= line, top, pltpu.roll(low, span - half, 1))
    wide = jnp.where(lane < half, both, pltpu.roll(low, half, 1))
    lane_q = lane[0:quarter]
    body = jnp.where(lane_q < total, wide[0:quarter], pltpu.roll(wide[quarter:half], total, 1))
    diag = jnp.sum(jnp.where(lane == line + half, low, 0.0), axis=0, keepdims=True)
    lane_1 = lane[0:8]
    tail = jnp.where(
        lane_1 < total, gram[total : total + 8], pltpu.roll(jnp.broadcast_to(diag, (8, span)), half, 1)
    )
    return jnp.concatenate([body, tail], axis=0)


def unpack_gram(packed, total):
    half, quarter = total // 2, total // 4
    span = 2 * total
    body, tail = packed[0:quarter], packed[quarter : quarter + 1]
    wide = jnp.concatenate([body, pltpu.roll(body, total, 1)], axis=0)
    low = pltpu.roll(wide, span - half, 1)
    lane = lax.broadcasted_iota(jnp.int32, (half, span), 1)
    line = lax.broadcasted_iota(jnp.int32, (half, span), 0)
    first = lane < half
    stacked = jnp.concatenate(
        [jnp.where(first, wide, 0.0), jnp.where(first, low, 0.0), jnp.zeros((total, span), F32)], axis=0
    )
    turned = stacked.T[0:half]
    top = jnp.where(first & (lane <= line), wide, turned)
    diag = pltpu.roll(jnp.broadcast_to(tail, (half, span)), span - half, 1)
    corner = jnp.where(lane > line, wide, turned)
    corner = pltpu.roll(jnp.where(first, corner, 0.0), half, 1)
    corner = jnp.where(lane == line + half, diag, corner)
    bottom = jnp.where(first, low, corner)
    return jnp.concatenate([top, bottom], axis=0), tail


def factor_inverse(system, total):
    span = 2 * total
    lane = lax.broadcasted_iota(jnp.int32, (total, span), 1)
    line = lax.broadcasted_iota(jnp.int32, (total, span), 0)
    work = jnp.where(lane < total, system, jnp.where(lane == line + total, 1.0, 0.0))
    tiles = [work[8 * g : 8 * g + 8] for g in range(total // 8)]
    step = 4
    below = lax.broadcasted_iota(jnp.int32, (8, span), 0)

    def lanes(x, k):
        return jnp.broadcast_to(x[:, k : k + 1], (8, span))

    def lines(x, s):
        return jnp.broadcast_to(x[s : s + 1], (8, span))

    for k in range(0, total, step):
        g, s = k // 8, k % 8
        columns = {t: [lanes(tiles[t], k + i) for i in range(step)] for t in range(g, total // 8)}
        pivots = [lines(tiles[g], s + i) for i in range(step)]
        block = [[lines(columns[g][j], s + i) for j in range(i + 1)] for i in range(step)]
        for j in range(step):
            scale = 1.0 / block[j][j]
            ratio = [None] * step
            for i in range(j + 1, step):
                ratio[i] = block[i][j] * scale
            for i in range(j + 1, step):
                for n in range(j + 1, i + 1):
                    block[i][n] = block[i][n] - ratio[i] * block[n][j]
                pivots[i] = pivots[i] - ratio[i] * pivots[j]
            scaled = pivots[j] * scale
            for t in columns:
                for i in range(j + 1, step):
                    columns[t][i] = columns[t][i] - ratio[i] * columns[t][j]
            for t in columns:
                column = columns[t][j]
                if t == g:
                    if s + j == 7:
                        continue
                    column = jnp.where(below > s + j, column, 0.0)
                tiles[t] = tiles[t] - column * scaled
    work = jnp.concatenate(tiles, axis=0)
    diag = jnp.sum(jnp.where(lane == line, work, 0.0), axis=1, keepdims=True)
    return jnp.where(lane < total, pltpu.roll(work, total, 1), 0.0) / jnp.sqrt(diag)


def mixing_columns(packed, total, members, count_mem, lower):
    span = 2 * total
    quarter = lax.axis_index("mem")
    system, proj = unpack_gram(packed, total)
    lane = lax.broadcasted_iota(jnp.int32, (total, span), 1)
    line = lax.broadcasted_iota(jnp.int32, (total, span), 0)
    inverse = factor_inverse(system + jnp.where(lane == line, float(total - 1), 0.0), total)
    first = jnp.sum(jnp.where(lane < total, inverse * proj, 0.0), axis=1, keepdims=True)
    mean_weights = jnp.sum(inverse * first, axis=0, keepdims=True)
    lower[...] = inverse
    mine = lower[pl.ds(pl.multiple_of(quarter * members, members), members)]
    coef = mean_weights + math.sqrt(total - 1) * mine
    short = lane[0:members]
    coef = jnp.where(short < total, coef, 0.0)
    mixing = coef + (1.0 - jnp.sum(coef, axis=1, keepdims=True)) * (1.0 / total)
    bit = 1
    while bit < count_mem:
        size = bit * members
        turned = jnp.where(
            lax.rem(short // size, 2) == 0, pltpu.roll(mixing, span - size, 1), pltpu.roll(mixing, size, 1)
        )
        swapped = (lax.rem(quarter // bit, 2) == 1).astype(F32)
        mixing = mixing + swapped * (turned - mixing)
        bit *= 2
    return mixing[:, 0:total]


def analysis_kernel(count_mem, sums, *refs):
    heights = refs[:count_mem]
    winds = refs[count_mem : 2 * count_mem]
    out, lower = refs[2 * count_mem :]
    _, members, cols = heights[0].shape
    rows = winds[0].shape[1]
    total = members * count_mem

    packed = sums[0]
    for d in range(1, sums.shape[0]):
        packed = packed + sums[d]
    packed = jnp.concatenate([packed[r] for r in range(packed.shape[0])], axis=0)
    mixing = mixing_columns(packed, total, members, count_mem, lower)
    high = mixing.astype(BF16)
    low = (mixing - high.astype(F32)).astype(BF16)
    left = jnp.concatenate([high, high, low], axis=1)
    for field in range(3):
        for r in range(rows):
            pieces = [heights[k][r] if field == 0 else winds[k][field - 1, r] for k in range(count_mem)]
            upper = [x.astype(BF16) for x in pieces]
            rest = [(x - y.astype(F32)).astype(BF16) for x, y in zip(pieces, upper)]
            stack = jnp.concatenate(upper + rest + upper, axis=0)
            out[:, field, r, :] = jnp.dot(left, stack, preferred_element_type=F32)


def swap(x, axis, bit):
    count = lax.axis_size(axis)
    return lax.ppermute(x, axis, [(i, i ^ bit) for i in range(count)])


def after(x, *others):
    return lax.optimization_barrier((x,) + others)[0]


def cost(flops, size):
    return pl.CostEstimate(flops=flops, bytes_accessed=size, transcendentals=0)


def local(state, depth, obs_cells, obs_weights, owner_map, obs_values, obs_precision):
    members, fields, rows, cols = state.shape
    count = lax.axis_size("space")
    count_mem = lax.axis_size("mem")
    total = members * count_mem
    blocks, width = obs_cells.shape[1:]
    share = blocks // count_mem
    peers = count // count_mem
    scale = math.sqrt((total - 1) / (count * blocks * width))

    to_above, to_below, *held = edges(peers, state, depth, obs_values, obs_precision)
    ends = count - 1
    below = lax.ppermute(to_above, "space", [(i + 1, i) for i in range(ends)])
    above = lax.ppermute(to_below, "space", [(i, i + 1) for i in range(ends)])
    held = [
        lax.ppermute(
            piece,
            ("space", "mem"),
            [
                (s * count_mem + q, (s ^ (peers * q + j)) * count_mem + q)
                for s in range(count)
                for q in range(count_mem)
            ],
        )
        for j, piece in enumerate(held)
    ]
    height, wind = forecast(ends, state, depth, above, below, held)

    group = 2
    early_shape = (share, group * members, width)
    split = pltpu.VMEM((rows * group * members, 2 * cols), BF16)
    params = pltpu.CompilerParams(vmem_limit_bytes=20 * 1024 * 1024)
    flops = 4 * obs_cells.shape[0] * share * width * rows * members * group * cols

    def predict(k):
        return pl.pallas_call(
            functools.partial(predict_kernel, group),
            out_shape=jax.ShapeDtypeStruct(early_shape, F32),
            in_specs=[VMEM] * (group + 2),
            out_specs=VMEM,
            scratch_shapes=[split],
            compiler_params=params,
            cost_estimate=cost(flops, 4 * height.size * group),
            name="predict",
        )(*[heights[i] for i in range(k, k + group)], obs_cells, obs_weights)

    heights = {0: height}
    winds = {0: wind}
    far = [1 << i for i in range(1, count_mem.bit_length() - 1)]
    for bit in far:
        heights[bit] = swap(height, "mem", bit)
    heights[1] = swap(height, "mem", 1)
    early = [predict(0)]
    for bit in far:
        heights[bit] = after(heights[bit], early[0])
        for k in range(1, bit):
            heights[bit + k] = swap(heights[bit], "mem", k) if k == 1 else swap(heights[bit + 1], "mem", k - 1)
    for bit in far:
        winds[bit] = swap(after(wind, heights[bit]), "mem", bit)
    winds[1] = swap(wind, "mem", 1)
    for bit in far:
        for k in range(1, bit):
            winds[bit + k] = swap(winds[bit], "mem", k) if k == 1 else swap(winds[bit + 1], "mem", k - 1)
    early += [predict(k) for k in range(group, count_mem - group, group)]
    heights = [heights[k] for k in range(count_mem)]
    winds = [winds[k] for k in range(count_mem)]

    owners = owner_map[:, 0]
    spread = total // 4 + 1
    devices = count * count_mem
    sent = pl.pallas_call(
        functools.partial(gram_kernel, scale, group, count_mem),
        out_shape=jax.ShapeDtypeStruct((devices, spread, 1, 2 * total), F32),
        in_specs=[SMEM] + [VMEM] * (count_mem + len(early) + 2),
        out_specs=VMEM,
        scratch_shapes=[
            split,
            pltpu.VMEM((count, obs_values.shape[2], cols), F32),
            pltpu.VMEM((share, width), F32),
            pltpu.VMEM((share, width), F32),
            pltpu.VMEM((2 * total, share * width), F32),
            pltpu.SMEM((count,), jnp.int32),
        ],
        compiler_params=params,
        cost_estimate=cost(flops, 4 * height.size * count_mem),
        name="gram",
    )(owners, *heights, *early, obs_cells, obs_weights)
    sums = lax.all_to_all(sent, ("space", "mem"), split_axis=0, concat_axis=0, tiled=True)

    return pl.pallas_call(
        functools.partial(analysis_kernel, count_mem),
        out_shape=jax.ShapeDtypeStruct(state.shape, F32),
        in_specs=[VMEM] * (1 + 2 * count_mem),
        out_specs=VMEM,
        scratch_shapes=[pltpu.VMEM((total, 2 * total), F32)],
        compiler_params=params,
        name="analysis",
    )(sums, *heights, *winds)


def solution(mesh):
    return jax.shard_map(
        local,
        mesh=mesh,
        in_specs=(
            P("mem", None, "space", None),
            P("space", None),
            P(None, "space", None),
            P(None, "space", None),
            P("space", None),
            P("space", None, None, None),
            P("space", None, None, None),
        ),
        out_specs=P("mem", None, "space", None),
        check_vma=False,
    )
```

```python
import functools
import math

import jax
import jax.numpy as jnp
from jax import lax
from jax.experimental import pallas as pl
from jax.experimental.pallas import tpu as pltpu
from jax.sharding import PartitionSpec as P

mass_rate = 0.2
wave_rate = 0.2
turn_rate = 0.1

VMEM = pl.BlockSpec(memory_space=pltpu.VMEM)
SMEM = pl.BlockSpec(memory_space=pltpu.SMEM)
F32 = jnp.float32
BF16 = jnp.bfloat16
PARAMS = pltpu.CompilerParams(vmem_limit_bytes=12 * 1024 * 1024)
FORECAST_FLOPS = 2 * 10**9


def cost(flops, size):
    return pl.CostEstimate(flops=flops, bytes_accessed=size, transcendentals=0)


def diff_cols(field):
    width = field.shape[-1]
    return pltpu.roll(field, width - 1, 1) - pltpu.roll(field, 1, 1)


def edge_kernel(peers, state, depth, values, precision, above, below, *held):
    members, _, rows, cols = state.shape
    width = values.shape[-1]
    for out, sign, at in ((above, 1.0, range(4)), (below, -1.0, range(rows - 1, rows - 5, -1))):
        deep = [jnp.broadcast_to(depth[t : t + 1], (members, cols)) for t in at]
        h = [state[:, 0, t, :] for t in at]
        u = [state[:, 1, t, :] for t in at]
        v = [state[:, 2, t, :] for t in at]
        flux = [d * e for d, e in zip(deep, u)]
        first = h[0] - mass_rate * (sign * flux[1] + diff_cols(deep[0] * v[0]))
        second, third = (
            h[i] - mass_rate * (sign * (flux[i + 1] - flux[i - 1]) + diff_cols(deep[i] * v[i]))
            for i in (1, 2)
        )
        east = u[0] - wave_rate * sign * second + turn_rate * v[0]
        east_next = u[1] - wave_rate * sign * third + turn_rate * v[1]
        north = v[0] - turn_rate * u[0] - wave_rate * diff_cols(first)
        twice = first - mass_rate * (
            sign * deep[1] * (east_next + sign * wave_rate * first) + diff_cols(deep[0] * north)
        )
        for i, part in enumerate((flux[0], first, east, twice)):
            out[i * members : (i + 1) * members] = part
        out[4 * members : 4 * members + 8] = jnp.concatenate(
            [deep[0][0:1], deep[1][0:1], jnp.zeros((6, cols), F32)], axis=0
        )
    for j, out in enumerate(held):
        peer = lax.bitwise_xor(lax.axis_index("space"), peers * lax.axis_index("mem") + j)
        out[:, 0:width] = values[0, peer]
        out[:, width : 2 * width] = precision[0, peer]


def edges(peers, state, depth, values, precision):
    members, _, _, cols = state.shape
    rim = jax.ShapeDtypeStruct((4 * members + 8, cols), F32)
    held = jax.ShapeDtypeStruct((values.shape[2], cols), F32)
    return pl.pallas_call(
        functools.partial(edge_kernel, peers),
        out_shape=(rim, rim) + (held,) * peers,
        in_specs=[VMEM] * 4,
        out_specs=(VMEM,) * (2 + peers),
        name="edges",
    )(state, depth, values, precision)


def forecast_kernel(last, state, depth, above, below, *refs):
    held = refs[:-6]
    height_out, wind_out, h, u, v, flux = refs[-6:]
    members, _, rows, cols = state.shape
    slots = held[0].shape[0]
    deep = [jnp.broadcast_to(depth[t : t + 1], (members, cols)) for t in range(rows)]
    sides = []
    place = lax.axis_index("space")
    for ref, sign, edge, inside in (
        (above, -1.0, 0, place > 0),
        (below, 1.0, rows - 1, place < last),
    ):
        parts = [ref[i * members : (i + 1) * members] for i in range(4)]
        deeps = [
            jnp.broadcast_to(ref[4 * members + i : 4 * members + i + 1], (members, cols))
            for i in range(2)
        ]
        sides.append((parts, deeps, sign, edge, inside.astype(F32)))

    def outer(edge):
        return 0 if edge == 0 else rows + 1

    for t in range(rows):
        h[t + 1] = state[:, 0, t, :]
        u[t] = state[:, 1, t, :]
        v[t] = state[:, 2, t, :]
        flux[t + 1] = deep[t] * u[t]
    deltas = []
    for (first_flux, _, _, _), _, sign, edge, inside in sides:
        deltas.append(sign * mass_rate * flux[edge + 1])
        flux[outer(edge)] = first_flux * inside

    def new_heights():
        for t in range(rows):
            h[t + 1] = h[t + 1] - mass_rate * (flux[t + 2] - flux[t] + diff_cols(deep[t] * v[t]))

    def new_winds(put):
        for t in range(rows):
            east, north = u[t], v[t]
            put(
                t,
                east - wave_rate * (h[t + 2] - h[t]) + turn_rate * north,
                north - wave_rate * diff_cols(h[t + 1]) - turn_rate * east,
            )

    def keep(t, east, north):
        u[t], v[t] = east, north
        flux[t + 1] = deep[t] * east

    def emit(t, east, north):
        wind_out[0, t] = east
        wind_out[1, t] = north

    new_heights()
    for delta, ((_, first, east, _), deeps, sign, edge, inside) in zip(deltas, sides):
        h[outer(edge)] = (first + delta) * inside
        flux[outer(edge)] = inside * deeps[0] * (east + sign * wave_rate * h[edge + 1])
    new_winds(keep)
    rims = []
    for delta, ((_, _, _, twice), deeps, sign, edge, inside) in zip(deltas, sides):
        turned = wave_rate * diff_cols(deeps[0] * diff_cols(delta))
        change = wave_rate * deeps[1] * delta - sign * flux[edge + 1] - turned
        rims.append((edge, (twice + delta - mass_rate * change) * inside))
    new_heights()
    for edge, rim in rims:
        h[outer(edge)] = rim
    new_winds(emit)
    for t in range(rows):
        height_out[t] = h[t + 1]
    for j, piece in enumerate(held):
        at = j * slots
        height_out[rows + at // members, at % members : at % members + slots, :] = piece[...]


def forecast(last, state, depth, above, below, held):
    members, _, rows, cols = state.shape
    extra = -(-len(held) * held[0].shape[0] // members)
    return pl.pallas_call(
        functools.partial(forecast_kernel, last),
        out_shape=(
            jax.ShapeDtypeStruct((rows + extra, members, cols), F32),
            jax.ShapeDtypeStruct((2, rows, members, cols), F32),
        ),
        in_specs=[VMEM] * (4 + len(held)),
        out_specs=(VMEM, VMEM),
        scratch_shapes=[
            pltpu.VMEM((rows + 2, members, cols), F32),
            pltpu.VMEM((rows, members, cols), F32),
            pltpu.VMEM((rows, members, cols), F32),
            pltpu.VMEM((rows + 2, members, cols), F32),
        ],
        compiler_params=PARAMS,
        cost_estimate=cost(FORECAST_FLOPS, 4 * state.size),
        name="forecast",
    )(state, depth, above, below, *held)


def interpolate(pieces, cells, weights, split, put):
    rows = split.shape[0] // (len(pieces) * pieces[0].shape[1])
    _, members, cols = pieces[0].shape
    total = members * len(pieces)
    points, blocks, width = cells.shape
    quarter = lax.axis_index("mem")
    blocks = blocks // lax.axis_size("mem")
    for k, piece in enumerate(pieces):
        who = lax.bitwise_xor(lax.rem(quarter, len(pieces)), k)
        for r in range(rows):
            x = piece[r]
            high = x.astype(BF16)
            low = (x - high.astype(F32)).astype(BF16)
            at = pl.ds(pl.multiple_of(r * total + who * members, members), members)
            split[at, 0:cols] = high
            split[at, cols : 2 * cols] = low

    def block(b, carry):
        result = None
        line = pl.ds(quarter * blocks + b, 1)
        for half in range(points // 2):
            cell = jnp.concatenate(
                [cells[2 * half, line, :], cells[2 * half + 1, line, :]], axis=1
            )
            share = jnp.concatenate(
                [weights[2 * half, line, :], weights[2 * half + 1, line, :]], axis=1
            )
            row = cell // cols
            col = jnp.broadcast_to(cell - row * cols, (cols, 2 * width))
            here = lax.broadcasted_iota(jnp.int32, (cols, 2 * width), 0) == col
            pick = jnp.where(here, 1.0, 0.0).astype(BF16)
            lines = jnp.dot(
                split[...], jnp.concatenate([pick, pick], axis=0), preferred_element_type=F32
            )
            for r in range(rows):
                term = lines[r * total : (r + 1) * total] * jnp.where(row == r, share, 0.0)
                term = term[:, :width] + term[:, width:]
                result = term if result is None else result + term
        put(b, result)
        return carry

    lax.fori_loop(0, blocks, block, 0, unroll=8)


def collect(got, pieces, split):
    _, members, _ = pieces[0].shape
    rows = split.shape[0] // (len(pieces) * members)
    slots = got.shape[1]
    peers = got.shape[0] // len(pieces)
    for k, piece in enumerate(pieces):
        for j in range(peers):
            at = j * slots
            got[k * peers + j] = piece[rows + at // members, at % members : at % members + slots, :]


def predict_kernel(count, owners, *refs):
    pieces = refs[:count]
    cells, weights, out, near, slots, split, used = refs[count:]
    share = slots.shape[0]
    collect(near, pieces, split)
    begin = lax.axis_index("mem") * share
    for owner in range(used.shape[0]):
        used[owner] = 0

    def skip(b, carry):
        used[owners[b]] += 1
        return carry

    lax.fori_loop(0, begin, skip, 0)
    for i in range(share):
        owner = owners[begin + i]
        slots[i] = used[owner]
        used[owner] += 1

    def put(b, result):
        out[b] = result

    interpolate(pieces, cells, weights, split, put)


def gram_kernel(scale, count, count_mem, owners, slots, *refs):
    pieces = refs[:count]
    cells, weights, near, early, out, split, lined, got = refs[count:]
    _, members, cols = pieces[0].shape
    total = members * count_mem
    part = members * count
    blocks, width = slots.shape[0], cells.shape[2]
    quarter = lax.axis_index("mem")
    peers = near.shape[0] // count
    got[0 : near.shape[0]] = near[...]
    collect(got.at[near.shape[0] :], pieces, split)

    mine = quarter // count
    base = pl.multiple_of(mine * part, part)
    final = pl.multiple_of(lax.bitwise_xor(mine, 1) * part, part)

    def put(b, result):
        at = pl.ds(pl.multiple_of(b * width, width), width)
        lined[pl.ds(final, part), at] = result
        lined[pl.ds(base, part), at] = early[b]

    interpolate(pieces, cells, weights, split, put)
    lined[total : 2 * total] = jnp.zeros((total, blocks * width), F32)
    for b in range(blocks):
        apart = lax.bitwise_xor(owners[quarter * blocks + b], lax.axis_index("space"))
        line = got[lax.bitwise_xor(apart, quarter * peers), pl.ds(slots[b], 1)]
        seen, much = line[:, 0:width], line[:, width : 2 * width] * scale
        at = pl.ds(b * width, width)
        values = lined[0:total, at]
        middle = jnp.sum(values, axis=0, keepdims=True) * (1.0 / total)
        lined[0:total, at] = (values - middle) * much
        lined[total : total + 1, at] = (seen - middle) * much

    x = lined[...]
    high = x.astype(BF16)
    low = (x - high.astype(F32)).astype(BF16)
    turned = (((1,), (1,)), ((), ()))
    gram = lax.dot_general(high, high, turned, preferred_element_type=F32)
    cross = lax.dot_general(high, low, turned, preferred_element_type=F32)
    gram = gram + (cross + cross.T)
    packed = pack_gram(gram, total)
    spread = out.shape[1]
    for d in range(out.shape[0]):
        for r in range(spread):
            out[d, r] = packed[r : r + 1]


def pack_gram(gram, total):
    half, quarter = total // 2, total // 4
    span = 2 * total
    top, low = gram[0:half], gram[half:total]
    lane = lax.broadcasted_iota(jnp.int32, (half, span), 1)
    line = lax.broadcasted_iota(jnp.int32, (half, span), 0)
    both = jnp.where(lane <= line, top, pltpu.roll(low, span - half, 1))
    wide = jnp.where(lane < half, both, pltpu.roll(low, half, 1))
    lane_q = lane[0:quarter]
    body = jnp.where(lane_q < total, wide[0:quarter], pltpu.roll(wide[quarter:half], total, 1))
    diag = jnp.sum(jnp.where(lane == line + half, low, 0.0), axis=0, keepdims=True)
    lane_1 = lane[0:8]
    tail = jnp.where(
        lane_1 < total, gram[total : total + 8], pltpu.roll(jnp.broadcast_to(diag, (8, span)), half, 1)
    )
    return jnp.concatenate([body, tail], axis=0)


def unpack_gram(packed, total):
    half, quarter = total // 2, total // 4
    span = 2 * total
    body, tail = packed[0:quarter], packed[quarter : quarter + 1]
    wide = jnp.concatenate([body, pltpu.roll(body, total, 1)], axis=0)
    low = pltpu.roll(wide, span - half, 1)
    lane = lax.broadcasted_iota(jnp.int32, (half, span), 1)
    line = lax.broadcasted_iota(jnp.int32, (half, span), 0)
    first = lane < half
    stacked = jnp.concatenate(
        [jnp.where(first, wide, 0.0), jnp.where(first, low, 0.0), jnp.zeros((total, span), F32)], axis=0
    )
    turned = stacked.T[0:half]
    top = jnp.where(first & (lane <= line), wide, turned)
    diag = pltpu.roll(jnp.broadcast_to(tail, (half, span)), span - half, 1)
    corner = jnp.where(lane > line, wide, turned)
    corner = pltpu.roll(jnp.where(first, corner, 0.0), half, 1)
    corner = jnp.where(lane == line + half, diag, corner)
    bottom = jnp.where(first, low, corner)
    return jnp.concatenate([top, bottom], axis=0), tail


def factor_inverse(system, total):
    span = 2 * total
    lane = lax.broadcasted_iota(jnp.int32, (total, span), 1)
    line = lax.broadcasted_iota(jnp.int32, (total, span), 0)
    work = jnp.where(lane < total, system, jnp.where(lane == line + total, 1.0, 0.0))
    tiles = [work[8 * g : 8 * g + 8] for g in range(total // 8)]
    step = 8
    below = lax.broadcasted_iota(jnp.int32, (8, span), 0)

    def lanes(x, k):
        return jnp.broadcast_to(x[:, k : k + 1], (8, span))

    def lines(x, s):
        return jnp.broadcast_to(x[s : s + 1], (8, span))

    for k in range(0, total, step):
        g, s = k // 8, k % 8
        columns = {t: [lanes(tiles[t], k + i) for i in range(step)] for t in range(g, total // 8)}
        pivots = [lines(tiles[g], s + i) for i in range(step)]
        block = [[lines(columns[g][j], s + i) for j in range(i + 1)] for i in range(step)]
        for j in range(step):
            scale = 1.0 / block[j][j]
            ratio = [None] * step
            for i in range(j + 1, step):
                ratio[i] = block[i][j] * scale
            for i in range(j + 1, step):
                for n in range(j + 1, i + 1):
                    block[i][n] = block[i][n] - ratio[i] * block[n][j]
                pivots[i] = pivots[i] - ratio[i] * pivots[j]
            scaled = pivots[j] * scale
            for t in columns:
                for i in range(j + 1, step):
                    columns[t][i] = columns[t][i] - ratio[i] * columns[t][j]
            for t in columns:
                column = columns[t][j]
                if t == g:
                    if s + j == 7:
                        continue
                    column = jnp.where(below > s + j, column, 0.0)
                tiles[t] = tiles[t] - column * scaled
    work = jnp.concatenate(tiles, axis=0)
    diag = jnp.sum(jnp.where(lane == line, work, 0.0), axis=1, keepdims=True)
    return jnp.where(lane < total, pltpu.roll(work, total, 1), 0.0) / jnp.sqrt(diag)


def mixing_columns(packed, total, members, count_mem, lower):
    span = 2 * total
    quarter = lax.axis_index("mem")
    system, proj = unpack_gram(packed, total)
    lane = lax.broadcasted_iota(jnp.int32, (total, span), 1)
    line = lax.broadcasted_iota(jnp.int32, (total, span), 0)
    inverse = factor_inverse(system + jnp.where(lane == line, float(total - 1), 0.0), total)
    first = jnp.sum(jnp.where(lane < total, inverse * proj, 0.0), axis=1, keepdims=True)
    mean_weights = jnp.sum(inverse * first, axis=0, keepdims=True)
    lower[...] = inverse
    mine = lower[pl.ds(pl.multiple_of(quarter * members, members), members)]
    coef = mean_weights + math.sqrt(total - 1) * mine
    short = lane[0:members]
    coef = jnp.where(short < total, coef, 0.0)
    mixing = coef + (1.0 - jnp.sum(coef, axis=1, keepdims=True)) * (1.0 / total)
    bit = 1
    while bit < count_mem:
        size = bit * members
        turned = jnp.where(
            lax.rem(short // size, 2) == 0, pltpu.roll(mixing, span - size, 1), pltpu.roll(mixing, size, 1)
        )
        swapped = (lax.rem(quarter // bit, 2) == 1).astype(F32)
        mixing = mixing + swapped * (turned - mixing)
        bit *= 2
    return mixing[:, 0:total]


def analysis_kernel(count_mem, sums, *refs):
    heights = refs[:count_mem]
    winds = refs[count_mem : 2 * count_mem]
    out, lower = refs[2 * count_mem :]
    _, members, cols = heights[0].shape
    rows = winds[0].shape[1]
    total = members * count_mem

    packed = sums[0]
    for d in range(1, sums.shape[0]):
        packed = packed + sums[d]
    packed = jnp.concatenate([packed[r] for r in range(packed.shape[0])], axis=0)
    mixing = mixing_columns(packed, total, members, count_mem, lower)
    high = mixing.astype(BF16)
    low = (mixing - high.astype(F32)).astype(BF16)
    left = jnp.concatenate([high, high, low], axis=1)
    for field in range(3):
        for r in range(rows):
            pieces = [heights[k][r] if field == 0 else winds[k][field - 1, r] for k in range(count_mem)]
            upper = [x.astype(BF16) for x in pieces]
            rest = [(x - y.astype(F32)).astype(BF16) for x, y in zip(pieces, upper)]
            stack = jnp.concatenate(upper + rest + upper, axis=0)
            out[:, field, r, :] = jnp.dot(left, stack, preferred_element_type=F32)


def swap(x, axis, bit):
    count = lax.axis_size(axis)
    return lax.ppermute(x, axis, [(i, i ^ bit) for i in range(count)])


def after(x, *others):
    return lax.optimization_barrier((x,) + others)[0]


def local(state, depth, obs_cells, obs_weights, owner_map, obs_values, obs_precision):
    members, fields, rows, cols = state.shape
    count = lax.axis_size("space")
    count_mem = lax.axis_size("mem")
    total = members * count_mem
    blocks, width = obs_cells.shape[1:]
    share = blocks // count_mem
    scale = math.sqrt((total - 1) / (count * blocks * width))

    peers = count // count_mem

    to_above, to_below, *held = edges(peers, state, depth, obs_values, obs_precision)
    ends = count - 1
    below = lax.ppermute(to_above, "space", [((i + 1) % count, i) for i in range(count)])
    above = lax.ppermute(to_below, "space", [(i, (i + 1) % count) for i in range(count)])
    held = [
        lax.ppermute(
            piece,
            ("space", "mem"),
            [
                (s * count_mem + q, (s ^ (peers * q + j)) * count_mem + q)
                for s in range(count)
                for q in range(count_mem)
            ],
        )
        for j, piece in enumerate(held)
    ]
    height, wind = forecast(ends, state, depth, above, below, held)

    near, far = 1, count_mem // 2
    early_shape = (share, far * members, width)
    split = pltpu.VMEM((rows * far * members, 2 * cols), BF16)
    flops = 4 * obs_cells.shape[0] * share * width * rows * members * far * cols
    owners = owner_map[:, 0]
    heights = {0: height}
    winds = {0: wind}
    heights[far] = swap(height, "mem", far)
    heights[near] = swap(height, "mem", near)
    near_shape = (far * peers, obs_values.shape[2], cols)
    early, first, slots = pl.pallas_call(
        functools.partial(predict_kernel, far),
        out_shape=(
            jax.ShapeDtypeStruct(early_shape, F32),
            jax.ShapeDtypeStruct(near_shape, F32),
            jax.ShapeDtypeStruct((share,), jnp.int32),
        ),
        in_specs=[SMEM] + [VMEM] * (far + 2),
        out_specs=(VMEM, VMEM, SMEM),
        scratch_shapes=[split, pltpu.SMEM((count,), jnp.int32)],
        compiler_params=PARAMS,
        cost_estimate=cost(flops, 4 * height.size * far),
        name="predict",
    )(owners, heights[0], heights[near], obs_cells, obs_weights)
    heights[far] = after(heights[far], early)
    heights[far + near] = swap(heights[far], "mem", near)
    winds[far] = swap(after(wind, heights[far]), "mem", far)
    winds[near] = swap(wind, "mem", near)
    winds[far + near] = swap(winds[far], "mem", near)
    heights = [heights[k] for k in range(count_mem)]
    winds = [winds[k] for k in range(count_mem)]

    spread = total // 4 + 1
    devices = count * count_mem
    sent = pl.pallas_call(
        functools.partial(gram_kernel, scale, far, count_mem),
        out_shape=jax.ShapeDtypeStruct((devices, spread, 1, 2 * total), F32),
        in_specs=[SMEM, SMEM] + [VMEM] * (far + 4),
        out_specs=VMEM,
        scratch_shapes=[
            split,
            pltpu.VMEM((2 * total, share * width), F32),
            pltpu.VMEM((count,) + near_shape[1:], F32),
        ],
        compiler_params=PARAMS,
        cost_estimate=cost(flops, 4 * height.size * count_mem),
        name="gram",
    )(owners, slots, *heights[far:], obs_cells, obs_weights, first, early)
    sums = lax.all_to_all(sent, ("space", "mem"), split_axis=0, concat_axis=0, tiled=True)

    return pl.pallas_call(
        functools.partial(analysis_kernel, count_mem),
        out_shape=jax.ShapeDtypeStruct(state.shape, F32),
        in_specs=[VMEM] * (1 + 2 * count_mem),
        out_specs=VMEM,
        scratch_shapes=[pltpu.VMEM((total, 2 * total), F32)],
        compiler_params=PARAMS,
        name="analysis",
    )(sums, *heights, *winds)


def solution(mesh):
    return jax.shard_map(
        local,
        mesh=mesh,
        in_specs=(
            P("mem", None, "space", None),
            P("space", None),
            P(None, "space", None),
            P(None, "space", None),
            P("space", None),
            P("space", None, None, None),
            P("space", None, None, None),
        ),
        out_specs=P("mem", None, "space", None),
        check_vma=False,
    )
```

```python
import functools
import math

import jax
import jax.numpy as jnp
from jax import lax
from jax.experimental import pallas as pl
from jax.experimental.pallas import tpu as pltpu
from jax.sharding import PartitionSpec as P

mass_rate = 0.2
wave_rate = 0.2
turn_rate = 0.1

VMEM = pl.BlockSpec(memory_space=pltpu.VMEM)
HBM = pl.BlockSpec(memory_space=pltpu.HBM)
SMEM = pl.BlockSpec(memory_space=pltpu.SMEM)
F32 = jnp.float32
BF16 = jnp.bfloat16
PARAMS = pltpu.CompilerParams(vmem_limit_bytes=12 * 1024 * 1024)
FORECAST_FLOPS = 2 * 10**9


def cost(flops, size):
    return pl.CostEstimate(flops=flops, bytes_accessed=size, transcendentals=0)


def diff_cols(field):
    width = field.shape[-1]
    return pltpu.roll(field, width - 1, 1) - pltpu.roll(field, 1, 1)


def far_shift(index):
    half = 2 + index // 2
    return half - 2 * half * (index % 2)


def edge_kernel(state_in, depth_in, values, precision, above, below, own, *refs):
    peers = len(refs) - 5
    held = refs[:peers]
    state, depth, seen, weight, sems = refs[peers:]
    members, _, rows, cols = state.shape
    width = values.shape[-1]
    half = members // 2
    copies = [
        pltpu.make_async_copy(state_in.at[0:half], state.at[0:half], sems.at[0]),
        pltpu.make_async_copy(state_in.at[half:members], state.at[half:members], sems.at[1]),
        pltpu.make_async_copy(depth_in, depth, sems.at[2]),
    ]
    place, count = lax.axis_index("space"), values.shape[1]
    peers_of = [place, lax.rem(place + count - 1, count), lax.rem(place + 1, count)]
    for j in range(peers):
        index = j * lax.axis_size("mem") + lax.axis_index("mem")
        half = 2 + lax.div(index, 2)
        shift = half - 2 * half * lax.rem(index, 2)
        peers_of.append(lax.rem(place + 2 * count - shift, count))
    for j, peer in enumerate(peers_of):
        copies.append(pltpu.make_async_copy(values.at[0, peer], seen.at[j], sems.at[3 + 2 * j]))
        copies.append(pltpu.make_async_copy(precision.at[0, peer], weight.at[j], sems.at[4 + 2 * j]))
    for copy in copies:
        copy.start()
    for copy in copies:
        copy.wait()
    for out, sign, at in ((above, 1.0, range(4)), (below, -1.0, range(rows - 1, rows - 5, -1))):
        deep = [jnp.broadcast_to(depth[t : t + 1], (members, cols)) for t in at]
        h = [state[:, 0, t, :] for t in at]
        u = [state[:, 1, t, :] for t in at]
        v = [state[:, 2, t, :] for t in at]
        flux = [d * e for d, e in zip(deep, u)]
        first = h[0] - mass_rate * (sign * flux[1] + diff_cols(deep[0] * v[0]))
        second, third = (
            h[i] - mass_rate * (sign * (flux[i + 1] - flux[i - 1]) + diff_cols(deep[i] * v[i]))
            for i in (1, 2)
        )
        east = u[0] - wave_rate * sign * second + turn_rate * v[0]
        east_next = u[1] - wave_rate * sign * third + turn_rate * v[1]
        north = v[0] - turn_rate * u[0] - wave_rate * diff_cols(first)
        twice = first - mass_rate * (
            sign * deep[1] * (east_next + sign * wave_rate * first) + diff_cols(deep[0] * north)
        )
        for i, part in enumerate((flux[0], first, east, twice)):
            out[i * members : (i + 1) * members] = part
        out[4 * members : 4 * members + 8] = jnp.concatenate(
            [deep[0][0:1], deep[1][0:1], jnp.zeros((6, cols), F32)], axis=0
        )
    rim = 4 * members + 8
    slots = seen.shape[1]
    places = [own, above.at[rim : rim + slots], below.at[rim : rim + slots]] + list(held)
    for j, out in enumerate(places):
        out[:, 0:width] = seen[j]
        out[:, width : 2 * width] = weight[j]


def edges(peers, state, depth, values, precision):
    members, _, _, cols = state.shape
    slots = values.shape[2]
    rim = jax.ShapeDtypeStruct((4 * members + 8 + slots, cols), F32)
    held = jax.ShapeDtypeStruct((slots, cols), F32)
    return pl.pallas_call(
        edge_kernel,
        out_shape=(rim, rim, held) + (held,) * peers,
        in_specs=[HBM] * 4,
        out_specs=(VMEM,) * (3 + peers),
        scratch_shapes=[
            pltpu.VMEM(state.shape, F32),
            pltpu.VMEM(depth.shape, F32),
            pltpu.VMEM((3 + peers,) + values.shape[2:], F32),
            pltpu.VMEM((3 + peers,) + values.shape[2:], F32),
            pltpu.SemaphoreType.DMA((9 + 2 * peers,)),
        ],
        compiler_params=pltpu.CompilerParams(vmem_limit_bytes=56 * 1024 * 1024),
        name="edges",
    )(state, depth, values, precision)


def forecast_kernel(last, state, depth, above, below, *refs):
    held = refs[:-7]
    height_out, east_out, north_out, h, u, v, flux = refs[-7:]
    members, _, rows, cols = state.shape
    slots = held[0].shape[0]
    deep = [jnp.broadcast_to(depth[t : t + 1], (members, cols)) for t in range(rows)]
    sides = []
    place = lax.axis_index("space")
    for ref, sign, edge, inside in (
        (above, -1.0, 0, place > 0),
        (below, 1.0, rows - 1, place < last),
    ):
        parts = [ref[i * members : (i + 1) * members] for i in range(4)]
        deeps = [
            jnp.broadcast_to(ref[4 * members + i : 4 * members + i + 1], (members, cols))
            for i in range(2)
        ]
        sides.append((parts, deeps, sign, edge, inside.astype(F32)))

    def outer(edge):
        return 0 if edge == 0 else rows + 1

    for t in range(rows):
        h[t + 1] = state[:, 0, t, :]
        u[t] = state[:, 1, t, :]
        v[t] = state[:, 2, t, :]
        flux[t + 1] = deep[t] * u[t]
    deltas = []
    for (first_flux, _, _, _), _, sign, edge, inside in sides:
        deltas.append(sign * mass_rate * flux[edge + 1])
        flux[outer(edge)] = first_flux * inside

    def new_heights():
        for t in range(rows):
            h[t + 1] = h[t + 1] - mass_rate * (flux[t + 2] - flux[t] + diff_cols(deep[t] * v[t]))

    def new_winds(put):
        for t in range(rows):
            east, north = u[t], v[t]
            put(
                t,
                east - wave_rate * (h[t + 2] - h[t]) + turn_rate * north,
                north - wave_rate * diff_cols(h[t + 1]) - turn_rate * east,
            )

    def keep(t, east, north):
        u[t], v[t] = east, north
        flux[t + 1] = deep[t] * east

    def emit(t, east, north):
        east_out[t] = east
        north_out[t] = north

    new_heights()
    for delta, ((_, first, east, _), deeps, sign, edge, inside) in zip(deltas, sides):
        h[outer(edge)] = (first + delta) * inside
        flux[outer(edge)] = inside * deeps[0] * (east + sign * wave_rate * h[edge + 1])
    new_winds(keep)
    rims = []
    for delta, ((_, _, _, twice), deeps, sign, edge, inside) in zip(deltas, sides):
        turned = wave_rate * diff_cols(deeps[0] * diff_cols(delta))
        change = wave_rate * deeps[1] * delta - sign * flux[edge + 1] - turned
        rims.append((edge, (twice + delta - mass_rate * change) * inside))
    new_heights()
    for edge, rim in rims:
        h[outer(edge)] = rim
    new_winds(emit)
    for t in range(rows):
        height_out[t] = h[t + 1]
    for j, piece in enumerate(held):
        at = j * slots
        height_out[rows + at // members, at % members : at % members + slots, :] = piece[...]


def forecast(last, state, depth, above, below, held):
    members, _, rows, cols = state.shape
    extra = -(-len(held) * held[0].shape[0] // members)
    return pl.pallas_call(
        functools.partial(forecast_kernel, last),
        out_shape=(
            jax.ShapeDtypeStruct((rows + extra, members, cols), F32),
            jax.ShapeDtypeStruct((rows, members, cols), F32),
            jax.ShapeDtypeStruct((rows, members, cols), F32),
        ),
        in_specs=[VMEM] * (4 + len(held)),
        out_specs=(VMEM, VMEM, VMEM),
        scratch_shapes=[
            pltpu.VMEM((rows + 2, members, cols), F32),
            pltpu.VMEM((rows, members, cols), F32),
            pltpu.VMEM((rows, members, cols), F32),
            pltpu.VMEM((rows + 2, members, cols), F32),
        ],
        compiler_params=PARAMS,
        cost_estimate=cost(FORECAST_FLOPS, 4 * state.size),
        name="forecast",
    )(state, depth, above, below, *held)


def interpolate(pieces, cells, weights, split, put):
    rows = split.shape[0] // (len(pieces) * pieces[0].shape[1])
    _, members, cols = pieces[0].shape
    total = members * len(pieces)
    points, blocks, width = cells.shape
    quarter = lax.axis_index("mem")
    blocks = blocks // lax.axis_size("mem")
    for k, piece in enumerate(pieces):
        who = lax.bitwise_xor(lax.rem(quarter, len(pieces)), k)
        for r in range(rows):
            x = piece[r]
            high = x.astype(BF16)
            low = (x - high.astype(F32)).astype(BF16)
            at = pl.ds(pl.multiple_of(r * total + who * members, members), members)
            split[at, 0:cols] = high
            split[at, cols : 2 * cols] = low

    def block(b, carry):
        result = None
        line = pl.ds(quarter * blocks + b, 1)
        for half in range(points // 2):
            cell = jnp.concatenate(
                [cells[2 * half, line, :], cells[2 * half + 1, line, :]], axis=1
            )
            share = jnp.concatenate(
                [weights[2 * half, line, :], weights[2 * half + 1, line, :]], axis=1
            )
            row = cell // cols
            col = jnp.broadcast_to(cell - row * cols, (cols, 2 * width))
            here = lax.broadcasted_iota(jnp.int32, (cols, 2 * width), 0) == col
            pick = jnp.where(here, 1.0, 0.0).astype(BF16)
            lines = jnp.dot(
                split[...], jnp.concatenate([pick, pick], axis=0), preferred_element_type=F32
            )
            for r in range(rows):
                term = lines[r * total : (r + 1) * total] * jnp.where(row == r, share, 0.0)
                term = term[:, :width] + term[:, width:]
                result = term if result is None else result + term
        put(b, result)
        return carry

    lax.fori_loop(0, blocks, block, 0, unroll=8)


def collect(got, pieces, split):
    _, members, _ = pieces[0].shape
    rows = split.shape[0] // (len(pieces) * members)
    slots = got.shape[1]
    peers = got.shape[0] // len(pieces)
    for k, piece in enumerate(pieces):
        for j in range(peers):
            at = j * slots
            got[k * peers + j] = piece[rows + at // members, at % members : at % members + slots, :]


def predict_kernel(count, owners, *refs):
    pieces = refs[:count]
    cells, weights, own, above, below, out, near, slots, spots, split, used = refs[count:]
    share = slots.shape[0]
    near[0] = own[...]
    rim = below.shape[0] - own.shape[0]
    near[1] = below[rim:]
    near[2] = above[rim:]
    collect(near.at[3:], pieces, split)
    peers = (near.shape[0] - 3) // count
    space, quarter = lax.axis_index("space"), lax.axis_index("mem")
    spaces, quarters = used.shape[0], lax.axis_size("mem")
    begin = quarter * share
    for owner in range(used.shape[0]):
        used[owner] = 0

    def skip(b, carry):
        used[owners[b]] += 1
        return carry

    lax.fori_loop(0, begin, skip, 0)
    for i in range(share):
        owner = owners[begin + i]
        slots[i] = used[owner]
        used[owner] += 1
        apart = lax.rem(owner + spaces - space, spaces)
        index = jnp.where(apart <= spaces // 2, 2 * (apart - 2), 2 * (spaces - apart - 2) + 1)
        who = lax.rem(index, quarters)
        spot = 3 + lax.bitwise_xor(who, quarter) * peers + lax.div(index, quarters)
        spot = jnp.where(apart <= 1, apart, spot)
        spots[i] = jnp.where(apart == spaces - 1, 2, spot)

    def put(b, result):
        out[b] = result

    interpolate(pieces, cells, weights, split, put)


def gram_kernel(scale, count, count_mem, spots, slots, *refs):
    pieces = refs[:count]
    cells, weights, near, early, keep, give, split, lined, got = refs[count:]
    _, members, cols = pieces[0].shape
    total = members * count_mem
    part = members * count
    blocks, width = slots.shape[0], cells.shape[2]
    quarter = lax.axis_index("mem")
    got[0 : near.shape[0]] = near[...]
    collect(got.at[near.shape[0] :], pieces, split)

    mine = quarter // count
    base = pl.multiple_of(mine * part, part)
    final = pl.multiple_of(lax.bitwise_xor(mine, 1) * part, part)

    def put(b, result):
        at = pl.ds(pl.multiple_of(b * width, width), width)
        lined[pl.ds(final, part), at] = result
        lined[pl.ds(base, part), at] = early[b]

    interpolate(pieces, cells, weights, split, put)
    lined[total : 2 * total] = jnp.zeros((total, blocks * width), F32)
    for b in range(blocks):
        line = got[spots[b], pl.ds(slots[b], 1)]
        seen, much = line[:, 0:width], line[:, width : 2 * width] * scale
        at = pl.ds(b * width, width)
        values = lined[0:total, at]
        middle = jnp.sum(values, axis=0, keepdims=True) * (1.0 / total)
        lined[0:total, at] = (values - middle) * much
        lined[total : total + 1, at] = (seen - middle) * much

    x = lined[...]
    high = x.astype(BF16)
    low = (x - high.astype(F32)).astype(BF16)
    turned = (((1,), (1,)), ((), ()))
    gram = lax.dot_general(high, high, turned, preferred_element_type=F32)
    cross = lax.dot_general(high, low, turned, preferred_element_type=F32)
    gram = gram + (cross + cross.T)
    packed = pack_gram(gram, total)
    half = keep.shape[0]
    odd = lax.rem(quarter, 2) == 1
    for r in range(half):
        low, high = packed[r : r + 1], packed[half + r : half + r + 1]
        keep[r] = jnp.where(odd, high, low)
        give[r] = jnp.where(odd, low, high)


def spread_kernel(keep, given, out):
    both = keep[...] + given[...]
    for d in range(out.shape[0]):
        out[d] = both


def pack_gram(gram, total):
    half, quarter = total // 2, total // 4
    span = 2 * total
    top, low = gram[0:half], gram[half:total]
    lane = lax.broadcasted_iota(jnp.int32, (half, span), 1)
    line = lax.broadcasted_iota(jnp.int32, (half, span), 0)
    both = jnp.where(lane <= line, top, pltpu.roll(low, span - half, 1))
    wide = jnp.where(lane < half, both, pltpu.roll(low, half, 1))
    lane_q = lane[0:quarter]
    body = jnp.where(lane_q < total, wide[0:quarter], pltpu.roll(wide[quarter:half], total, 1))
    diag = jnp.sum(jnp.where(lane == line + half, low, 0.0), axis=0, keepdims=True)
    lane_1 = lane[0:8]
    tail = jnp.where(
        lane_1 < total, gram[total : total + 8], pltpu.roll(jnp.broadcast_to(diag, (8, span)), half, 1)
    )
    return jnp.concatenate([body, tail], axis=0)


def unpack_gram(packed, total):
    half, quarter = total // 2, total // 4
    span = 2 * total
    body, tail = packed[0:quarter], packed[quarter : quarter + 1]
    wide = jnp.concatenate([body, pltpu.roll(body, total, 1)], axis=0)
    low = pltpu.roll(wide, span - half, 1)
    lane = lax.broadcasted_iota(jnp.int32, (half, span), 1)
    line = lax.broadcasted_iota(jnp.int32, (half, span), 0)
    first = lane < half
    stacked = jnp.concatenate(
        [jnp.where(first, wide, 0.0), jnp.where(first, low, 0.0), jnp.zeros((total, span), F32)], axis=0
    )
    turned = stacked.T[0:half]
    top = jnp.where(first & (lane <= line), wide, turned)
    diag = pltpu.roll(jnp.broadcast_to(tail, (half, span)), span - half, 1)
    corner = jnp.where(lane > line, wide, turned)
    corner = pltpu.roll(jnp.where(first, corner, 0.0), half, 1)
    corner = jnp.where(lane == line + half, diag, corner)
    bottom = jnp.where(first, low, corner)
    return jnp.concatenate([top, bottom], axis=0), tail


def factor_inverse(system, total):
    span = 2 * total
    lane = lax.broadcasted_iota(jnp.int32, (total, span), 1)
    line = lax.broadcasted_iota(jnp.int32, (total, span), 0)
    work = jnp.where(lane < total, system, jnp.where(lane == line + total, 1.0, 0.0))
    tiles = [work[8 * g : 8 * g + 8] for g in range(total // 8)]
    step = 8
    below = lax.broadcasted_iota(jnp.int32, (8, span), 0)

    def lanes(x, k):
        return jnp.broadcast_to(x[:, k : k + 1], (8, span))

    def lines(x, s):
        return jnp.broadcast_to(x[s : s + 1], (8, span))

    for k in range(0, total, step):
        g, s = k // 8, k % 8
        columns = {t: [lanes(tiles[t], k + i) for i in range(step)] for t in range(g, total // 8)}
        pivots = [lines(tiles[g], s + i) for i in range(step)]
        block = [[lines(columns[g][j], s + i) for j in range(i + 1)] for i in range(step)]
        for j in range(step):
            scale = 1.0 / block[j][j]
            ratio = [None] * step
            for i in range(j + 1, step):
                ratio[i] = block[i][j] * scale
            for i in range(j + 1, step):
                for n in range(j + 1, i + 1):
                    block[i][n] = block[i][n] - ratio[i] * block[n][j]
                pivots[i] = pivots[i] - ratio[i] * pivots[j]
            scaled = pivots[j] * scale
            for t in columns:
                for i in range(j + 1, step):
                    columns[t][i] = columns[t][i] - ratio[i] * columns[t][j]
            for t in columns:
                column = columns[t][j]
                if t == g:
                    if s + j == 7:
                        continue
                    column = jnp.where(below > s + j, column, 0.0)
                tiles[t] = tiles[t] - column * scaled
    work = jnp.concatenate(tiles, axis=0)
    diag = jnp.sum(jnp.where(lane == line, work, 0.0), axis=1, keepdims=True)
    return jnp.where(lane < total, pltpu.roll(work, total, 1), 0.0) / jnp.sqrt(diag)


def mixing_columns(packed, total, members, count_mem, lower):
    span = 2 * total
    quarter = lax.axis_index("mem")
    system, proj = unpack_gram(packed, total)
    lane = lax.broadcasted_iota(jnp.int32, (total, span), 1)
    line = lax.broadcasted_iota(jnp.int32, (total, span), 0)
    inverse = factor_inverse(system + jnp.where(lane == line, float(total - 1), 0.0), total)
    first = jnp.sum(jnp.where(lane < total, inverse * proj, 0.0), axis=1, keepdims=True)
    mean_weights = jnp.sum(inverse * first, axis=0, keepdims=True)
    lower[...] = inverse
    mine = lower[pl.ds(pl.multiple_of(quarter * members, members), members)]
    coef = mean_weights + math.sqrt(total - 1) * mine
    short = lane[0:members]
    coef = jnp.where(short < total, coef, 0.0)
    mixing = coef + (1.0 - jnp.sum(coef, axis=1, keepdims=True)) * (1.0 / total)
    bit = 1
    while bit < count_mem:
        size = bit * members
        turned = jnp.where(
            lax.rem(short // size, 2) == 0, pltpu.roll(mixing, span - size, 1), pltpu.roll(mixing, size, 1)
        )
        swapped = (lax.rem(quarter // bit, 2) == 1).astype(F32)
        mixing = mixing + swapped * (turned - mixing)
        bit *= 2
    return mixing[:, 0:total]


def analysis_kernel(count_mem, sums, *refs):
    fields = [refs[f * count_mem : (f + 1) * count_mem] for f in range(3)]
    out, lower = refs[3 * count_mem :]
    rows, members, cols = fields[1][0].shape
    total = members * count_mem

    halves = [sums[0], sums[1]]
    for d in range(2, sums.shape[0]):
        halves[d % 2] = halves[d % 2] + sums[d]
    packed = jnp.concatenate([half[r] for half in halves for r in range(half.shape[0])], axis=0)
    mixing = mixing_columns(packed, total, members, count_mem, lower)
    high = mixing.astype(BF16)
    low = (mixing - high.astype(F32)).astype(BF16)
    left = jnp.concatenate([high, high, low], axis=1)
    for field in range(3):
        for r in range(rows):
            pieces = [piece[r] for piece in fields[field]]
            upper = [x.astype(BF16) for x in pieces]
            rest = [(x - y.astype(F32)).astype(BF16) for x, y in zip(pieces, upper)]
            stack = jnp.concatenate(upper + rest + upper, axis=0)
            out[:, field, r, :] = jnp.dot(left, stack, preferred_element_type=F32)


def swap(x, axis, bit):
    count = lax.axis_size(axis)
    return lax.ppermute(x, axis, [(i, i ^ bit) for i in range(count)])


def after(x, *others):
    return lax.optimization_barrier((x,) + others)[0]


def local(state, depth, obs_cells, obs_weights, owner_map, obs_values, obs_precision):
    members, fields, rows, cols = state.shape
    count = lax.axis_size("space")
    count_mem = lax.axis_size("mem")
    total = members * count_mem
    blocks, width = obs_cells.shape[1:]
    share = blocks // count_mem
    scale = math.sqrt((total - 1) / (count * blocks * width))

    peers = -(-(count - 3) // count_mem)

    to_above, to_below, own, *held = edges(peers, state, depth, obs_values, obs_precision)
    ends = count - 1
    below = lax.ppermute(to_above, "space", [((i + 1) % count, i) for i in range(count)])
    above = lax.ppermute(to_below, "space", [(i, (i + 1) % count) for i in range(count)])
    held = [
        lax.ppermute(
            piece,
            ("space", "mem"),
            [
                (s * count_mem + q, (s - far_shift(j * count_mem + q)) % count * count_mem + q)
                for s in range(count)
                for q in range(count_mem)
                if j * count_mem + q < count - 3
            ],
        )
        for j, piece in enumerate(held)
    ]
    height, *parts = forecast(ends, state, depth, above, below, held)

    near, far = 1, count_mem // 2
    early_shape = (share, far * members, width)
    split = pltpu.VMEM((rows * far * members, 2 * cols), BF16)
    flops = 4 * obs_cells.shape[0] * share * width * rows * members * far * cols
    owners = owner_map[:, 0]
    heights = {0: height}
    winds = [{0: part} for part in parts]
    heights[far] = swap(height, "mem", far)
    heights[near] = swap(height, "mem", near)
    near_shape = (3 + far * peers, obs_values.shape[2], cols)
    early, first, slots, spots = pl.pallas_call(
        functools.partial(predict_kernel, far),
        out_shape=(
            jax.ShapeDtypeStruct(early_shape, F32),
            jax.ShapeDtypeStruct(near_shape, F32),
            jax.ShapeDtypeStruct((share,), jnp.int32),
            jax.ShapeDtypeStruct((share,), jnp.int32),
        ),
        in_specs=[SMEM] + [VMEM] * (far + 5),
        out_specs=(VMEM, VMEM, SMEM, SMEM),
        scratch_shapes=[split, pltpu.SMEM((count,), jnp.int32)],
        compiler_params=PARAMS,
        cost_estimate=cost(flops, 4 * height.size * far),
        name="predict",
    )(owners, heights[0], heights[near], obs_cells, obs_weights, own, above, below)
    heights[far] = after(heights[far], early)
    heights[far + near] = swap(heights[far], "mem", near)
    for wind in winds:
        wind[far] = swap(after(wind[0], heights[far]), "mem", far)
        wind[near] = swap(wind[0], "mem", near)
    for wind in winds:
        wind[far + near] = swap(wind[far], "mem", near)
    heights = [heights[k] for k in range(count_mem)]
    winds = [wind[k] for wind in winds for k in range(count_mem)]

    half = (total // 4 + 2) // 2
    devices = count * count_mem
    part = jax.ShapeDtypeStruct((half, 1, 2 * total), F32)
    keep, give = pl.pallas_call(
        functools.partial(gram_kernel, scale, far, count_mem),
        out_shape=(part, part),
        in_specs=[SMEM, SMEM] + [VMEM] * (far + 4),
        out_specs=(VMEM, VMEM),
        scratch_shapes=[
            split,
            pltpu.VMEM((2 * total, share * width), F32),
            pltpu.VMEM((3 + count_mem * peers,) + near_shape[1:], F32),
        ],
        compiler_params=PARAMS,
        cost_estimate=cost(flops, 4 * height.size * count_mem),
        name="gram",
    )(spots, slots, *heights[far:], obs_cells, obs_weights, first, early)
    sent = pl.pallas_call(
        spread_kernel,
        out_shape=jax.ShapeDtypeStruct((devices,) + part.shape, F32),
        in_specs=[VMEM, VMEM],
        out_specs=VMEM,
        compiler_params=PARAMS,
        name="spread",
    )(keep, swap(give, "mem", near))
    sums = lax.all_to_all(sent, ("space", "mem"), split_axis=0, concat_axis=0, tiled=True)

    return pl.pallas_call(
        functools.partial(analysis_kernel, count_mem),
        out_shape=jax.ShapeDtypeStruct(state.shape, F32),
        in_specs=[VMEM] * (1 + 3 * count_mem),
        out_specs=VMEM,
        scratch_shapes=[pltpu.VMEM((total, 2 * total), F32)],
        compiler_params=PARAMS,
        name="analysis",
    )(sums, *heights, *winds)


def solution(mesh):
    return jax.shard_map(
        local,
        mesh=mesh,
        in_specs=(
            P("mem", None, "space", None),
            P("space", None),
            P(None, "space", None),
            P(None, "space", None),
            P("space", None),
            P("space", None, None, None),
            P("space", None, None, None),
        ),
        out_specs=P("mem", None, "space", None),
        check_vma=False,
    )
```

```python
import functools
import math

import jax
import jax.numpy as jnp
from jax import lax
from jax.experimental import pallas as pl
from jax.experimental.pallas import tpu as pltpu
from jax.sharding import PartitionSpec as P

mass_rate = 0.2
wave_rate = 0.2
turn_rate = 0.1

ANY = pl.BlockSpec(memory_space=pl.ANY)
VMEM = pl.BlockSpec(memory_space=pltpu.VMEM)
HBM = pl.BlockSpec(memory_space=pltpu.HBM)
SMEM = pl.BlockSpec(memory_space=pltpu.SMEM)
F32 = jnp.float32
BF16 = jnp.bfloat16
PARAMS = pltpu.CompilerParams(vmem_limit_bytes=12 * 1024 * 1024)
FORECAST_FLOPS = 2 * 10**9
RIM = 3


def hold(arrays, *others):
    return pl.pallas_call(
        lambda *refs: None,
        out_shape=tuple(jax.ShapeDtypeStruct(x.shape, x.dtype) for x in arrays),
        in_specs=[ANY] * (len(arrays) + len(others)),
        out_specs=(ANY,) * len(arrays),
        input_output_aliases={i: i for i in range(len(arrays))},
        compiler_params=PARAMS,
        cost_estimate=cost(1, 1),
        name="hold",
    )(*arrays, *others)


def cost(flops, size):
    return pl.CostEstimate(flops=flops, bytes_accessed=size, transcendentals=0)


def diff_cols(field):
    width = field.shape[-1]
    return pltpu.roll(field, width - 1, 1) - pltpu.roll(field, 1, 1)


def far_shift(index):
    half = 2 + index // 2
    return half - 2 * half * (index % 2)


def edge_kernel(peers, state_in, depth_in, values, precision, above, below, own, *refs):
    held = refs[:-5]
    state, depth, seen, weight, sems = refs[-5:]
    members, _, rows, cols = state.shape
    width = values.shape[-1]
    half = members // 2
    copies = [
        pltpu.make_async_copy(state_in.at[0:half], state.at[0:half], sems.at[0]),
        pltpu.make_async_copy(state_in.at[half:members], state.at[half:members], sems.at[1]),
        pltpu.make_async_copy(depth_in, depth, sems.at[2]),
    ]
    place, count = lax.axis_index("space"), values.shape[1]
    peers_of = [place, lax.rem(place + count - 1, count), lax.rem(place + 1, count)]
    quarters = lax.axis_size("mem")
    for j in range(peers):
        index = j * quarters + lax.axis_index("mem")
        half = 2 + lax.div(index, 2)
        shift = half - 2 * half * lax.rem(index, 2)
        peers_of.append(lax.rem(place + 2 * count - shift, count))
    for index in range(peers * quarters, count - 3):
        peers_of.append(lax.rem(place + 2 * count - far_shift(index), count))
    for j, peer in enumerate(peers_of):
        copies.append(pltpu.make_async_copy(values.at[0, peer], seen.at[j], sems.at[3 + 2 * j]))
        copies.append(pltpu.make_async_copy(precision.at[0, peer], weight.at[j], sems.at[4 + 2 * j]))
    for copy in copies:
        copy.start()
    for copy in copies:
        copy.wait()
    for out, sign, at in ((above, 1.0, range(4)), (below, -1.0, range(rows - 1, rows - 5, -1))):
        deep = [jnp.broadcast_to(depth[t : t + 1], (members, cols)) for t in at]
        h = [state[:, 0, t, :] for t in at]
        u = [state[:, 1, t, :] for t in at]
        v = [state[:, 2, t, :] for t in at]
        flux = [d * e for d, e in zip(deep, u)]
        first = h[0] - mass_rate * (sign * flux[1] + diff_cols(deep[0] * v[0]))
        second, third = (
            h[i] - mass_rate * (sign * (flux[i + 1] - flux[i - 1]) + diff_cols(deep[i] * v[i]))
            for i in (1, 2)
        )
        east = u[0] - wave_rate * sign * second + turn_rate * v[0]
        east_next = u[1] - wave_rate * sign * third + turn_rate * v[1]
        north = v[0] - turn_rate * u[0] - wave_rate * diff_cols(first)
        twice = first - mass_rate * (
            sign * deep[1] * (east_next + sign * wave_rate * first) + diff_cols(deep[0] * north)
        )
        for i, part in enumerate((flux[0], first, east, twice)):
            out[i * members : (i + 1) * members] = part
        out[4 * members : 4 * members + 8] = jnp.concatenate(
            [deep[0][0:1], deep[1][0:1], jnp.zeros((6, cols), F32)], axis=0
        )
    rim = 4 * members + 8
    slots = seen.shape[1]
    places = [own, above.at[rim : rim + slots], below.at[rim : rim + slots]] + list(held)
    for j, out in enumerate(places):
        out[:, 0:width] = seen[j]
        out[:, width : 2 * width] = weight[j]


def edges(peers, state, depth, values, precision):
    members, _, _, cols = state.shape
    slots = values.shape[2]
    rim = jax.ShapeDtypeStruct((4 * members + 8 + slots, cols), F32)
    held = jax.ShapeDtypeStruct((slots, cols), F32)
    owners = peers + (values.shape[1] - 3) % lax.axis_size("mem")
    return pl.pallas_call(
        functools.partial(edge_kernel, peers),
        out_shape=(rim, rim, held) + (held,) * owners,
        in_specs=[HBM] * 4,
        out_specs=(VMEM,) * (3 + owners),
        scratch_shapes=[
            pltpu.VMEM(state.shape, F32),
            pltpu.VMEM(depth.shape, F32),
            pltpu.VMEM((3 + owners,) + values.shape[2:], F32),
            pltpu.VMEM((3 + owners,) + values.shape[2:], F32),
            pltpu.SemaphoreType.DMA((9 + 2 * owners,)),
        ],
        compiler_params=pltpu.CompilerParams(vmem_limit_bytes=56 * 1024 * 1024),
        name="edges",
    )(state, depth, values, precision)


def inner_kernel(state, depth, out):
    members, _, rows, cols = state.shape
    deep = [jnp.broadcast_to(depth[t : t + 1], (members, cols)) for t in range(rows)]
    h = [state[:, 0, t, :] for t in range(rows)]
    u = [state[:, 1, t, :] for t in range(rows)]
    v = [state[:, 2, t, :] for t in range(rows)]
    for step in range(2):
        edge = 2 * step + 1
        flux = [d * e if e is not None else None for d, e in zip(deep, u)]
        new = [None] * rows
        for t in range(edge, rows - edge):
            new[t] = h[t] - mass_rate * (flux[t + 1] - flux[t - 1] + diff_cols(deep[t] * v[t]))
        h = new
        if step == 1:
            break
        east, north = [None] * rows, [None] * rows
        for t in range(edge + 1, rows - edge - 1):
            east[t] = u[t] - wave_rate * (h[t + 1] - h[t - 1]) + turn_rate * v[t]
            north[t] = v[t] - wave_rate * diff_cols(h[t]) - turn_rate * u[t]
        u, v = east, north
    for t in range(RIM, rows - RIM):
        out[t - RIM] = h[t]


def inner_heights(state, depth):
    members, _, rows, cols = state.shape
    return pl.pallas_call(
        inner_kernel,
        out_shape=jax.ShapeDtypeStruct((rows - 2 * RIM, members, cols), F32),
        in_specs=[VMEM] * 2,
        out_specs=VMEM,
        compiler_params=PARAMS,
        cost_estimate=cost(FORECAST_FLOPS, 4 * state.size),
        name="inner",
    )(state, depth)


def forecast_kernel(last, state, depth, above, below, *refs):
    held = refs[:-7]
    height_out, east_out, north_out, h, u, v, flux = refs[-7:]
    members, _, rows, cols = state.shape
    slots = held[0].shape[0]
    deep = [jnp.broadcast_to(depth[t : t + 1], (members, cols)) for t in range(rows)]
    sides = []
    place = lax.axis_index("space")
    for ref, sign, edge, inside in (
        (above, -1.0, 0, place > 0),
        (below, 1.0, rows - 1, place < last),
    ):
        parts = [ref[i * members : (i + 1) * members] for i in range(4)]
        deeps = [
            jnp.broadcast_to(ref[4 * members + i : 4 * members + i + 1], (members, cols))
            for i in range(2)
        ]
        sides.append((parts, deeps, sign, edge, inside.astype(F32)))

    def outer(edge):
        return 0 if edge == 0 else rows + 1

    for t in range(rows):
        h[t + 1] = state[:, 0, t, :]
        u[t] = state[:, 1, t, :]
        v[t] = state[:, 2, t, :]
        flux[t + 1] = deep[t] * u[t]
    deltas = []
    for (first_flux, _, _, _), _, sign, edge, inside in sides:
        deltas.append(sign * mass_rate * flux[edge + 1])
        flux[outer(edge)] = first_flux * inside

    def new_heights():
        for t in range(rows):
            h[t + 1] = h[t + 1] - mass_rate * (flux[t + 2] - flux[t] + diff_cols(deep[t] * v[t]))

    def new_winds(put):
        for t in range(rows):
            east, north = u[t], v[t]
            put(
                t,
                east - wave_rate * (h[t + 2] - h[t]) + turn_rate * north,
                north - wave_rate * diff_cols(h[t + 1]) - turn_rate * east,
            )

    def keep(t, east, north):
        u[t], v[t] = east, north
        flux[t + 1] = deep[t] * east

    def emit(t, east, north):
        east_out[t] = east
        north_out[t] = north

    new_heights()
    for delta, ((_, first, east, _), deeps, sign, edge, inside) in zip(deltas, sides):
        h[outer(edge)] = (first + delta) * inside
        flux[outer(edge)] = inside * deeps[0] * (east + sign * wave_rate * h[edge + 1])
    new_winds(keep)
    rims = []
    for delta, ((_, _, _, twice), deeps, sign, edge, inside) in zip(deltas, sides):
        turned = wave_rate * diff_cols(deeps[0] * diff_cols(delta))
        change = wave_rate * deeps[1] * delta - sign * flux[edge + 1] - turned
        rims.append((edge, (twice + delta - mass_rate * change) * inside))
    new_heights()
    for edge, rim in rims:
        h[outer(edge)] = rim
    new_winds(emit)
    outer_rows = list(range(RIM)) + list(range(rows - RIM, rows))
    for i, t in enumerate(outer_rows):
        height_out[i] = h[t + 1]
    for j, piece in enumerate(held):
        at = j * slots
        height_out[2 * RIM + at // members, at % members : at % members + slots, :] = piece[...]


def forecast(last, state, depth, above, below, held):
    members, _, rows, cols = state.shape
    extra = -(-len(held) * held[0].shape[0] // members)
    return pl.pallas_call(
        functools.partial(forecast_kernel, last),
        out_shape=(
            jax.ShapeDtypeStruct((2 * RIM + extra, members, cols), F32),
            jax.ShapeDtypeStruct((rows, members, cols), F32),
            jax.ShapeDtypeStruct((rows, members, cols), F32),
        ),
        in_specs=[VMEM] * (4 + len(held)),
        out_specs=(VMEM, VMEM, VMEM),
        scratch_shapes=[
            pltpu.VMEM((rows + 2, members, cols), F32),
            pltpu.VMEM((rows, members, cols), F32),
            pltpu.VMEM((rows, members, cols), F32),
            pltpu.VMEM((rows + 2, members, cols), F32),
        ],
        compiler_params=PARAMS,
        cost_estimate=cost(FORECAST_FLOPS, 4 * state.size),
        name="forecast",
    )(state, depth, above, below, *held)


def interpolate(groups, cells, weights, split, put):
    _, members, cols = groups[0][0][0].shape
    total = members * len(groups[0][0])
    points, blocks, width = cells.shape
    quarter = lax.axis_index("mem")
    blocks = blocks // lax.axis_size("mem")
    first = 0
    for pieces, lines_of in groups:
        for k, piece in enumerate(pieces):
            who = lax.bitwise_xor(lax.rem(quarter, len(pieces)), k)
            for r in range(len(lines_of)):
                x = piece[r]
                high = x.astype(BF16)
                low = (x - high.astype(F32)).astype(BF16)
                at = pl.ds(pl.multiple_of((first + r) * total + who * members, members), members)
                split[at, 0:cols] = high
                split[at, cols : 2 * cols] = low
        first += len(lines_of)

    def block(b, carry):
        results = [None] * len(groups)
        line = pl.ds(quarter * blocks + b, 1)
        for half in range(points // 2):
            cell = jnp.concatenate(
                [cells[2 * half, line, :], cells[2 * half + 1, line, :]], axis=1
            )
            share = jnp.concatenate(
                [weights[2 * half, line, :], weights[2 * half + 1, line, :]], axis=1
            )
            row = cell // cols
            col = jnp.broadcast_to(cell - row * cols, (cols, 2 * width))
            here = lax.broadcasted_iota(jnp.int32, (cols, 2 * width), 0) == col
            pick = jnp.where(here, 1.0, 0.0).astype(BF16)
            lines = jnp.dot(
                split[...], jnp.concatenate([pick, pick], axis=0), preferred_element_type=F32
            )
            first = 0
            for g, (_, lines_of) in enumerate(groups):
                for r, at in enumerate(lines_of):
                    term = lines[(first + r) * total : (first + r + 1) * total]
                    term = term * jnp.where(row == at, share, 0.0)
                    term = term[:, :width] + term[:, width:]
                    results[g] = term if results[g] is None else results[g] + term
                first += len(lines_of)
        put(b, *results)
        return carry

    lax.fori_loop(0, blocks, block, 0, unroll=8)


def collect(got, pieces):
    members = pieces[0].shape[1]
    rows = 2 * RIM
    slots = got.shape[1]
    peers = got.shape[0] // len(pieces)
    for k, piece in enumerate(pieces):
        for j in range(peers):
            at = j * slots
            got[k * peers + j] = piece[rows + at // members, at % members : at % members + slots, :]


def block_lines(owners, share, spaces, slots, peers):
    space, quarter = lax.axis_index("space"), lax.axis_index("mem")
    quarters = lax.axis_size("mem")
    shift = quarters.bit_length() - 1
    blocks = owners.shape[1]
    lane = lax.broadcasted_iota(jnp.int32, (share, blocks), 1)
    line = lax.broadcasted_iota(jnp.int32, (share, blocks), 0) + quarter * share
    row = jnp.broadcast_to(owners[...], (share, blocks)).astype(F32)
    mine = jnp.sum(jnp.where(lane == line, row, 0.0), axis=1, keepdims=True)
    slot = jnp.sum(jnp.where((row == mine) & (lane < line), 1.0, 0.0), axis=1, keepdims=True)
    apart = mine.astype(jnp.int32) - space
    apart = jnp.where(apart < 0, apart + spaces, apart)
    index = jnp.where(apart <= spaces // 2, 2 * (apart - 2), 2 * (spaces - apart - 2) + 1)
    who = lax.bitwise_xor(lax.bitwise_and(index, quarters - 1), quarter)
    spot = 3 + who * peers + lax.shift_right_arithmetic(index, shift)
    spot = jnp.where(index >= peers * quarters, 3 + index, spot)
    spot = jnp.where(apart <= 1, apart, spot)
    spot = jnp.where(apart == spaces - 1, 2, spot)
    return spot * slots + slot.astype(jnp.int32)


def near_inner_kernel(lines_of, count, *refs):
    pieces = refs[:count]
    cells, weights, owners, out, owners_out, split = refs[count:]
    owners_out[...] = owners[...]

    def put(b, result):
        out[b] = result

    interpolate([(pieces, lines_of)], cells, weights, split, put)


def middle_kernel(inner_rows, outer_rows, count, *refs):
    far, near = refs[:count], refs[count : 2 * count]
    cells, weights, early, own, above, below, out, out_far, got, split = refs[2 * count :]
    got[0] = own[...]
    rim = below.shape[0] - own.shape[0]
    got[1] = below[rim:]
    got[2] = above[rim:]
    collect(got.at[3:], near)

    def put(b, result_far, result):
        out_far[b] = result_far
        out[b] = result + early[b]

    interpolate([(far, inner_rows), (near, outer_rows)], cells, weights, split, put)


def gram_kernel(lines_of, scale, count, count_mem, peers, owners, *refs):
    pieces = refs[:count]
    cells, weights, near, early, early_far = refs[count : count + 5]
    direct = refs[count + 5 : -5]
    keep, give, split, lined, got = refs[-5:]
    _, members, cols = pieces[0].shape
    total = members * count_mem
    part = members * count
    blocks, width = cells.shape[1] // count_mem, cells.shape[2]
    quarter = lax.axis_index("mem")
    got[0 : near.shape[0]] = near[...]
    later = got.shape[0] - len(direct)
    collect(got.at[near.shape[0] : later], pieces)
    for i, piece in enumerate(direct):
        got[later + i] = piece[...]

    mine = quarter // count
    base = pl.multiple_of(mine * part, part)
    final = pl.multiple_of(lax.bitwise_xor(mine, 1) * part, part)

    def put(b, result):
        at = pl.ds(pl.multiple_of(b * width, width), width)
        lined[pl.ds(final, part), at] = result + early_far[b]
        lined[pl.ds(base, part), at] = early[b]

    interpolate([(pieces, lines_of)], cells, weights, split, put)
    lined[total : 2 * total] = jnp.zeros((total, blocks * width), F32)
    spaces, slots, across = got.shape
    picks = block_lines(owners, blocks, spaces, slots, peers)
    lane = lax.broadcasted_iota(jnp.int32, (blocks, spaces * slots), 1)
    taken = jnp.dot(
        jnp.where(lane == picks, 1.0, 0.0),
        got[...].reshape(spaces * slots, across),
        precision=lax.Precision.HIGHEST,
        preferred_element_type=F32,
    )
    for b in range(blocks):
        line = taken[b : b + 1]
        seen, much = line[:, 0:width], line[:, width : 2 * width] * scale
        at = pl.ds(b * width, width)
        values = lined[0:total, at]
        middle = jnp.sum(values, axis=0, keepdims=True) * (1.0 / total)
        lined[0:total, at] = (values - middle) * much
        lined[total : total + 1, at] = (seen - middle) * much

    x = lined[...]
    high = x.astype(BF16)
    low = (x - high.astype(F32)).astype(BF16)
    turned = (((1,), (1,)), ((), ()))
    gram = lax.dot_general(high, high, turned, preferred_element_type=F32)
    cross = lax.dot_general(high, low, turned, preferred_element_type=F32)
    gram = gram + (cross + cross.T)
    packed = pack_gram(gram, total)
    half = keep.shape[0]
    odd = lax.rem(quarter, 2) == 1
    for r in range(half):
        low, high = packed[r : r + 1], packed[half + r : half + r + 1]
        keep[r] = jnp.where(odd, high, low)
        give[r] = jnp.where(odd, low, high)


def spread_kernel(keep, given, out):
    both = keep[...] + given[...]
    for d in range(out.shape[0]):
        out[d] = both


def pack_gram(gram, total):
    half, quarter = total // 2, total // 4
    span = 2 * total
    top, low = gram[0:half], gram[half:total]
    lane = lax.broadcasted_iota(jnp.int32, (half, span), 1)
    line = lax.broadcasted_iota(jnp.int32, (half, span), 0)
    both = jnp.where(lane <= line, top, pltpu.roll(low, span - half, 1))
    wide = jnp.where(lane < half, both, pltpu.roll(low, half, 1))
    lane_q = lane[0:quarter]
    body = jnp.where(lane_q < total, wide[0:quarter], pltpu.roll(wide[quarter:half], total, 1))
    diag = jnp.sum(jnp.where(lane == line + half, low, 0.0), axis=0, keepdims=True)
    lane_1 = lane[0:8]
    tail = jnp.where(
        lane_1 < total, gram[total : total + 8], pltpu.roll(jnp.broadcast_to(diag, (8, span)), half, 1)
    )
    return jnp.concatenate([body, tail], axis=0)


def unpack_gram(packed, total):
    half, quarter = total // 2, total // 4
    span = 2 * total
    body, tail = packed[0:quarter], packed[quarter : quarter + 1]
    wide = jnp.concatenate([body, pltpu.roll(body, total, 1)], axis=0)
    low = pltpu.roll(wide, span - half, 1)
    lane = lax.broadcasted_iota(jnp.int32, (half, span), 1)
    line = lax.broadcasted_iota(jnp.int32, (half, span), 0)
    first = lane < half
    stacked = jnp.concatenate(
        [jnp.where(first, wide, 0.0), jnp.where(first, low, 0.0), jnp.zeros((total, span), F32)], axis=0
    )
    turned = stacked.T[0:half]
    top = jnp.where(first & (lane <= line), wide, turned)
    diag = pltpu.roll(jnp.broadcast_to(tail, (half, span)), span - half, 1)
    corner = jnp.where(lane > line, wide, turned)
    corner = pltpu.roll(jnp.where(first, corner, 0.0), half, 1)
    corner = jnp.where(lane == line + half, diag, corner)
    bottom = jnp.where(first, low, corner)
    return jnp.concatenate([top, bottom], axis=0), tail


def factor_inverse(system, total):
    span = 2 * total
    lane = lax.broadcasted_iota(jnp.int32, (total, span), 1)
    line = lax.broadcasted_iota(jnp.int32, (total, span), 0)
    work = jnp.where(lane < total, system, jnp.where(lane == line + total, 1.0, 0.0))
    tiles = [work[8 * g : 8 * g + 8] for g in range(total // 8)]
    step = 8
    below = lax.broadcasted_iota(jnp.int32, (8, span), 0)

    def lanes(x, k):
        return jnp.broadcast_to(x[:, k : k + 1], (8, span))

    def lines(x, s):
        return jnp.broadcast_to(x[s : s + 1], (8, span))

    for k in range(0, total, step):
        g, s = k // 8, k % 8
        columns = {t: [lanes(tiles[t], k + i) for i in range(step)] for t in range(g, total // 8)}
        pivots = [lines(tiles[g], s + i) for i in range(step)]
        block = [[lines(columns[g][j], s + i) for j in range(i + 1)] for i in range(step)]
        for j in range(step):
            scale = 1.0 / block[j][j]
            ratio = [None] * step
            for i in range(j + 1, step):
                ratio[i] = block[i][j] * scale
            for i in range(j + 1, step):
                for n in range(j + 1, i + 1):
                    block[i][n] = block[i][n] - ratio[i] * block[n][j]
                pivots[i] = pivots[i] - ratio[i] * pivots[j]
            scaled = pivots[j] * scale
            for t in columns:
                for i in range(j + 1, step):
                    columns[t][i] = columns[t][i] - ratio[i] * columns[t][j]
            for t in columns:
                column = columns[t][j]
                if t == g:
                    if s + j == 7:
                        continue
                    column = jnp.where(below > s + j, column, 0.0)
                tiles[t] = tiles[t] - column * scaled
    work = jnp.concatenate(tiles, axis=0)
    diag = jnp.sum(jnp.where(lane == line, work, 0.0), axis=1, keepdims=True)
    return jnp.where(lane < total, pltpu.roll(work, total, 1), 0.0) / jnp.sqrt(diag)


def mixing_columns(packed, total, members, count_mem, lower):
    span = 2 * total
    quarter = lax.axis_index("mem")
    system, proj = unpack_gram(packed, total)
    lane = lax.broadcasted_iota(jnp.int32, (total, span), 1)
    line = lax.broadcasted_iota(jnp.int32, (total, span), 0)
    inverse = factor_inverse(system + jnp.where(lane == line, float(total - 1), 0.0), total)
    first = jnp.sum(jnp.where(lane < total, inverse * proj, 0.0), axis=1, keepdims=True)
    mean_weights = jnp.sum(inverse * first, axis=0, keepdims=True)
    lower[...] = inverse
    mine = lower[pl.ds(pl.multiple_of(quarter * members, members), members)]
    coef = mean_weights + math.sqrt(total - 1) * mine
    short = lane[0:members]
    coef = jnp.where(short < total, coef, 0.0)
    mixing = coef + (1.0 - jnp.sum(coef, axis=1, keepdims=True)) * (1.0 / total)
    bit = 1
    while bit < count_mem:
        size = bit * members
        turned = jnp.where(
            lax.rem(short // size, 2) == 0, pltpu.roll(mixing, span - size, 1), pltpu.roll(mixing, size, 1)
        )
        swapped = (lax.rem(quarter // bit, 2) == 1).astype(F32)
        mixing = mixing + swapped * (turned - mixing)
        bit *= 2
    return mixing[:, 0:total]


def analysis_kernel(count_mem, sums, *refs):
    inner, outer, *winds = [refs[f * count_mem : (f + 1) * count_mem] for f in range(4)]
    out, lower = refs[4 * count_mem :]
    rows, members, cols = winds[0][0].shape
    total = members * count_mem

    halves = [sums[0], sums[1]]
    for d in range(2, sums.shape[0]):
        halves[d % 2] = halves[d % 2] + sums[d]
    packed = jnp.concatenate([half[r] for half in halves for r in range(half.shape[0])], axis=0)
    mixing = mixing_columns(packed, total, members, count_mem, lower)
    high = mixing.astype(BF16)
    low = (mixing - high.astype(F32)).astype(BF16)
    left = jnp.concatenate([high, high, low], axis=1)
    for field in range(3):
        for r in range(rows):
            if field > 0:
                pieces = [piece[r] for piece in winds[field - 1]]
            elif RIM <= r < rows - RIM:
                pieces = [piece[r - RIM] for piece in inner]
            else:
                pieces = [piece[r if r < RIM else r - rows + 2 * RIM] for piece in outer]
            upper = [x.astype(BF16) for x in pieces]
            rest = [(x - y.astype(F32)).astype(BF16) for x, y in zip(pieces, upper)]
            stack = jnp.concatenate(upper + rest + upper, axis=0)
            out[:, field, r, :] = jnp.dot(left, stack, preferred_element_type=F32)


def swap(x, axis, bit):
    count = lax.axis_size(axis)
    return lax.ppermute(x, axis, [(i, i ^ bit) for i in range(count)])


def after(x, *others):
    return lax.optimization_barrier((x,) + others)[0]


def local(state, depth, obs_cells, obs_weights, owner_map, obs_values, obs_precision):
    members, fields, rows, cols = state.shape
    count = lax.axis_size("space")
    count_mem = lax.axis_size("mem")
    total = members * count_mem
    blocks, width = obs_cells.shape[1:]
    share = blocks // count_mem
    scale = math.sqrt((total - 1) / (count * blocks * width))

    peers = (count - 3) // count_mem

    to_above, to_below, own, *blocks_out = edges(peers, state, depth, obs_values, obs_precision)
    ends = count - 1
    below = lax.ppermute(to_above, "space", [((i + 1) % count, i) for i in range(count)])
    above = lax.ppermute(to_below, "space", [(i, (i + 1) % count) for i in range(count)])
    held = [
        lax.ppermute(
            piece,
            ("space", "mem"),
            [
                (s * count_mem + q, (s - far_shift(j * count_mem + q)) % count * count_mem + q)
                for s in range(count)
                for q in range(count_mem)
            ],
        )
        for j, piece in enumerate(blocks_out[:peers])
    ]
    near, far = 1, count_mem // 2
    inner_rows = list(range(RIM, rows - RIM))
    outer_rows = list(range(RIM)) + list(range(rows - RIM, rows))
    early = jax.ShapeDtypeStruct((share, far * members, width), F32)
    owners = owner_map.reshape(1, blocks)

    def work(lines_of):
        return dict(
            compiler_params=PARAMS,
            cost_estimate=cost(
                4 * obs_cells.shape[0] * share * width * len(lines_of) * members * far * cols,
                4 * len(lines_of) * members * cols * far,
            ),
        )

    def split(lines_of):
        return pltpu.VMEM((len(lines_of) * far * members, 2 * cols), BF16)

    inner = {0: inner_heights(state, after(depth, to_above))}
    inner[far] = swap(inner[0], "mem", far)
    inner[near] = swap(inner[0], "mem", near)
    inner[far + near] = swap(inner[0], "mem", far + near)
    first, owners = pl.pallas_call(
        functools.partial(near_inner_kernel, inner_rows, far),
        out_shape=(early, jax.ShapeDtypeStruct(owners.shape, owners.dtype)),
        in_specs=[VMEM] * (far + 3),
        out_specs=(VMEM, VMEM),
        scratch_shapes=[split(inner_rows)],
        name="near_inner",
        **work(inner_rows),
    )(inner[0], inner[near], obs_cells, obs_weights, owners)

    above, below = (after(x, first) for x in (above, below))
    height, *parts = forecast(ends, state, depth, above, below, held)
    outer = {0: height}
    outer[far] = swap(height, "mem", far)
    direct = []
    for i, piece in enumerate(blocks_out[peers:]):
        shift = far_shift(peers * count_mem + i)
        ring = [(s, (s - shift) % count) for s in range(count)]
        direct.append(lax.ppermute(after(piece, height), "space", ring))
    outer[near] = swap(height, "mem", near)
    outer[far + near] = swap(height, "mem", far + near)
    near_shape = (3 + far * peers, obs_values.shape[2], cols)
    first, second, near_blocks = pl.pallas_call(
        functools.partial(middle_kernel, inner_rows, outer_rows, far),
        out_shape=(early, early, jax.ShapeDtypeStruct(near_shape, F32)),
        in_specs=[VMEM] * (2 * far + 6),
        out_specs=(VMEM,) * 3,
        scratch_shapes=[split(inner_rows + outer_rows)],
        name="middle",
        **work(inner_rows + outer_rows),
    )(
        *[inner[k] for k in range(far, 2 * far)],
        *[outer[k] for k in range(far)],
        obs_cells,
        obs_weights,
        first,
        own,
        above,
        below,
    )
    parts = hold(parts, outer[far], outer[far + near], second, *direct)
    winds = [{0: part} for part in parts]
    for wind in winds:
        wind[far] = swap(wind[0], "mem", far)
        wind[near] = swap(wind[0], "mem", near)
        wind[far + near] = swap(wind[far], "mem", near)
    inner, outer = ([x[k] for k in range(count_mem)] for x in (inner, outer))
    winds = [wind[k] for wind in winds for k in range(count_mem)]

    half = (total // 4 + 2) // 2
    devices = count * count_mem
    part = jax.ShapeDtypeStruct((half, 1, 2 * total), F32)
    keep, give = pl.pallas_call(
        functools.partial(gram_kernel, outer_rows, scale, far, count_mem, peers),
        out_shape=(part, part),
        in_specs=[VMEM] * (far + 6 + len(direct)),
        out_specs=(VMEM, VMEM),
        scratch_shapes=[
            split(outer_rows),
            pltpu.VMEM((2 * total, share * width), F32),
            pltpu.VMEM((count,) + near_shape[1:], F32),
        ],
        name="gram",
        **work(outer_rows),
    )(owners, *outer[far:], obs_cells, obs_weights, near_blocks, first, second, *direct)
    sent = pl.pallas_call(
        spread_kernel,
        out_shape=jax.ShapeDtypeStruct((devices,) + part.shape, F32),
        in_specs=[VMEM, VMEM],
        out_specs=VMEM,
        compiler_params=PARAMS,
        name="spread",
    )(keep, swap(give, "mem", near))
    sums = lax.all_to_all(sent, ("space", "mem"), split_axis=0, concat_axis=0, tiled=True)

    return pl.pallas_call(
        functools.partial(analysis_kernel, count_mem),
        out_shape=jax.ShapeDtypeStruct(state.shape, F32),
        in_specs=[VMEM] * (1 + 4 * count_mem),
        out_specs=VMEM,
        scratch_shapes=[pltpu.VMEM((total, 2 * total), F32)],
        compiler_params=PARAMS,
        name="analysis",
    )(sums, *inner, *outer, *winds)


def solution(mesh):
    return jax.shard_map(
        local,
        mesh=mesh,
        in_specs=(
            P("mem", None, "space", None),
            P("space", None),
            P(None, "space", None),
            P(None, "space", None),
            P("space", None),
            P("space", None, None, None),
            P("space", None, None, None),
        ),
        out_specs=P("mem", None, "space", None),
        check_vma=False,
    )
```

```python
import functools
import math

import jax
import jax.numpy as jnp
from jax import lax
from jax.experimental import pallas as pl
from jax.experimental.pallas import tpu as pltpu
from jax.sharding import PartitionSpec as P

mass_rate = 0.2
wave_rate = 0.2
turn_rate = 0.1

ANY = pl.BlockSpec(memory_space=pl.ANY)
VMEM = pl.BlockSpec(memory_space=pltpu.VMEM)
HBM = pl.BlockSpec(memory_space=pltpu.HBM)
SMEM = pl.BlockSpec(memory_space=pltpu.SMEM)
F32 = jnp.float32
BF16 = jnp.bfloat16
PARAMS = pltpu.CompilerParams(vmem_limit_bytes=12 * 1024 * 1024)
FORECAST_FLOPS = 2 * 10**9
RIM = 3


def hold(arrays, *others):
    return pl.pallas_call(
        lambda *refs: None,
        out_shape=tuple(jax.ShapeDtypeStruct(x.shape, x.dtype) for x in arrays),
        in_specs=[ANY] * (len(arrays) + len(others)),
        out_specs=(ANY,) * len(arrays),
        input_output_aliases={i: i for i in range(len(arrays))},
        compiler_params=PARAMS,
        cost_estimate=cost(1, 1),
        name="hold",
    )(*arrays, *others)


def cost(flops, size):
    return pl.CostEstimate(flops=flops, bytes_accessed=size, transcendentals=0)


def diff_cols(field):
    width = field.shape[-1]
    return pltpu.roll(field, width - 1, 1) - pltpu.roll(field, 1, 1)


def far_shift(index):
    half = 2 + index // 2
    return half - 2 * half * (index % 2)


def edge_kernel(peers, state_in, depth_in, values, precision, above, below, own, *refs):
    held = refs[:-5]
    state, depth, seen, weight, sems = refs[-5:]
    members, _, rows, cols = state.shape
    width = values.shape[-1]
    half = members // 2
    copies = [
        pltpu.make_async_copy(state_in.at[0:half], state.at[0:half], sems.at[0]),
        pltpu.make_async_copy(state_in.at[half:members], state.at[half:members], sems.at[1]),
        pltpu.make_async_copy(depth_in, depth, sems.at[2]),
    ]
    place, count = lax.axis_index("space"), values.shape[1]
    peers_of = [place, lax.rem(place + count - 1, count), lax.rem(place + 1, count)]
    quarters = lax.axis_size("mem")
    for j in range(peers):
        index = j * quarters + lax.axis_index("mem")
        half = 2 + lax.div(index, 2)
        shift = half - 2 * half * lax.rem(index, 2)
        peers_of.append(lax.rem(place + 2 * count - shift, count))
    for index in range(peers * quarters, count - 3):
        peers_of.append(lax.rem(place + 2 * count - far_shift(index), count))
    for j, peer in enumerate(peers_of):
        copies.append(pltpu.make_async_copy(values.at[0, peer], seen.at[j], sems.at[3 + 2 * j]))
        copies.append(pltpu.make_async_copy(precision.at[0, peer], weight.at[j], sems.at[4 + 2 * j]))
    for copy in copies:
        copy.start()
    for copy in copies:
        copy.wait()
    for out, sign, at in ((above, 1.0, range(4)), (below, -1.0, range(rows - 1, rows - 5, -1))):
        deep = [jnp.broadcast_to(depth[t : t + 1], (members, cols)) for t in at]
        h = [state[:, 0, t, :] for t in at]
        u = [state[:, 1, t, :] for t in at]
        v = [state[:, 2, t, :] for t in at]
        flux = [d * e for d, e in zip(deep, u)]
        first = h[0] - mass_rate * (sign * flux[1] + diff_cols(deep[0] * v[0]))
        second, third = (
            h[i] - mass_rate * (sign * (flux[i + 1] - flux[i - 1]) + diff_cols(deep[i] * v[i]))
            for i in (1, 2)
        )
        east = u[0] - wave_rate * sign * second + turn_rate * v[0]
        east_next = u[1] - wave_rate * sign * third + turn_rate * v[1]
        north = v[0] - turn_rate * u[0] - wave_rate * diff_cols(first)
        twice = first - mass_rate * (
            sign * deep[1] * (east_next + sign * wave_rate * first) + diff_cols(deep[0] * north)
        )
        for i, part in enumerate((flux[0], first, east, twice)):
            out[i * members : (i + 1) * members] = part
        out[4 * members : 4 * members + 8] = jnp.concatenate(
            [deep[0][0:1], deep[1][0:1], jnp.zeros((6, cols), F32)], axis=0
        )
    rim = 4 * members + 8
    slots = seen.shape[1]
    places = [own, above.at[rim : rim + slots], below.at[rim : rim + slots]] + list(held)
    for j, out in enumerate(places):
        out[:, 0:width] = seen[j]
        out[:, width : 2 * width] = weight[j]


def edges(peers, state, depth, values, precision):
    members, _, _, cols = state.shape
    slots = values.shape[2]
    rim = jax.ShapeDtypeStruct((4 * members + 8 + slots, cols), F32)
    held = jax.ShapeDtypeStruct((slots, cols), F32)
    owners = peers + (values.shape[1] - 3) % lax.axis_size("mem")
    return pl.pallas_call(
        functools.partial(edge_kernel, peers),
        out_shape=(rim, rim, held) + (held,) * owners,
        in_specs=[HBM] * 4,
        out_specs=(VMEM,) * (3 + owners),
        scratch_shapes=[
            pltpu.VMEM(state.shape, F32),
            pltpu.VMEM(depth.shape, F32),
            pltpu.VMEM((3 + owners,) + values.shape[2:], F32),
            pltpu.VMEM((3 + owners,) + values.shape[2:], F32),
            pltpu.SemaphoreType.DMA((9 + 2 * owners,)),
        ],
        compiler_params=pltpu.CompilerParams(vmem_limit_bytes=56 * 1024 * 1024),
        name="edges",
    )(state, depth, values, precision)


def inner_kernel(state, depth, out):
    members, _, rows, cols = state.shape
    deep = [jnp.broadcast_to(depth[t : t + 1], (members, cols)) for t in range(rows)]
    h = [state[:, 0, t, :] for t in range(rows)]
    u = [state[:, 1, t, :] for t in range(rows)]
    v = [state[:, 2, t, :] for t in range(rows)]
    for step in range(2):
        edge = 2 * step + 1
        flux = [d * e if e is not None else None for d, e in zip(deep, u)]
        new = [None] * rows
        for t in range(edge, rows - edge):
            new[t] = h[t] - mass_rate * (flux[t + 1] - flux[t - 1] + diff_cols(deep[t] * v[t]))
        h = new
        if step == 1:
            break
        east, north = [None] * rows, [None] * rows
        for t in range(edge + 1, rows - edge - 1):
            east[t] = u[t] - wave_rate * (h[t + 1] - h[t - 1]) + turn_rate * v[t]
            north[t] = v[t] - wave_rate * diff_cols(h[t]) - turn_rate * u[t]
        u, v = east, north
    for t in range(RIM, rows - RIM):
        out[t - RIM] = h[t]


def inner_heights(state, depth):
    members, _, rows, cols = state.shape
    return pl.pallas_call(
        inner_kernel,
        out_shape=jax.ShapeDtypeStruct((rows - 2 * RIM, members, cols), F32),
        in_specs=[VMEM] * 2,
        out_specs=VMEM,
        compiler_params=PARAMS,
        cost_estimate=cost(FORECAST_FLOPS, 4 * state.size),
        name="inner",
    )(state, depth)


def forecast_kernel(last, state, depth, above, below, *refs):
    held = refs[:-6]
    height_out, wind_out, h, u, v, flux = refs[-6:]
    members, _, rows, cols = state.shape
    slots = held[0].shape[0]
    deep = [jnp.broadcast_to(depth[t : t + 1], (members, cols)) for t in range(rows)]
    sides = []
    place = lax.axis_index("space")
    for ref, sign, edge, inside in (
        (above, -1.0, 0, place > 0),
        (below, 1.0, rows - 1, place < last),
    ):
        parts = [ref[i * members : (i + 1) * members] for i in range(4)]
        deeps = [
            jnp.broadcast_to(ref[4 * members + i : 4 * members + i + 1], (members, cols))
            for i in range(2)
        ]
        sides.append((parts, deeps, sign, edge, inside.astype(F32)))

    def outer(edge):
        return 0 if edge == 0 else rows + 1

    for t in range(rows):
        h[t + 1] = state[:, 0, t, :]
        u[t] = state[:, 1, t, :]
        v[t] = state[:, 2, t, :]
        flux[t + 1] = deep[t] * u[t]
    deltas = []
    for (first_flux, _, _, _), _, sign, edge, inside in sides:
        deltas.append(sign * mass_rate * flux[edge + 1])
        flux[outer(edge)] = first_flux * inside

    def new_heights():
        for t in range(rows):
            h[t + 1] = h[t + 1] - mass_rate * (flux[t + 2] - flux[t] + diff_cols(deep[t] * v[t]))

    def new_winds(put):
        for t in range(rows):
            east, north = u[t], v[t]
            put(
                t,
                east - wave_rate * (h[t + 2] - h[t]) + turn_rate * north,
                north - wave_rate * diff_cols(h[t + 1]) - turn_rate * east,
            )

    def keep(t, east, north):
        u[t], v[t] = east, north
        flux[t + 1] = deep[t] * east

    def emit(t, east, north):
        wind_out[t] = east
        wind_out[rows + t] = north

    new_heights()
    for delta, ((_, first, east, _), deeps, sign, edge, inside) in zip(deltas, sides):
        h[outer(edge)] = (first + delta) * inside
        flux[outer(edge)] = inside * deeps[0] * (east + sign * wave_rate * h[edge + 1])
    new_winds(keep)
    rims = []
    for delta, ((_, _, _, twice), deeps, sign, edge, inside) in zip(deltas, sides):
        turned = wave_rate * diff_cols(deeps[0] * diff_cols(delta))
        change = wave_rate * deeps[1] * delta - sign * flux[edge + 1] - turned
        rims.append((edge, (twice + delta - mass_rate * change) * inside))
    new_heights()
    for edge, rim in rims:
        h[outer(edge)] = rim
    new_winds(emit)
    outer_rows = list(range(RIM)) + list(range(rows - RIM, rows))
    for i, t in enumerate(outer_rows):
        height_out[i] = h[t + 1]
    for j, piece in enumerate(held):
        at = j * slots
        height_out[2 * RIM + at // members, at % members : at % members + slots, :] = piece[...]


def forecast(last, state, depth, above, below, held):
    members, _, rows, cols = state.shape
    extra = -(-len(held) * held[0].shape[0] // members)
    return pl.pallas_call(
        functools.partial(forecast_kernel, last),
        out_shape=(
            jax.ShapeDtypeStruct((2 * RIM + extra, members, cols), F32),
            jax.ShapeDtypeStruct((2 * rows, members, cols), F32),
        ),
        in_specs=[VMEM] * (4 + len(held)),
        out_specs=(VMEM, VMEM),
        scratch_shapes=[
            pltpu.VMEM((rows + 2, members, cols), F32),
            pltpu.VMEM((rows, members, cols), F32),
            pltpu.VMEM((rows, members, cols), F32),
            pltpu.VMEM((rows + 2, members, cols), F32),
        ],
        compiler_params=PARAMS,
        cost_estimate=cost(FORECAST_FLOPS, 4 * state.size),
        name="forecast",
    )(state, depth, above, below, *held)


def interpolate(groups, cells, weights, split, put):
    _, members, cols = groups[0][0][0].shape
    total = members * len(groups[0][0])
    points, blocks, width = cells.shape
    quarter = lax.axis_index("mem")
    blocks = blocks // lax.axis_size("mem")
    first = 0
    for pieces, lines_of in groups:
        for k, piece in enumerate(pieces):
            who = lax.bitwise_xor(lax.rem(quarter, len(pieces)), k)
            for r in range(len(lines_of)):
                x = piece[r]
                high = x.astype(BF16)
                low = (x - high.astype(F32)).astype(BF16)
                at = pl.ds(pl.multiple_of((first + r) * total + who * members, members), members)
                split[at, 0:cols] = high
                split[at, cols : 2 * cols] = low
        first += len(lines_of)

    def block(b, carry):
        results = [None] * len(groups)
        line = pl.ds(quarter * blocks + b, 1)
        for half in range(points // 2):
            cell = jnp.concatenate(
                [cells[2 * half, line, :], cells[2 * half + 1, line, :]], axis=1
            )
            share = jnp.concatenate(
                [weights[2 * half, line, :], weights[2 * half + 1, line, :]], axis=1
            )
            row = cell // cols
            col = jnp.broadcast_to(cell - row * cols, (cols, 2 * width))
            here = lax.broadcasted_iota(jnp.int32, (cols, 2 * width), 0) == col
            pick = jnp.where(here, 1.0, 0.0).astype(BF16)
            lines = jnp.dot(
                split[...], jnp.concatenate([pick, pick], axis=0), preferred_element_type=F32
            )
            first = 0
            for g, (_, lines_of) in enumerate(groups):
                for r, at in enumerate(lines_of):
                    term = lines[(first + r) * total : (first + r + 1) * total]
                    term = term * jnp.where(row == at, share, 0.0)
                    term = term[:, :width] + term[:, width:]
                    results[g] = term if results[g] is None else results[g] + term
                first += len(lines_of)
        put(b, *results)
        return carry

    lax.fori_loop(0, blocks, block, 0, unroll=16)


def collect(got, pieces):
    members = pieces[0].shape[1]
    rows = 2 * RIM
    slots = got.shape[1]
    peers = got.shape[0] // len(pieces)
    for k, piece in enumerate(pieces):
        for j in range(peers):
            at = j * slots
            got[k * peers + j] = piece[rows + at // members, at % members : at % members + slots, :]


def block_lines(owners, share, spaces, slots, peers):
    space, quarter = lax.axis_index("space"), lax.axis_index("mem")
    quarters = lax.axis_size("mem")
    shift = quarters.bit_length() - 1
    blocks = owners.shape[1]
    lane = lax.broadcasted_iota(jnp.int32, (share, blocks), 1)
    line = lax.broadcasted_iota(jnp.int32, (share, blocks), 0) + quarter * share
    row = jnp.broadcast_to(owners[...], (share, blocks)).astype(F32)
    mine = jnp.sum(jnp.where(lane == line, row, 0.0), axis=1, keepdims=True)
    slot = jnp.sum(jnp.where((row == mine) & (lane < line), 1.0, 0.0), axis=1, keepdims=True)
    apart = mine.astype(jnp.int32) - space
    apart = jnp.where(apart < 0, apart + spaces, apart)
    index = jnp.where(apart <= spaces // 2, 2 * (apart - 2), 2 * (spaces - apart - 2) + 1)
    who = lax.bitwise_xor(lax.bitwise_and(index, quarters - 1), quarter)
    spot = 3 + who * peers + lax.shift_right_arithmetic(index, shift)
    spot = jnp.where(index >= peers * quarters, 3 + index, spot)
    spot = jnp.where(apart <= 1, apart, spot)
    spot = jnp.where(apart == spaces - 1, 2, spot)
    return spot * slots + slot.astype(jnp.int32)


def near_inner_kernel(lines_of, count, *refs):
    pieces = refs[:count]
    cells, weights, owners, out, owners_out, split = refs[count:]
    owners_out[...] = owners[...]

    def put(b, result):
        out[b] = result

    interpolate([(pieces, lines_of)], cells, weights, split, put)


def middle_kernel(inner_rows, outer_rows, count, *refs):
    far, near = refs[:count], refs[count : 2 * count]
    cells, weights, early, own, above, below, out, out_far, got, split = refs[2 * count :]
    got[0] = own[...]
    rim = below.shape[0] - own.shape[0]
    got[1] = below[rim:]
    got[2] = above[rim:]
    collect(got.at[3:], near)

    def put(b, result_far, result):
        out_far[b] = result_far
        out[b] = result + early[b]

    interpolate([(far, inner_rows), (near, outer_rows)], cells, weights, split, put)


def gram_kernel(lines_of, scale, count, count_mem, peers, owners, *refs):
    pieces = refs[:count]
    cells, weights, near, early, early_far = refs[count : count + 5]
    direct = refs[count + 5 : -5]
    keep, give, split, lined, got = refs[-5:]
    _, members, cols = pieces[0].shape
    total = members * count_mem
    part = members * count
    blocks, width = cells.shape[1] // count_mem, cells.shape[2]
    quarter = lax.axis_index("mem")
    got[0 : near.shape[0]] = near[...]
    later = got.shape[0] - len(direct)
    collect(got.at[near.shape[0] : later], pieces)
    for i, piece in enumerate(direct):
        got[later + i] = piece[...]

    mine = quarter // count
    base = pl.multiple_of(mine * part, part)
    final = pl.multiple_of(lax.bitwise_xor(mine, 1) * part, part)

    def put(b, result):
        at = pl.ds(pl.multiple_of(b * width, width), width)
        lined[pl.ds(final, part), at] = result + early_far[b]
        lined[pl.ds(base, part), at] = early[b]

    interpolate([(pieces, lines_of)], cells, weights, split, put)
    lined[total : 2 * total] = jnp.zeros((total, blocks * width), F32)
    spaces, slots, across = got.shape
    picks = block_lines(owners, blocks, spaces, slots, peers)
    lane = lax.broadcasted_iota(jnp.int32, (blocks, spaces * slots), 1)
    taken = jnp.dot(
        jnp.where(lane == picks, 1.0, 0.0),
        got[...].reshape(spaces * slots, across),
        precision=lax.Precision.HIGHEST,
        preferred_element_type=F32,
    )
    for b in range(blocks):
        line = taken[b : b + 1]
        seen, much = line[:, 0:width], line[:, width : 2 * width] * scale
        at = pl.ds(b * width, width)
        values = lined[0:total, at]
        middle = jnp.sum(values, axis=0, keepdims=True) * (1.0 / total)
        lined[0:total, at] = (values - middle) * much
        lined[total : total + 1, at] = (seen - middle) * much

    x = lined[...]
    high = x.astype(BF16)
    low = (x - high.astype(F32)).astype(BF16)
    turned = (((1,), (1,)), ((), ()))
    gram = lax.dot_general(high, high, turned, preferred_element_type=F32)
    cross = lax.dot_general(high, low, turned, preferred_element_type=F32)
    gram = gram + (cross + cross.T)
    packed = pack_gram(gram, total)
    half = keep.shape[0]
    odd = lax.rem(quarter, 2) == 1
    for r in range(half):
        low, high = packed[r : r + 1], packed[half + r : half + r + 1]
        keep[r] = jnp.where(odd, high, low)
        give[r] = jnp.where(odd, low, high)


def spread_kernel(keep, given, out):
    both = keep[...] + given[...]
    for d in range(out.shape[0]):
        out[d] = both


def pack_gram(gram, total):
    half, quarter = total // 2, total // 4
    span = 2 * total
    top, low = gram[0:half], gram[half:total]
    lane = lax.broadcasted_iota(jnp.int32, (half, span), 1)
    line = lax.broadcasted_iota(jnp.int32, (half, span), 0)
    both = jnp.where(lane <= line, top, pltpu.roll(low, span - half, 1))
    wide = jnp.where(lane < half, both, pltpu.roll(low, half, 1))
    lane_q = lane[0:quarter]
    body = jnp.where(lane_q < total, wide[0:quarter], pltpu.roll(wide[quarter:half], total, 1))
    diag = jnp.sum(jnp.where(lane == line + half, low, 0.0), axis=0, keepdims=True)
    lane_1 = lane[0:8]
    tail = jnp.where(
        lane_1 < total, gram[total : total + 8], pltpu.roll(jnp.broadcast_to(diag, (8, span)), half, 1)
    )
    return jnp.concatenate([body, tail], axis=0)


def unpack_gram(packed, total):
    half, quarter = total // 2, total // 4
    span = 2 * total
    body, tail = packed[0:quarter], packed[quarter : quarter + 1]
    wide = jnp.concatenate([body, pltpu.roll(body, total, 1)], axis=0)
    low = pltpu.roll(wide, span - half, 1)
    lane = lax.broadcasted_iota(jnp.int32, (half, span), 1)
    line = lax.broadcasted_iota(jnp.int32, (half, span), 0)
    first = lane < half
    stacked = jnp.concatenate(
        [jnp.where(first, wide, 0.0), jnp.where(first, low, 0.0), jnp.zeros((total, span), F32)], axis=0
    )
    turned = stacked.T[0:half]
    top = jnp.where(first & (lane <= line), wide, turned)
    diag = pltpu.roll(jnp.broadcast_to(tail, (half, span)), span - half, 1)
    corner = jnp.where(lane > line, wide, turned)
    corner = pltpu.roll(jnp.where(first, corner, 0.0), half, 1)
    corner = jnp.where(lane == line + half, diag, corner)
    bottom = jnp.where(first, low, corner)
    return jnp.concatenate([top, bottom], axis=0), tail


def factor_inverse(system, total):
    span = 2 * total
    lane = lax.broadcasted_iota(jnp.int32, (total, span), 1)
    line = lax.broadcasted_iota(jnp.int32, (total, span), 0)
    work = jnp.where(lane < total, system, jnp.where(lane == line + total, 1.0, 0.0))
    tiles = [work[8 * g : 8 * g + 8] for g in range(total // 8)]
    step = 8
    below = lax.broadcasted_iota(jnp.int32, (8, span), 0)

    def lanes(x, k):
        return jnp.broadcast_to(x[:, k : k + 1], (8, span))

    def lines(x, s):
        return jnp.broadcast_to(x[s : s + 1], (8, span))

    for k in range(0, total, step):
        g, s = k // 8, k % 8
        columns = {t: [lanes(tiles[t], k + i) for i in range(step)] for t in range(g, total // 8)}
        pivots = [lines(tiles[g], s + i) for i in range(step)]
        block = [[lines(columns[g][j], s + i) for j in range(i + 1)] for i in range(step)]
        for j in range(step):
            scale = 1.0 / block[j][j]
            ratio = [None] * step
            for i in range(j + 1, step):
                ratio[i] = block[i][j] * scale
            for i in range(j + 1, step):
                for n in range(j + 1, i + 1):
                    block[i][n] = block[i][n] - ratio[i] * block[n][j]
                pivots[i] = pivots[i] - ratio[i] * pivots[j]
            scaled = pivots[j] * scale
            for t in columns:
                for i in range(j + 1, step):
                    columns[t][i] = columns[t][i] - ratio[i] * columns[t][j]
            for t in columns:
                column = columns[t][j]
                if t == g:
                    if s + j == 7:
                        continue
                    column = jnp.where(below > s + j, column, 0.0)
                tiles[t] = tiles[t] - column * scaled
    work = jnp.concatenate(tiles, axis=0)
    diag = jnp.sum(jnp.where(lane == line, work, 0.0), axis=1, keepdims=True)
    return jnp.where(lane < total, pltpu.roll(work, total, 1), 0.0) / jnp.sqrt(diag)


def mixing_columns(packed, total, members, count_mem, lower):
    span = 2 * total
    quarter = lax.axis_index("mem")
    system, proj = unpack_gram(packed, total)
    lane = lax.broadcasted_iota(jnp.int32, (total, span), 1)
    line = lax.broadcasted_iota(jnp.int32, (total, span), 0)
    inverse = factor_inverse(system + jnp.where(lane == line, float(total - 1), 0.0), total)
    first = jnp.sum(jnp.where(lane < total, inverse * proj, 0.0), axis=1, keepdims=True)
    mean_weights = jnp.sum(inverse * first, axis=0, keepdims=True)
    lower[...] = inverse
    mine = lower[pl.ds(pl.multiple_of(quarter * members, members), members)]
    coef = mean_weights + math.sqrt(total - 1) * mine
    short = lane[0:members]
    coef = jnp.where(short < total, coef, 0.0)
    mixing = coef + (1.0 - jnp.sum(coef, axis=1, keepdims=True)) * (1.0 / total)
    bit = 1
    while bit < count_mem:
        size = bit * members
        turned = jnp.where(
            lax.rem(short // size, 2) == 0, pltpu.roll(mixing, span - size, 1), pltpu.roll(mixing, size, 1)
        )
        swapped = (lax.rem(quarter // bit, 2) == 1).astype(F32)
        mixing = mixing + swapped * (turned - mixing)
        bit *= 2
    return mixing[:, 0:total]


def analysis_kernel(count_mem, sums, *refs):
    inner, outer, *winds = [refs[f * count_mem : (f + 1) * count_mem] for f in range(4)]
    out, lower = refs[4 * count_mem :]
    rows, members, cols = winds[0][0].shape
    total = members * count_mem

    halves = [sums[0], sums[1]]
    for d in range(2, sums.shape[0]):
        halves[d % 2] = halves[d % 2] + sums[d]
    packed = jnp.concatenate([half[r] for half in halves for r in range(half.shape[0])], axis=0)
    mixing = mixing_columns(packed, total, members, count_mem, lower)
    high = mixing.astype(BF16)
    low = (mixing - high.astype(F32)).astype(BF16)
    left = jnp.concatenate([high, high, low], axis=1)
    for field in range(3):
        for r in range(rows):
            if field > 0:
                pieces = [piece[r] for piece in winds[field - 1]]
            elif RIM <= r < rows - RIM:
                pieces = [piece[r - RIM] for piece in inner]
            else:
                pieces = [piece[r if r < RIM else r - rows + 2 * RIM] for piece in outer]
            upper = [x.astype(BF16) for x in pieces]
            rest = [(x - y.astype(F32)).astype(BF16) for x, y in zip(pieces, upper)]
            stack = jnp.concatenate(upper + rest + upper, axis=0)
            out[:, field, r, :] = jnp.dot(left, stack, preferred_element_type=F32)


def swap(x, axis, bit):
    count = lax.axis_size(axis)
    return lax.ppermute(x, axis, [(i, i ^ bit) for i in range(count)])


def after(x, *others):
    return lax.optimization_barrier((x,) + others)[0]


def local(state, depth, obs_cells, obs_weights, owner_map, obs_values, obs_precision):
    members, fields, rows, cols = state.shape
    count = lax.axis_size("space")
    count_mem = lax.axis_size("mem")
    total = members * count_mem
    blocks, width = obs_cells.shape[1:]
    share = blocks // count_mem
    scale = math.sqrt((total - 1) / (count * blocks * width))

    peers = (count - 3) // count_mem

    to_above, to_below, own, *blocks_out = edges(peers, state, depth, obs_values, obs_precision)
    ends = count - 1
    below = lax.ppermute(to_above, "space", [((i + 1) % count, i) for i in range(count)])
    above = lax.ppermute(to_below, "space", [(i, (i + 1) % count) for i in range(count)])
    held = [
        lax.ppermute(
            piece,
            ("space", "mem"),
            [
                (s * count_mem + q, (s - far_shift(j * count_mem + q)) % count * count_mem + q)
                for s in range(count)
                for q in range(count_mem)
            ],
        )
        for j, piece in enumerate(blocks_out[:peers])
    ]
    near, far = 1, count_mem // 2
    inner_rows = list(range(RIM, rows - RIM))
    outer_rows = list(range(RIM)) + list(range(rows - RIM, rows))
    early = jax.ShapeDtypeStruct((share, far * members, width), F32)
    owners = owner_map.reshape(1, blocks)

    def work(lines_of):
        return dict(
            compiler_params=PARAMS,
            cost_estimate=cost(
                4 * obs_cells.shape[0] * share * width * len(lines_of) * members * far * cols,
                4 * len(lines_of) * members * cols * far,
            ),
        )

    def split(lines_of):
        return pltpu.VMEM((len(lines_of) * far * members, 2 * cols), BF16)

    inner = {0: inner_heights(state, after(depth, to_above))}
    inner[near] = swap(inner[0], "mem", near)
    (inner[0],) = hold([inner[0]], inner[near])
    inner[far] = swap(inner[0], "mem", far)
    inner[far + near] = swap(inner[0], "mem", far + near)
    first, owners = pl.pallas_call(
        functools.partial(near_inner_kernel, inner_rows, far),
        out_shape=(early, jax.ShapeDtypeStruct(owners.shape, owners.dtype)),
        in_specs=[VMEM] * (far + 3),
        out_specs=(VMEM, VMEM),
        scratch_shapes=[split(inner_rows)],
        name="near_inner",
        **work(inner_rows),
    )(inner[0], inner[near], obs_cells, obs_weights, owners)

    above, below = (after(x, first) for x in (above, below))
    height, *parts = forecast(ends, state, depth, above, below, held)
    outer = {0: height}
    outer[far] = swap(height, "mem", far)
    direct = []
    for i, piece in enumerate(blocks_out[peers:]):
        shift = far_shift(peers * count_mem + i)
        ring = [(s, (s - shift) % count) for s in range(count)]
        direct.append(lax.ppermute(after(piece, height), "space", ring))
    outer[near] = swap(height, "mem", near)
    outer[far + near] = swap(height, "mem", far + near)
    near_shape = (3 + far * peers, obs_values.shape[2], cols)
    first, second, near_blocks = pl.pallas_call(
        functools.partial(middle_kernel, inner_rows, outer_rows, far),
        out_shape=(early, early, jax.ShapeDtypeStruct(near_shape, F32)),
        in_specs=[VMEM] * (2 * far + 6),
        out_specs=(VMEM,) * 3,
        scratch_shapes=[split(inner_rows + outer_rows)],
        name="middle",
        **work(inner_rows + outer_rows),
    )(
        *[inner[k] for k in range(far, 2 * far)],
        *[outer[k] for k in range(far)],
        obs_cells,
        obs_weights,
        first,
        own,
        above,
        below,
    )
    parts = hold(parts, outer[far], outer[far + near], second, *direct)
    both = {0: parts[0], far: swap(parts[0], "mem", far)}
    winds = [{k: x[i * rows : (i + 1) * rows] for k, x in both.items()} for i in range(2)]
    for wind in winds:
        wind[near] = swap(wind[0], "mem", near)
        wind[far + near] = swap(wind[far], "mem", near)
    inner, outer = ([x[k] for k in range(count_mem)] for x in (inner, outer))
    winds = [wind[k] for wind in winds for k in range(count_mem)]

    half = (total // 4 + 2) // 2
    devices = count * count_mem
    part = jax.ShapeDtypeStruct((half, 1, 2 * total), F32)
    keep, give = pl.pallas_call(
        functools.partial(gram_kernel, outer_rows, scale, far, count_mem, peers),
        out_shape=(part, part),
        in_specs=[VMEM] * (far + 6 + len(direct)),
        out_specs=(VMEM, VMEM),
        scratch_shapes=[
            split(outer_rows),
            pltpu.VMEM((2 * total, share * width), F32),
            pltpu.VMEM((count,) + near_shape[1:], F32),
        ],
        name="gram",
        **work(outer_rows),
    )(owners, *outer[far:], obs_cells, obs_weights, near_blocks, first, second, *direct)
    sent = pl.pallas_call(
        spread_kernel,
        out_shape=jax.ShapeDtypeStruct((devices,) + part.shape, F32),
        in_specs=[VMEM, VMEM],
        out_specs=VMEM,
        compiler_params=PARAMS,
        name="spread",
    )(keep, swap(give, "mem", near))
    sums = lax.all_to_all(sent, ("space", "mem"), split_axis=0, concat_axis=0, tiled=True)

    return pl.pallas_call(
        functools.partial(analysis_kernel, count_mem),
        out_shape=jax.ShapeDtypeStruct(state.shape, F32),
        in_specs=[VMEM] * (1 + 4 * count_mem),
        out_specs=VMEM,
        scratch_shapes=[pltpu.VMEM((total, 2 * total), F32)],
        compiler_params=PARAMS,
        name="analysis",
    )(sums, *inner, *outer, *winds)


def solution(mesh):
    return jax.shard_map(
        local,
        mesh=mesh,
        in_specs=(
            P("mem", None, "space", None),
            P("space", None),
            P(None, "space", None),
            P(None, "space", None),
            P("space", None),
            P("space", None, None, None),
            P("space", None, None, None),
        ),
        out_specs=P("mem", None, "space", None),
        check_vma=False,
    )
```

```python
import functools
import math

import jax
import jax.numpy as jnp
from jax import lax
from jax.experimental import pallas as pl
from jax.experimental.pallas import tpu as pltpu
from jax.sharding import PartitionSpec as P

mass_rate = 0.2
wave_rate = 0.2
turn_rate = 0.1

ANY = pl.BlockSpec(memory_space=pl.ANY)
VMEM = pl.BlockSpec(memory_space=pltpu.VMEM)
HBM = pl.BlockSpec(memory_space=pltpu.HBM)
SMEM = pl.BlockSpec(memory_space=pltpu.SMEM)
F32 = jnp.float32
BF16 = jnp.bfloat16
PARAMS = pltpu.CompilerParams(vmem_limit_bytes=12 * 1024 * 1024)
FORECAST_FLOPS = 2 * 10**9
RIM = 3


def hold(arrays, *others):
    return pl.pallas_call(
        lambda *refs: None,
        out_shape=tuple(jax.ShapeDtypeStruct(x.shape, x.dtype) for x in arrays),
        in_specs=[ANY] * (len(arrays) + len(others)),
        out_specs=(ANY,) * len(arrays),
        input_output_aliases={i: i for i in range(len(arrays))},
        compiler_params=PARAMS,
        cost_estimate=cost(1, 1),
        name="hold",
    )(*arrays, *others)


def cost(flops, size):
    return pl.CostEstimate(flops=flops, bytes_accessed=size, transcendentals=0)


def diff_cols(field):
    width = field.shape[-1]
    return pltpu.roll(field, width - 1, 1) - pltpu.roll(field, 1, 1)


def far_shift(index):
    half = 2 + index // 2
    return half - 2 * half * (index % 2)


def edge_kernel(peers, state_in, depth_in, values, precision, above, below, own, *refs):
    held = refs[:-5]
    state, depth, seen, weight, sems = refs[-5:]
    members, _, rows, cols = state.shape
    width = values.shape[-1]
    half = members // 2
    copies = [
        pltpu.make_async_copy(state_in.at[0:half], state.at[0:half], sems.at[0]),
        pltpu.make_async_copy(state_in.at[half:members], state.at[half:members], sems.at[1]),
        pltpu.make_async_copy(depth_in, depth, sems.at[2]),
    ]
    place, count = lax.axis_index("space"), values.shape[1]
    peers_of = [place, lax.rem(place + count - 1, count), lax.rem(place + 1, count)]
    quarters = lax.axis_size("mem")
    for j in range(peers):
        index = j * quarters + lax.axis_index("mem")
        half = 2 + lax.div(index, 2)
        shift = half - 2 * half * lax.rem(index, 2)
        peers_of.append(lax.rem(place + 2 * count - shift, count))
    for index in range(peers * quarters, count - 3):
        peers_of.append(lax.rem(place + 2 * count - far_shift(index), count))
    for j, peer in enumerate(peers_of):
        copies.append(pltpu.make_async_copy(values.at[0, peer], seen.at[j], sems.at[3 + 2 * j]))
        copies.append(pltpu.make_async_copy(precision.at[0, peer], weight.at[j], sems.at[4 + 2 * j]))
    for copy in copies:
        copy.start()
    for copy in copies:
        copy.wait()
    for out, sign, at in ((above, 1.0, range(4)), (below, -1.0, range(rows - 1, rows - 5, -1))):
        deep = [jnp.broadcast_to(depth[t : t + 1], (members, cols)) for t in at]
        h = [state[:, 0, t, :] for t in at]
        u = [state[:, 1, t, :] for t in at]
        v = [state[:, 2, t, :] for t in at]
        flux = [d * e for d, e in zip(deep, u)]
        first = h[0] - mass_rate * (sign * flux[1] + diff_cols(deep[0] * v[0]))
        second, third = (
            h[i] - mass_rate * (sign * (flux[i + 1] - flux[i - 1]) + diff_cols(deep[i] * v[i]))
            for i in (1, 2)
        )
        east = u[0] - wave_rate * sign * second + turn_rate * v[0]
        east_next = u[1] - wave_rate * sign * third + turn_rate * v[1]
        north = v[0] - turn_rate * u[0] - wave_rate * diff_cols(first)
        twice = first - mass_rate * (
            sign * deep[1] * (east_next + sign * wave_rate * first) + diff_cols(deep[0] * north)
        )
        for i, part in enumerate((flux[0], first, east, twice)):
            out[i * members : (i + 1) * members] = part
        out[4 * members : 4 * members + 8] = jnp.concatenate(
            [deep[0][0:1], deep[1][0:1], jnp.zeros((6, cols), F32)], axis=0
        )
    rim = 4 * members + 8
    slots = seen.shape[1]
    places = [own, above.at[rim : rim + slots], below.at[rim : rim + slots]] + list(held)
    for j, out in enumerate(places):
        out[:, 0:width] = seen[j]
        out[:, width : 2 * width] = weight[j]


def edges(peers, state, depth, values, precision):
    members, _, _, cols = state.shape
    slots = values.shape[2]
    rim = jax.ShapeDtypeStruct((4 * members + 8 + slots, cols), F32)
    held = jax.ShapeDtypeStruct((slots, cols), F32)
    owners = peers + (values.shape[1] - 3) % lax.axis_size("mem")
    return pl.pallas_call(
        functools.partial(edge_kernel, peers),
        out_shape=(rim, rim, held) + (held,) * owners,
        in_specs=[HBM] * 4,
        out_specs=(VMEM,) * (3 + owners),
        scratch_shapes=[
            pltpu.VMEM(state.shape, F32),
            pltpu.VMEM(depth.shape, F32),
            pltpu.VMEM((3 + owners,) + values.shape[2:], F32),
            pltpu.VMEM((3 + owners,) + values.shape[2:], F32),
            pltpu.SemaphoreType.DMA((9 + 2 * owners,)),
        ],
        compiler_params=pltpu.CompilerParams(vmem_limit_bytes=56 * 1024 * 1024),
        name="edges",
    )(state, depth, values, precision)


def inner_kernel(state, depth, out):
    members, _, rows, cols = state.shape
    deep = [jnp.broadcast_to(depth[t : t + 1], (members, cols)) for t in range(rows)]
    h = [state[:, 0, t, :] for t in range(rows)]
    u = [state[:, 1, t, :] for t in range(rows)]
    v = [state[:, 2, t, :] for t in range(rows)]
    for step in range(2):
        edge = 2 * step + 1
        flux = [d * e if e is not None else None for d, e in zip(deep, u)]
        new = [None] * rows
        for t in range(edge, rows - edge):
            new[t] = h[t] - mass_rate * (flux[t + 1] - flux[t - 1] + diff_cols(deep[t] * v[t]))
        h = new
        if step == 1:
            break
        east, north = [None] * rows, [None] * rows
        for t in range(edge + 1, rows - edge - 1):
            east[t] = u[t] - wave_rate * (h[t + 1] - h[t - 1]) + turn_rate * v[t]
            north[t] = v[t] - wave_rate * diff_cols(h[t]) - turn_rate * u[t]
        u, v = east, north
    for t in range(RIM, rows - RIM):
        out[t - RIM] = h[t]


def inner_heights(state, depth):
    members, _, rows, cols = state.shape
    return pl.pallas_call(
        inner_kernel,
        out_shape=jax.ShapeDtypeStruct((rows - 2 * RIM, members, cols), F32),
        in_specs=[VMEM] * 2,
        out_specs=VMEM,
        compiler_params=PARAMS,
        cost_estimate=cost(FORECAST_FLOPS, 4 * state.size),
        name="inner",
    )(state, depth)


def forecast_kernel(last, state, depth, above, below, *refs):
    held = refs[:-6]
    height_out, wind_out, h, u, v, flux = refs[-6:]
    members, _, rows, cols = state.shape
    slots = held[0].shape[0]
    deep = [jnp.broadcast_to(depth[t : t + 1], (members, cols)) for t in range(rows)]
    sides = []
    place = lax.axis_index("space")
    for ref, sign, edge, inside in (
        (above, -1.0, 0, place > 0),
        (below, 1.0, rows - 1, place < last),
    ):
        parts = [ref[i * members : (i + 1) * members] for i in range(4)]
        deeps = [
            jnp.broadcast_to(ref[4 * members + i : 4 * members + i + 1], (members, cols))
            for i in range(2)
        ]
        sides.append((parts, deeps, sign, edge, inside.astype(F32)))

    def outer(edge):
        return 0 if edge == 0 else rows + 1

    for t in range(rows):
        h[t + 1] = state[:, 0, t, :]
        u[t] = state[:, 1, t, :]
        v[t] = state[:, 2, t, :]
        flux[t + 1] = deep[t] * u[t]
    deltas = []
    for (first_flux, _, _, _), _, sign, edge, inside in sides:
        deltas.append(sign * mass_rate * flux[edge + 1])
        flux[outer(edge)] = first_flux * inside

    def new_heights():
        for t in range(rows):
            h[t + 1] = h[t + 1] - mass_rate * (flux[t + 2] - flux[t] + diff_cols(deep[t] * v[t]))

    def new_winds(put):
        for t in range(rows):
            east, north = u[t], v[t]
            put(
                t,
                east - wave_rate * (h[t + 2] - h[t]) + turn_rate * north,
                north - wave_rate * diff_cols(h[t + 1]) - turn_rate * east,
            )

    def keep(t, east, north):
        u[t], v[t] = east, north
        flux[t + 1] = deep[t] * east

    def emit(t, east, north):
        wind_out[t] = east
        wind_out[rows + t] = north

    new_heights()
    for delta, ((_, first, east, _), deeps, sign, edge, inside) in zip(deltas, sides):
        h[outer(edge)] = (first + delta) * inside
        flux[outer(edge)] = inside * deeps[0] * (east + sign * wave_rate * h[edge + 1])
    new_winds(keep)
    rims = []
    for delta, ((_, _, _, twice), deeps, sign, edge, inside) in zip(deltas, sides):
        turned = wave_rate * diff_cols(deeps[0] * diff_cols(delta))
        change = wave_rate * deeps[1] * delta - sign * flux[edge + 1] - turned
        rims.append((edge, (twice + delta - mass_rate * change) * inside))
    new_heights()
    for edge, rim in rims:
        h[outer(edge)] = rim
    new_winds(emit)
    outer_rows = list(range(RIM)) + list(range(rows - RIM, rows))
    for i, t in enumerate(outer_rows):
        height_out[i] = h[t + 1]
    for j, piece in enumerate(held):
        at = j * slots
        height_out[2 * RIM + at // members, at % members : at % members + slots, :] = piece[...]


def forecast(last, state, depth, above, below, held):
    members, _, rows, cols = state.shape
    extra = -(-len(held) * held[0].shape[0] // members)
    return pl.pallas_call(
        functools.partial(forecast_kernel, last),
        out_shape=(
            jax.ShapeDtypeStruct((2 * RIM + extra, members, cols), F32),
            jax.ShapeDtypeStruct((2 * rows, members, cols), F32),
        ),
        in_specs=[VMEM] * (4 + len(held)),
        out_specs=(VMEM, VMEM),
        scratch_shapes=[
            pltpu.VMEM((rows + 2, members, cols), F32),
            pltpu.VMEM((rows, members, cols), F32),
            pltpu.VMEM((rows, members, cols), F32),
            pltpu.VMEM((rows + 2, members, cols), F32),
        ],
        compiler_params=PARAMS,
        cost_estimate=cost(FORECAST_FLOPS, 4 * state.size),
        name="forecast",
    )(state, depth, above, below, *held)


def interpolate(groups, cells, weights, split, put):
    _, members, cols = groups[0][0][0].shape
    total = members * len(groups[0][0])
    points, blocks, width = cells.shape
    quarter = lax.axis_index("mem")
    blocks = blocks // lax.axis_size("mem")
    first = 0
    for pieces, lines_of in groups:
        for k, piece in enumerate(pieces):
            who = lax.bitwise_xor(lax.rem(quarter, len(pieces)), k)
            for r in range(len(lines_of)):
                x = piece[r]
                high = x.astype(BF16)
                low = (x - high.astype(F32)).astype(BF16)
                at = pl.ds(pl.multiple_of((first + r) * total + who * members, members), members)
                split[at, 0:cols] = high
                split[at, cols : 2 * cols] = low
        first += len(lines_of)

    def block(b, carry):
        results = [None] * len(groups)
        line = pl.ds(quarter * blocks + b, 1)
        for half in range(points // 2):
            cell = jnp.concatenate(
                [cells[2 * half, line, :], cells[2 * half + 1, line, :]], axis=1
            )
            share = jnp.concatenate(
                [weights[2 * half, line, :], weights[2 * half + 1, line, :]], axis=1
            )
            row = cell // cols
            col = jnp.broadcast_to(cell - row * cols, (cols, 2 * width))
            here = lax.broadcasted_iota(jnp.int32, (cols, 2 * width), 0) == col
            pick = jnp.where(here, 1.0, 0.0).astype(BF16)
            lines = jnp.dot(
                split[...], jnp.concatenate([pick, pick], axis=0), preferred_element_type=F32
            )
            first = 0
            for g, (_, lines_of) in enumerate(groups):
                for r, at in enumerate(lines_of):
                    term = lines[(first + r) * total : (first + r + 1) * total]
                    term = term * jnp.where(row == at, share, 0.0)
                    term = term[:, :width] + term[:, width:]
                    results[g] = term if results[g] is None else results[g] + term
                first += len(lines_of)
        put(b, *results)
        return carry

    lax.fori_loop(0, blocks, block, 0, unroll=16)


def collect(got, pieces):
    members = pieces[0].shape[1]
    rows = 2 * RIM
    slots = got.shape[1]
    peers = got.shape[0] // len(pieces)
    for k, piece in enumerate(pieces):
        for j in range(peers):
            at = j * slots
            got[k * peers + j] = piece[rows + at // members, at % members : at % members + slots, :]


def block_lines(owners, share, spaces, slots, peers):
    space, quarter = lax.axis_index("space"), lax.axis_index("mem")
    quarters = lax.axis_size("mem")
    shift = quarters.bit_length() - 1
    blocks = owners.shape[1]
    lane = lax.broadcasted_iota(jnp.int32, (share, blocks), 1)
    line = lax.broadcasted_iota(jnp.int32, (share, blocks), 0) + quarter * share
    row = jnp.broadcast_to(owners[...], (share, blocks)).astype(F32)
    mine = jnp.sum(jnp.where(lane == line, row, 0.0), axis=1, keepdims=True)
    slot = jnp.sum(jnp.where((row == mine) & (lane < line), 1.0, 0.0), axis=1, keepdims=True)
    apart = mine.astype(jnp.int32) - space
    apart = jnp.where(apart < 0, apart + spaces, apart)
    index = jnp.where(apart <= spaces // 2, 2 * (apart - 2), 2 * (spaces - apart - 2) + 1)
    who = lax.bitwise_xor(lax.bitwise_and(index, quarters - 1), quarter)
    spot = 3 + who * peers + lax.shift_right_arithmetic(index, shift)
    spot = jnp.where(index >= peers * quarters, 3 + index, spot)
    spot = jnp.where(apart <= 1, apart, spot)
    spot = jnp.where(apart == spaces - 1, 2, spot)
    return spot * slots + slot.astype(jnp.int32)


def near_inner_kernel(lines_of, count, *refs):
    pieces = refs[:count]
    cells, weights, owners, out, owners_out, split = refs[count:]
    owners_out[...] = owners[...]

    def put(b, result):
        out[b] = result

    interpolate([(pieces, lines_of)], cells, weights, split, put)


def middle_kernel(inner_rows, outer_rows, count, *refs):
    far, near = refs[:count], refs[count : 2 * count]
    cells, weights, early, own, above, below, out, out_far, got, split = refs[2 * count :]
    got[0] = own[...]
    rim = below.shape[0] - own.shape[0]
    got[1] = below[rim:]
    got[2] = above[rim:]
    collect(got.at[3:], near)

    def put(b, result_far, result):
        out_far[b] = result_far
        out[b] = result + early[b]

    interpolate([(far, inner_rows), (near, outer_rows)], cells, weights, split, put)


def gram_kernel(lines_of, scale, count, count_mem, peers, owners, *refs):
    pieces = refs[:count]
    cells, weights, near, early, early_far = refs[count : count + 5]
    direct = refs[count + 5 : -5]
    keep, give, split, lined, got = refs[-5:]
    _, members, cols = pieces[0].shape
    total = members * count_mem
    part = members * count
    blocks, width = cells.shape[1] // count_mem, cells.shape[2]
    quarter = lax.axis_index("mem")
    got[0 : near.shape[0]] = near[...]
    later = got.shape[0] - len(direct)
    collect(got.at[near.shape[0] : later], pieces)
    for i, piece in enumerate(direct):
        got[later + i] = piece[...]

    mine = quarter // count
    base = pl.multiple_of(mine * part, part)
    final = pl.multiple_of(lax.bitwise_xor(mine, 1) * part, part)

    def put(b, result):
        at = pl.ds(pl.multiple_of(b * width, width), width)
        lined[pl.ds(final, part), at] = result + early_far[b]
        lined[pl.ds(base, part), at] = early[b]

    interpolate([(pieces, lines_of)], cells, weights, split, put)
    lined[total : 2 * total] = jnp.zeros((total, blocks * width), F32)
    spaces, slots, across = got.shape
    picks = block_lines(owners, blocks, spaces, slots, peers)
    lane = lax.broadcasted_iota(jnp.int32, (blocks, spaces * slots), 1)
    taken = jnp.dot(
        jnp.where(lane == picks, 1.0, 0.0),
        got[...].reshape(spaces * slots, across),
        precision=lax.Precision.HIGHEST,
        preferred_element_type=F32,
    )
    for b in range(blocks):
        line = taken[b : b + 1]
        seen, much = line[:, 0:width], line[:, width : 2 * width] * scale
        at = pl.ds(b * width, width)
        values = lined[0:total, at]
        middle = jnp.sum(values, axis=0, keepdims=True) * (1.0 / total)
        lined[0:total, at] = (values - middle) * much
        lined[total : total + 1, at] = (seen - middle) * much

    x = lined[...]
    high = x.astype(BF16)
    low = (x - high.astype(F32)).astype(BF16)
    turned = (((1,), (1,)), ((), ()))
    gram = lax.dot_general(high, high, turned, preferred_element_type=F32)
    cross = lax.dot_general(high, low, turned, preferred_element_type=F32)
    gram = gram + (cross + cross.T)
    packed = pack_gram(gram, total)
    half = keep.shape[0]
    odd = lax.rem(quarter, 2) == 1
    for r in range(half):
        low, high = packed[r : r + 1], packed[half + r : half + r + 1]
        keep[r] = jnp.where(odd, high, low)
        give[r] = jnp.where(odd, low, high)


def spread_kernel(keep, given, out):
    both = keep[...] + given[...]
    for d in range(out.shape[0]):
        out[d] = both


def pack_gram(gram, total):
    half, quarter = total // 2, total // 4
    span = 2 * total
    top, low = gram[0:half], gram[half:total]
    lane = lax.broadcasted_iota(jnp.int32, (half, span), 1)
    line = lax.broadcasted_iota(jnp.int32, (half, span), 0)
    both = jnp.where(lane <= line, top, pltpu.roll(low, span - half, 1))
    wide = jnp.where(lane < half, both, pltpu.roll(low, half, 1))
    lane_q = lane[0:quarter]
    body = jnp.where(lane_q < total, wide[0:quarter], pltpu.roll(wide[quarter:half], total, 1))
    diag = jnp.sum(jnp.where(lane == line + half, low, 0.0), axis=0, keepdims=True)
    lane_1 = lane[0:8]
    tail = jnp.where(
        lane_1 < total, gram[total : total + 8], pltpu.roll(jnp.broadcast_to(diag, (8, span)), half, 1)
    )
    return jnp.concatenate([body, tail], axis=0)


def unpack_gram(packed, total):
    half, quarter = total // 2, total // 4
    span = 2 * total
    body, tail = packed[0:quarter], packed[quarter : quarter + 1]
    wide = jnp.concatenate([body, pltpu.roll(body, total, 1)], axis=0)
    low = pltpu.roll(wide, span - half, 1)
    lane = lax.broadcasted_iota(jnp.int32, (half, span), 1)
    line = lax.broadcasted_iota(jnp.int32, (half, span), 0)
    first = lane < half
    stacked = jnp.concatenate(
        [jnp.where(first, wide, 0.0), jnp.where(first, low, 0.0), jnp.zeros((total, span), F32)], axis=0
    )
    turned = stacked.T[0:half]
    top = jnp.where(first & (lane <= line), wide, turned)
    diag = pltpu.roll(jnp.broadcast_to(tail, (half, span)), span - half, 1)
    corner = jnp.where(lane > line, wide, turned)
    corner = pltpu.roll(jnp.where(first, corner, 0.0), half, 1)
    corner = jnp.where(lane == line + half, diag, corner)
    bottom = jnp.where(first, low, corner)
    return jnp.concatenate([top, bottom], axis=0), tail


def factor_inverse(system, total):
    span = 2 * total
    lane = lax.broadcasted_iota(jnp.int32, (total, span), 1)
    line = lax.broadcasted_iota(jnp.int32, (total, span), 0)
    work = jnp.where(lane < total, system, jnp.where(lane == line + total, 1.0, 0.0))
    tiles = [work[8 * g : 8 * g + 8] for g in range(total // 8)]
    step = 8
    below = lax.broadcasted_iota(jnp.int32, (8, span), 0)

    def lanes(x, k):
        return jnp.broadcast_to(x[:, k : k + 1], (8, span))

    def lines(x, s):
        return jnp.broadcast_to(x[s : s + 1], (8, span))

    for k in range(0, total, step):
        g, s = k // 8, k % 8
        columns = {t: [lanes(tiles[t], k + i) for i in range(step)] for t in range(g, total // 8)}
        pivots = [lines(tiles[g], s + i) for i in range(step)]
        block = [[lines(columns[g][j], s + i) for j in range(i + 1)] for i in range(step)]
        for j in range(step):
            scale = 1.0 / block[j][j]
            ratio = [None] * step
            for i in range(j + 1, step):
                ratio[i] = block[i][j] * scale
            for i in range(j + 1, step):
                for n in range(j + 1, i + 1):
                    block[i][n] = block[i][n] - ratio[i] * block[n][j]
                pivots[i] = pivots[i] - ratio[i] * pivots[j]
            scaled = pivots[j] * scale
            for t in columns:
                for i in range(j + 1, step):
                    columns[t][i] = columns[t][i] - ratio[i] * columns[t][j]
            for t in columns:
                column = columns[t][j]
                if t == g:
                    if s + j == 7:
                        continue
                    column = jnp.where(below > s + j, column, 0.0)
                tiles[t] = tiles[t] - column * scaled
    work = jnp.concatenate(tiles, axis=0)
    diag = jnp.sum(jnp.where(lane == line, work, 0.0), axis=1, keepdims=True)
    return jnp.where(lane < total, pltpu.roll(work, total, 1), 0.0) / jnp.sqrt(diag)


def mixing_columns(packed, total, members, count_mem, lower):
    span = 2 * total
    quarter = lax.axis_index("mem")
    system, proj = unpack_gram(packed, total)
    lane = lax.broadcasted_iota(jnp.int32, (total, span), 1)
    line = lax.broadcasted_iota(jnp.int32, (total, span), 0)
    inverse = factor_inverse(system + jnp.where(lane == line, float(total - 1), 0.0), total)
    first = jnp.sum(jnp.where(lane < total, inverse * proj, 0.0), axis=1, keepdims=True)
    mean_weights = jnp.sum(inverse * first, axis=0, keepdims=True)
    lower[...] = inverse
    mine = lower[pl.ds(pl.multiple_of(quarter * members, members), members)]
    coef = mean_weights + math.sqrt(total - 1) * mine
    short = lane[0:members]
    coef = jnp.where(short < total, coef, 0.0)
    mixing = coef + (1.0 - jnp.sum(coef, axis=1, keepdims=True)) * (1.0 / total)
    bit = 1
    while bit < count_mem:
        size = bit * members
        turned = jnp.where(
            lax.rem(short // size, 2) == 0, pltpu.roll(mixing, span - size, 1), pltpu.roll(mixing, size, 1)
        )
        swapped = (lax.rem(quarter // bit, 2) == 1).astype(F32)
        mixing = mixing + swapped * (turned - mixing)
        bit *= 2
    return mixing[:, 0:total]


def analysis_kernel(count_mem, sums, *refs):
    inner, outer, *winds = [refs[f * count_mem : (f + 1) * count_mem] for f in range(4)]
    out, lower = refs[4 * count_mem :]
    rows, members, cols = winds[0][0].shape
    total = members * count_mem

    halves = [sums[0], sums[1]]
    for d in range(2, sums.shape[0]):
        halves[d % 2] = halves[d % 2] + sums[d]
    packed = jnp.concatenate([half[r] for half in halves for r in range(half.shape[0])], axis=0)
    mixing = mixing_columns(packed, total, members, count_mem, lower)
    high = mixing.astype(BF16)
    low = (mixing - high.astype(F32)).astype(BF16)
    left = jnp.concatenate([high, high, low], axis=1)
    for field in range(3):
        for r in range(rows):
            if field > 0:
                pieces = [piece[r] for piece in winds[field - 1]]
            elif RIM <= r < rows - RIM:
                pieces = [piece[r - RIM] for piece in inner]
            else:
                pieces = [piece[r if r < RIM else r - rows + 2 * RIM] for piece in outer]
            upper = [x.astype(BF16) for x in pieces]
            rest = [(x - y.astype(F32)).astype(BF16) for x, y in zip(pieces, upper)]
            stack = jnp.concatenate(upper + rest + upper, axis=0)
            out[:, field, r, :] = jnp.dot(left, stack, preferred_element_type=F32)


def swap(x, axis, bit):
    count = lax.axis_size(axis)
    return lax.ppermute(x, axis, [(i, i ^ bit) for i in range(count)])


def after(x, *others):
    return lax.optimization_barrier((x,) + others)[0]


def local(state, depth, obs_cells, obs_weights, owner_map, obs_values, obs_precision):
    members, fields, rows, cols = state.shape
    count = lax.axis_size("space")
    count_mem = lax.axis_size("mem")
    total = members * count_mem
    blocks, width = obs_cells.shape[1:]
    share = blocks // count_mem
    scale = math.sqrt((total - 1) / (count * blocks * width))

    peers = (count - 3) // count_mem

    to_above, to_below, own, *blocks_out = edges(peers, state, depth, obs_values, obs_precision)
    ends = count - 1
    below = lax.ppermute(to_above, "space", [((i + 1) % count, i) for i in range(count)])
    above = lax.ppermute(to_below, "space", [(i, (i + 1) % count) for i in range(count)])
    held = [
        lax.ppermute(
            piece,
            ("space", "mem"),
            [
                (s * count_mem + q, (s - far_shift(j * count_mem + q)) % count * count_mem + q)
                for s in range(count)
                for q in range(count_mem)
            ],
        )
        for j, piece in enumerate(blocks_out[:peers])
    ]
    near, far = 1, count_mem // 2
    inner_rows = list(range(RIM, rows - RIM))
    outer_rows = list(range(RIM)) + list(range(rows - RIM, rows))
    early = jax.ShapeDtypeStruct((share, far * members, width), F32)
    owners = owner_map.reshape(1, blocks)

    def work(lines_of):
        return dict(
            compiler_params=PARAMS,
            cost_estimate=cost(
                4 * obs_cells.shape[0] * share * width * len(lines_of) * members * far * cols,
                4 * len(lines_of) * members * cols * far,
            ),
        )

    def split(lines_of):
        return pltpu.VMEM((len(lines_of) * far * members, 2 * cols), BF16)

    inner = {0: inner_heights(state, after(depth, to_above))}
    inner[near] = swap(inner[0], "mem", near)
    (inner[0],) = hold([inner[0]], inner[near])
    inner[far] = swap(inner[0], "mem", far)
    first, owners = pl.pallas_call(
        functools.partial(near_inner_kernel, inner_rows, far),
        out_shape=(early, jax.ShapeDtypeStruct(owners.shape, owners.dtype)),
        in_specs=[VMEM] * (far + 3),
        out_specs=(VMEM, VMEM),
        scratch_shapes=[split(inner_rows)],
        name="near_inner",
        **work(inner_rows),
    )(inner[0], inner[near], obs_cells, obs_weights, owners)

    above, below = (after(x, first) for x in (above, below))
    height, *parts = forecast(ends, state, depth, above, below, held)
    (inner[far],) = hold([inner[far]], height)
    inner[far + near] = swap(inner[far], "mem", near)
    outer = {0: height}
    outer[far] = swap(height, "mem", far)
    direct = []
    for i, piece in enumerate(blocks_out[peers:]):
        shift = far_shift(peers * count_mem + i)
        ring = [(s, (s - shift) % count) for s in range(count)]
        direct.append(lax.ppermute(after(piece, height), "space", ring))
    outer[near] = swap(height, "mem", near)
    outer[far + near] = swap(height, "mem", far + near)
    near_shape = (3 + far * peers, obs_values.shape[2], cols)
    first, second, near_blocks = pl.pallas_call(
        functools.partial(middle_kernel, inner_rows, outer_rows, far),
        out_shape=(early, early, jax.ShapeDtypeStruct(near_shape, F32)),
        in_specs=[VMEM] * (2 * far + 6),
        out_specs=(VMEM,) * 3,
        scratch_shapes=[split(inner_rows + outer_rows)],
        name="middle",
        **work(inner_rows + outer_rows),
    )(
        *[inner[k] for k in range(far, 2 * far)],
        *[outer[k] for k in range(far)],
        obs_cells,
        obs_weights,
        first,
        own,
        above,
        below,
    )
    both = {0: parts[0], far: swap(parts[0], "mem", far)}
    winds = [{k: x[i * rows : (i + 1) * rows] for k, x in both.items()} for i in range(2)]
    for wind in winds:
        wind[near] = swap(wind[0], "mem", near)
        wind[far + near] = swap(wind[far], "mem", near)
    inner, outer = ([x[k] for k in range(count_mem)] for x in (inner, outer))
    winds = [wind[k] for wind in winds for k in range(count_mem)]

    half = (total // 4 + 2) // 2
    devices = count * count_mem
    part = jax.ShapeDtypeStruct((half, 1, 2 * total), F32)
    keep, give = pl.pallas_call(
        functools.partial(gram_kernel, outer_rows, scale, far, count_mem, peers),
        out_shape=(part, part),
        in_specs=[VMEM] * (far + 6 + len(direct)),
        out_specs=(VMEM, VMEM),
        scratch_shapes=[
            split(outer_rows),
            pltpu.VMEM((2 * total, share * width), F32),
            pltpu.VMEM((count,) + near_shape[1:], F32),
        ],
        name="gram",
        compiler_params=PARAMS,
        cost_estimate=cost(1000, 1000),
    )(owners, *outer[far:], obs_cells, obs_weights, near_blocks, first, second, *direct)
    sent = jnp.broadcast_to(keep + swap(give, "mem", near), (devices,) + part.shape)
    sums = lax.all_to_all(sent, ("space", "mem"), split_axis=0, concat_axis=0, tiled=True)

    return pl.pallas_call(
        functools.partial(analysis_kernel, count_mem),
        out_shape=jax.ShapeDtypeStruct(state.shape, F32),
        in_specs=[VMEM] * (1 + 4 * count_mem),
        out_specs=VMEM,
        scratch_shapes=[pltpu.VMEM((total, 2 * total), F32)],
        compiler_params=PARAMS,
        name="analysis",
    )(sums, *inner, *outer, *winds)


def solution(mesh):
    return jax.shard_map(
        local,
        mesh=mesh,
        in_specs=(
            P("mem", None, "space", None),
            P("space", None),
            P(None, "space", None),
            P(None, "space", None),
            P("space", None),
            P("space", None, None, None),
            P("space", None, None, None),
        ),
        out_specs=P("mem", None, "space", None),
        check_vma=False,
    )
```

```python
import functools
import math

import jax
import jax.numpy as jnp
from jax import lax
from jax.experimental import pallas as pl
from jax.experimental.pallas import tpu as pltpu
from jax.sharding import PartitionSpec as P

mass_rate = 0.2
wave_rate = 0.2
turn_rate = 0.1

ANY = pl.BlockSpec(memory_space=pl.ANY)
VMEM = pl.BlockSpec(memory_space=pltpu.VMEM)
HBM = pl.BlockSpec(memory_space=pltpu.HBM)
SMEM = pl.BlockSpec(memory_space=pltpu.SMEM)
F32 = jnp.float32
BF16 = jnp.bfloat16
PARAMS = pltpu.CompilerParams(vmem_limit_bytes=12 * 1024 * 1024)
FORECAST_FLOPS = 2 * 10**9
RIM = 3


def hold(arrays, *others):
    return pl.pallas_call(
        lambda *refs: None,
        out_shape=tuple(jax.ShapeDtypeStruct(x.shape, x.dtype) for x in arrays),
        in_specs=[ANY] * (len(arrays) + len(others)),
        out_specs=(ANY,) * len(arrays),
        input_output_aliases={i: i for i in range(len(arrays))},
        compiler_params=PARAMS,
        cost_estimate=cost(1, 1),
        name="hold",
    )(*arrays, *others)


def cost(flops, size):
    return pl.CostEstimate(flops=flops, bytes_accessed=size, transcendentals=0)


def diff_cols(field):
    width = field.shape[-1]
    return pltpu.roll(field, width - 1, 1) - pltpu.roll(field, 1, 1)


def far_shift(index):
    half = 2 + index // 2
    return half - 2 * half * (index % 2)


def edge_kernel(peers, state_in, depth_in, values, precision, above, below, own, *refs):
    held = refs[:-5]
    state, depth, seen, weight, sems = refs[-5:]
    members, _, rows, cols = state.shape
    width = values.shape[-1]
    half = members // 2
    copies = [
        pltpu.make_async_copy(state_in.at[0:half], state.at[0:half], sems.at[0]),
        pltpu.make_async_copy(state_in.at[half:members], state.at[half:members], sems.at[1]),
        pltpu.make_async_copy(depth_in, depth, sems.at[2]),
    ]
    place, count = lax.axis_index("space"), values.shape[1]
    peers_of = [place, lax.rem(place + count - 1, count), lax.rem(place + 1, count)]
    quarters = lax.axis_size("mem")
    for j in range(peers):
        index = j * quarters + lax.axis_index("mem")
        half = 2 + lax.div(index, 2)
        shift = half - 2 * half * lax.rem(index, 2)
        peers_of.append(lax.rem(place + 2 * count - shift, count))
    for index in range(peers * quarters, count - 3):
        peers_of.append(lax.rem(place + 2 * count - far_shift(index), count))
    for j, peer in enumerate(peers_of):
        copies.append(pltpu.make_async_copy(values.at[0, peer], seen.at[j], sems.at[3 + 2 * j]))
        copies.append(pltpu.make_async_copy(precision.at[0, peer], weight.at[j], sems.at[4 + 2 * j]))
    for copy in copies:
        copy.start()
    for copy in copies:
        copy.wait()
    for out, sign, at in ((above, 1.0, range(4)), (below, -1.0, range(rows - 1, rows - 5, -1))):
        deep = [jnp.broadcast_to(depth[t : t + 1], (members, cols)) for t in at]
        h = [state[:, 0, t, :] for t in at]
        u = [state[:, 1, t, :] for t in at]
        v = [state[:, 2, t, :] for t in at]
        flux = [d * e for d, e in zip(deep, u)]
        first = h[0] - mass_rate * (sign * flux[1] + diff_cols(deep[0] * v[0]))
        second, third = (
            h[i] - mass_rate * (sign * (flux[i + 1] - flux[i - 1]) + diff_cols(deep[i] * v[i]))
            for i in (1, 2)
        )
        east = u[0] - wave_rate * sign * second + turn_rate * v[0]
        east_next = u[1] - wave_rate * sign * third + turn_rate * v[1]
        north = v[0] - turn_rate * u[0] - wave_rate * diff_cols(first)
        twice = first - mass_rate * (
            sign * deep[1] * (east_next + sign * wave_rate * first) + diff_cols(deep[0] * north)
        )
        for i, part in enumerate((flux[0], first, east, twice)):
            out[i * members : (i + 1) * members] = part
        out[4 * members : 4 * members + 8] = jnp.concatenate(
            [deep[0][0:1], deep[1][0:1], jnp.zeros((6, cols), F32)], axis=0
        )
    rim = 4 * members + 8
    slots = seen.shape[1]
    places = [own, above.at[rim : rim + slots], below.at[rim : rim + slots]] + list(held)
    for j, out in enumerate(places):
        out[:, 0:width] = seen[j]
        out[:, width : 2 * width] = weight[j]


def edges(peers, state, depth, values, precision):
    members, _, _, cols = state.shape
    slots = values.shape[2]
    rim = jax.ShapeDtypeStruct((4 * members + 8 + slots, cols), F32)
    held = jax.ShapeDtypeStruct((slots, cols), F32)
    owners = peers + (values.shape[1] - 3) % lax.axis_size("mem")
    return pl.pallas_call(
        functools.partial(edge_kernel, peers),
        out_shape=(rim, rim, held) + (held,) * owners,
        in_specs=[HBM] * 4,
        out_specs=(VMEM,) * (3 + owners),
        scratch_shapes=[
            pltpu.VMEM(state.shape, F32),
            pltpu.VMEM(depth.shape, F32),
            pltpu.VMEM((3 + owners,) + values.shape[2:], F32),
            pltpu.VMEM((3 + owners,) + values.shape[2:], F32),
            pltpu.SemaphoreType.DMA((9 + 2 * owners,)),
        ],
        compiler_params=pltpu.CompilerParams(vmem_limit_bytes=56 * 1024 * 1024),
        name="edges",
    )(state, depth, values, precision)


def inner_kernel(state, depth, out):
    members, _, rows, cols = state.shape
    deep = [jnp.broadcast_to(depth[t : t + 1], (members, cols)) for t in range(rows)]
    h = [state[:, 0, t, :] for t in range(rows)]
    u = [state[:, 1, t, :] for t in range(rows)]
    v = [state[:, 2, t, :] for t in range(rows)]
    for step in range(2):
        edge = 2 * step + 1
        flux = [d * e if e is not None else None for d, e in zip(deep, u)]
        new = [None] * rows
        for t in range(edge, rows - edge):
            new[t] = h[t] - mass_rate * (flux[t + 1] - flux[t - 1] + diff_cols(deep[t] * v[t]))
        h = new
        if step == 1:
            break
        east, north = [None] * rows, [None] * rows
        for t in range(edge + 1, rows - edge - 1):
            east[t] = u[t] - wave_rate * (h[t + 1] - h[t - 1]) + turn_rate * v[t]
            north[t] = v[t] - wave_rate * diff_cols(h[t]) - turn_rate * u[t]
        u, v = east, north
    for t in range(RIM, rows - RIM):
        out[t - RIM] = h[t]


def inner_heights(state, depth):
    members, _, rows, cols = state.shape
    return pl.pallas_call(
        inner_kernel,
        out_shape=jax.ShapeDtypeStruct((rows - 2 * RIM, members, cols), F32),
        in_specs=[VMEM] * 2,
        out_specs=VMEM,
        compiler_params=PARAMS,
        cost_estimate=cost(FORECAST_FLOPS, 4 * state.size),
        name="inner",
    )(state, depth)


def forecast_kernel(last, state, depth, above, below, *refs):
    held = refs[:-6]
    height_out, wind_out, h, u, v, flux = refs[-6:]
    members, _, rows, cols = state.shape
    slots = held[0].shape[0]
    deep = [jnp.broadcast_to(depth[t : t + 1], (members, cols)) for t in range(rows)]
    sides = []
    place = lax.axis_index("space")
    for ref, sign, edge, inside in (
        (above, -1.0, 0, place > 0),
        (below, 1.0, rows - 1, place < last),
    ):
        parts = [ref[i * members : (i + 1) * members] for i in range(4)]
        deeps = [
            jnp.broadcast_to(ref[4 * members + i : 4 * members + i + 1], (members, cols))
            for i in range(2)
        ]
        sides.append((parts, deeps, sign, edge, inside.astype(F32)))

    def outer(edge):
        return 0 if edge == 0 else rows + 1

    for t in range(rows):
        h[t + 1] = state[:, 0, t, :]
        u[t] = state[:, 1, t, :]
        v[t] = state[:, 2, t, :]
        flux[t + 1] = deep[t] * u[t]
    deltas = []
    for (first_flux, _, _, _), _, sign, edge, inside in sides:
        deltas.append(sign * mass_rate * flux[edge + 1])
        flux[outer(edge)] = first_flux * inside

    def new_heights():
        for t in range(rows):
            h[t + 1] = h[t + 1] - mass_rate * (flux[t + 2] - flux[t] + diff_cols(deep[t] * v[t]))

    def new_winds(put):
        for t in range(rows):
            east, north = u[t], v[t]
            put(
                t,
                east - wave_rate * (h[t + 2] - h[t]) + turn_rate * north,
                north - wave_rate * diff_cols(h[t + 1]) - turn_rate * east,
            )

    def keep(t, east, north):
        u[t], v[t] = east, north
        flux[t + 1] = deep[t] * east

    def emit(t, east, north):
        wind_out[t] = east
        wind_out[rows + t] = north

    new_heights()
    for delta, ((_, first, east, _), deeps, sign, edge, inside) in zip(deltas, sides):
        h[outer(edge)] = (first + delta) * inside
        flux[outer(edge)] = inside * deeps[0] * (east + sign * wave_rate * h[edge + 1])
    new_winds(keep)
    rims = []
    for delta, ((_, _, _, twice), deeps, sign, edge, inside) in zip(deltas, sides):
        turned = wave_rate * diff_cols(deeps[0] * diff_cols(delta))
        change = wave_rate * deeps[1] * delta - sign * flux[edge + 1] - turned
        rims.append((edge, (twice + delta - mass_rate * change) * inside))
    new_heights()
    for edge, rim in rims:
        h[outer(edge)] = rim
    new_winds(emit)
    outer_rows = list(range(RIM)) + list(range(rows - RIM, rows))
    for i, t in enumerate(outer_rows):
        height_out[i] = h[t + 1]
    for j, piece in enumerate(held):
        at = j * slots
        height_out[2 * RIM + at // members, at % members : at % members + slots, :] = piece[...]


def forecast(last, state, depth, above, below, held):
    members, _, rows, cols = state.shape
    extra = -(-len(held) * held[0].shape[0] // members)
    return pl.pallas_call(
        functools.partial(forecast_kernel, last),
        out_shape=(
            jax.ShapeDtypeStruct((2 * RIM + extra, members, cols), F32),
            jax.ShapeDtypeStruct((2 * rows, members, cols), F32),
        ),
        in_specs=[VMEM] * (4 + len(held)),
        out_specs=(VMEM, VMEM),
        scratch_shapes=[
            pltpu.VMEM((rows + 2, members, cols), F32),
            pltpu.VMEM((rows, members, cols), F32),
            pltpu.VMEM((rows, members, cols), F32),
            pltpu.VMEM((rows + 2, members, cols), F32),
        ],
        compiler_params=PARAMS,
        cost_estimate=cost(FORECAST_FLOPS, 4 * state.size),
        name="forecast",
    )(state, depth, above, below, *held)


def interpolate(groups, cells, weights, split, put):
    _, members, cols = groups[0][0][0].shape
    total = members * len(groups[0][0])
    points, blocks, width = cells.shape
    quarter = lax.axis_index("mem")
    blocks = blocks // lax.axis_size("mem")
    first = 0
    for pieces, lines_of in groups:
        for k, piece in enumerate(pieces):
            who = lax.bitwise_xor(lax.rem(quarter, len(pieces)), k)
            for r in range(len(lines_of)):
                x = piece[r]
                high = x.astype(BF16)
                low = (x - high.astype(F32)).astype(BF16)
                at = pl.ds(pl.multiple_of((first + r) * total + who * members, members), members)
                split[at, 0:cols] = high
                split[at, cols : 2 * cols] = low
        first += len(lines_of)

    def block(b, carry):
        results = [None] * len(groups)
        line = pl.ds(quarter * blocks + b, 1)
        for half in range(points // 2):
            cell = jnp.concatenate(
                [cells[2 * half, line, :], cells[2 * half + 1, line, :]], axis=1
            )
            share = jnp.concatenate(
                [weights[2 * half, line, :], weights[2 * half + 1, line, :]], axis=1
            )
            row = cell // cols
            col = jnp.broadcast_to(cell - row * cols, (cols, 2 * width))
            here = lax.broadcasted_iota(jnp.int32, (cols, 2 * width), 0) == col
            pick = jnp.where(here, 1.0, 0.0).astype(BF16)
            lines = jnp.dot(
                split[...], jnp.concatenate([pick, pick], axis=0), preferred_element_type=F32
            )
            first = 0
            for g, (_, lines_of) in enumerate(groups):
                for r, at in enumerate(lines_of):
                    term = lines[(first + r) * total : (first + r + 1) * total]
                    term = term * jnp.where(row == at, share, 0.0)
                    term = term[:, :width] + term[:, width:]
                    results[g] = term if results[g] is None else results[g] + term
                first += len(lines_of)
        put(b, *results)
        return carry

    lax.fori_loop(0, blocks, block, 0, unroll=16)


def collect(got, pieces):
    members = pieces[0].shape[1]
    rows = 2 * RIM
    slots = got.shape[1]
    peers = got.shape[0] // len(pieces)
    for k, piece in enumerate(pieces):
        for j in range(peers):
            at = j * slots
            got[k * peers + j] = piece[rows + at // members, at % members : at % members + slots, :]


def block_lines(owners, share, spaces, slots, peers):
    space, quarter = lax.axis_index("space"), lax.axis_index("mem")
    quarters = lax.axis_size("mem")
    shift = quarters.bit_length() - 1
    blocks = owners.shape[1]
    lane = lax.broadcasted_iota(jnp.int32, (share, blocks), 1)
    line = lax.broadcasted_iota(jnp.int32, (share, blocks), 0) + quarter * share
    row = jnp.broadcast_to(owners[...], (share, blocks)).astype(F32)
    mine = jnp.sum(jnp.where(lane == line, row, 0.0), axis=1, keepdims=True)
    slot = jnp.sum(jnp.where((row == mine) & (lane < line), 1.0, 0.0), axis=1, keepdims=True)
    apart = mine.astype(jnp.int32) - space
    apart = jnp.where(apart < 0, apart + spaces, apart)
    index = jnp.where(apart <= spaces // 2, 2 * (apart - 2), 2 * (spaces - apart - 2) + 1)
    who = lax.bitwise_xor(lax.bitwise_and(index, quarters - 1), quarter)
    spot = 3 + who * peers + lax.shift_right_arithmetic(index, shift)
    spot = jnp.where(index >= peers * quarters, 3 + index, spot)
    spot = jnp.where(apart <= 1, apart, spot)
    spot = jnp.where(apart == spaces - 1, 2, spot)
    return spot * slots + slot.astype(jnp.int32)


def near_inner_kernel(lines_of, count, *refs):
    pieces = refs[:count]
    cells, weights, owners, out, owners_out, split = refs[count:]
    owners_out[...] = owners[...]

    def put(b, result):
        out[b] = result

    interpolate([(pieces, lines_of)], cells, weights, split, put)


def middle_kernel(inner_rows, outer_rows, count, *refs):
    far, near = refs[:count], refs[count : 2 * count]
    cells, weights, early, own, above, below, out, out_far, got, split = refs[2 * count :]
    got[0] = own[...]
    rim = below.shape[0] - own.shape[0]
    got[1] = below[rim:]
    got[2] = above[rim:]
    collect(got.at[3:], near)

    def put(b, result_far, result):
        out_far[b] = result_far
        out[b] = result + early[b]

    interpolate([(far, inner_rows), (near, outer_rows)], cells, weights, split, put)


def gram_kernel(lines_of, scale, count, count_mem, peers, owners, *refs):
    pieces = refs[:count]
    cells, weights, near, early, early_far = refs[count : count + 5]
    direct = refs[count + 5 : -5]
    keep, give, split, lined, got = refs[-5:]
    _, members, cols = pieces[0].shape
    total = members * count_mem
    part = members * count
    blocks, width = cells.shape[1] // count_mem, cells.shape[2]
    quarter = lax.axis_index("mem")
    got[0 : near.shape[0]] = near[...]
    later = got.shape[0] - len(direct)
    collect(got.at[near.shape[0] : later], pieces)
    for i, piece in enumerate(direct):
        got[later + i] = piece[...]

    mine = quarter // count
    base = pl.multiple_of(mine * part, part)
    final = pl.multiple_of(lax.bitwise_xor(mine, 1) * part, part)

    def put(b, result):
        at = pl.ds(pl.multiple_of(b * width, width), width)
        lined[pl.ds(final, part), at] = result + early_far[b]
        lined[pl.ds(base, part), at] = early[b]

    interpolate([(pieces, lines_of)], cells, weights, split, put)
    lined[total : 2 * total] = jnp.zeros((total, blocks * width), F32)
    spaces, slots, across = got.shape
    picks = block_lines(owners, blocks, spaces, slots, peers)
    lane = lax.broadcasted_iota(jnp.int32, (blocks, spaces * slots), 1)
    taken = jnp.dot(
        jnp.where(lane == picks, 1.0, 0.0),
        got[...].reshape(spaces * slots, across),
        precision=lax.Precision.HIGHEST,
        preferred_element_type=F32,
    )
    for b in range(blocks):
        line = taken[b : b + 1]
        seen, much = line[:, 0:width], line[:, width : 2 * width] * scale
        at = pl.ds(b * width, width)
        values = lined[0:total, at]
        middle = jnp.sum(values, axis=0, keepdims=True) * (1.0 / total)
        lined[0:total, at] = (values - middle) * much
        lined[total : total + 1, at] = (seen - middle) * much

    x = lined[...]
    high = x.astype(BF16)
    low = (x - high.astype(F32)).astype(BF16)
    turned = (((1,), (1,)), ((), ()))
    gram = lax.dot_general(high, high, turned, preferred_element_type=F32)
    cross = lax.dot_general(high, low, turned, preferred_element_type=F32)
    gram = gram + (cross + cross.T)
    packed = pack_gram(gram, total)
    half = keep.shape[0]
    odd = lax.rem(quarter, 2) == 1
    for r in range(half):
        low, high = packed[r : r + 1], packed[half + r : half + r + 1]
        keep[r] = jnp.where(odd, high, low)
        give[r] = jnp.where(odd, low, high)


def spread_kernel(keep, given, out):
    both = keep[...] + given[...]
    for d in range(out.shape[0]):
        out[d] = both


def pack_gram(gram, total):
    half, quarter = total // 2, total // 4
    span = 2 * total
    top, low = gram[0:half], gram[half:total]
    lane = lax.broadcasted_iota(jnp.int32, (half, span), 1)
    line = lax.broadcasted_iota(jnp.int32, (half, span), 0)
    both = jnp.where(lane <= line, top, pltpu.roll(low, span - half, 1))
    wide = jnp.where(lane < half, both, pltpu.roll(low, half, 1))
    lane_q = lane[0:quarter]
    body = jnp.where(lane_q < total, wide[0:quarter], pltpu.roll(wide[quarter:half], total, 1))
    diag = jnp.sum(jnp.where(lane == line + half, low, 0.0), axis=0, keepdims=True)
    lane_1 = lane[0:8]
    tail = jnp.where(
        lane_1 < total, gram[total : total + 8], pltpu.roll(jnp.broadcast_to(diag, (8, span)), half, 1)
    )
    return jnp.concatenate([body, tail], axis=0)


def unpack_gram(packed, total):
    half, quarter = total // 2, total // 4
    span = 2 * total
    body, tail = packed[0:quarter], packed[quarter : quarter + 1]
    wide = jnp.concatenate([body, pltpu.roll(body, total, 1)], axis=0)
    low = pltpu.roll(wide, span - half, 1)
    lane = lax.broadcasted_iota(jnp.int32, (half, span), 1)
    line = lax.broadcasted_iota(jnp.int32, (half, span), 0)
    first = lane < half
    stacked = jnp.concatenate(
        [jnp.where(first, wide, 0.0), jnp.where(first, low, 0.0), jnp.zeros((total, span), F32)], axis=0
    )
    turned = stacked.T[0:half]
    top = jnp.where(first & (lane <= line), wide, turned)
    diag = pltpu.roll(jnp.broadcast_to(tail, (half, span)), span - half, 1)
    corner = jnp.where(lane > line, wide, turned)
    corner = pltpu.roll(jnp.where(first, corner, 0.0), half, 1)
    corner = jnp.where(lane == line + half, diag, corner)
    bottom = jnp.where(first, low, corner)
    return jnp.concatenate([top, bottom], axis=0), tail


def factor_inverse(system, total):
    span = 2 * total
    lane = lax.broadcasted_iota(jnp.int32, (total, span), 1)
    line = lax.broadcasted_iota(jnp.int32, (total, span), 0)
    work = jnp.where(lane < total, system, jnp.where(lane == line + total, 1.0, 0.0))
    tiles = [work[8 * g : 8 * g + 8] for g in range(total // 8)]
    step = 8
    below = lax.broadcasted_iota(jnp.int32, (8, span), 0)

    def lanes(x, k):
        return jnp.broadcast_to(x[:, k : k + 1], (8, span))

    def lines(x, s):
        return jnp.broadcast_to(x[s : s + 1], (8, span))

    for k in range(0, total, step):
        g, s = k // 8, k % 8
        columns = {t: [lanes(tiles[t], k + i) for i in range(step)] for t in range(g, total // 8)}
        pivots = [lines(tiles[g], s + i) for i in range(step)]
        block = [[lines(columns[g][j], s + i) for j in range(i + 1)] for i in range(step)]
        for j in range(step):
            scale = 1.0 / block[j][j]
            ratio = [None] * step
            for i in range(j + 1, step):
                ratio[i] = block[i][j] * scale
            for i in range(j + 1, step):
                for n in range(j + 1, i + 1):
                    block[i][n] = block[i][n] - ratio[i] * block[n][j]
                pivots[i] = pivots[i] - ratio[i] * pivots[j]
            scaled = pivots[j] * scale
            for t in columns:
                for i in range(j + 1, step):
                    columns[t][i] = columns[t][i] - ratio[i] * columns[t][j]
            for t in columns:
                column = columns[t][j]
                if t == g:
                    if s + j == 7:
                        continue
                    column = jnp.where(below > s + j, column, 0.0)
                tiles[t] = tiles[t] - column * scaled
    work = jnp.concatenate(tiles, axis=0)
    diag = jnp.sum(jnp.where(lane == line, work, 0.0), axis=1, keepdims=True)
    return jnp.where(lane < total, pltpu.roll(work, total, 1), 0.0) / jnp.sqrt(diag)


def mixing_columns(packed, total, members, count_mem, lower):
    span = 2 * total
    quarter = lax.axis_index("mem")
    system, proj = unpack_gram(packed, total)
    lane = lax.broadcasted_iota(jnp.int32, (total, span), 1)
    line = lax.broadcasted_iota(jnp.int32, (total, span), 0)
    inverse = factor_inverse(system + jnp.where(lane == line, float(total - 1), 0.0), total)
    first = jnp.sum(jnp.where(lane < total, inverse * proj, 0.0), axis=1, keepdims=True)
    mean_weights = jnp.sum(inverse * first, axis=0, keepdims=True)
    lower[...] = inverse
    mine = lower[pl.ds(pl.multiple_of(quarter * members, members), members)]
    coef = mean_weights + math.sqrt(total - 1) * mine
    short = lane[0:members]
    coef = jnp.where(short < total, coef, 0.0)
    mixing = coef + (1.0 - jnp.sum(coef, axis=1, keepdims=True)) * (1.0 / total)
    bit = 1
    while bit < count_mem:
        size = bit * members
        turned = jnp.where(
            lax.rem(short // size, 2) == 0, pltpu.roll(mixing, span - size, 1), pltpu.roll(mixing, size, 1)
        )
        swapped = (lax.rem(quarter // bit, 2) == 1).astype(F32)
        mixing = mixing + swapped * (turned - mixing)
        bit *= 2
    return mixing[:, 0:total]


def analysis_kernel(count_mem, sums, *refs):
    inner, outer = refs[:count_mem], refs[count_mem : 2 * count_mem]
    *both, east, north, out, lower = refs[2 * count_mem :]
    rows, members, cols = east.shape
    total = members * count_mem

    halves = [sums[0], sums[1]]
    for d in range(2, sums.shape[0]):
        halves[d % 2] = halves[d % 2] + sums[d]
    packed = jnp.concatenate([half[r] for half in halves for r in range(half.shape[0])], axis=0)
    mixing = mixing_columns(packed, total, members, count_mem, lower)
    high = mixing.astype(BF16)
    low = (mixing - high.astype(F32)).astype(BF16)
    left = jnp.concatenate([high, high, low], axis=1)
    for field in range(3):
        for r in range(rows):
            if field > 0:
                last = east if field == 1 else north
                pieces = [piece[(field - 1) * rows + r] for piece in both] + [last[r]]
            elif RIM <= r < rows - RIM:
                pieces = [piece[r - RIM] for piece in inner]
            else:
                pieces = [piece[r if r < RIM else r - rows + 2 * RIM] for piece in outer]
            upper = [x.astype(BF16) for x in pieces]
            rest = [(x - y.astype(F32)).astype(BF16) for x, y in zip(pieces, upper)]
            stack = jnp.concatenate(upper + rest + upper, axis=0)
            out[:, field, r, :] = jnp.dot(left, stack, preferred_element_type=F32)


def swap(x, axis, bit):
    count = lax.axis_size(axis)
    return lax.ppermute(x, axis, [(i, i ^ bit) for i in range(count)])


def after(x, *others):
    return lax.optimization_barrier((x,) + others)[0]


def local(state, depth, obs_cells, obs_weights, owner_map, obs_values, obs_precision):
    members, fields, rows, cols = state.shape
    count = lax.axis_size("space")
    count_mem = lax.axis_size("mem")
    total = members * count_mem
    blocks, width = obs_cells.shape[1:]
    share = blocks // count_mem
    scale = math.sqrt((total - 1) / (count * blocks * width))

    peers = (count - 3) // count_mem

    to_above, to_below, own, *blocks_out = edges(peers, state, depth, obs_values, obs_precision)
    ends = count - 1
    below = lax.ppermute(to_above, "space", [((i + 1) % count, i) for i in range(count)])
    above = lax.ppermute(to_below, "space", [(i, (i + 1) % count) for i in range(count)])
    held = [
        lax.ppermute(
            piece,
            ("space", "mem"),
            [
                (s * count_mem + q, (s - far_shift(j * count_mem + q)) % count * count_mem + q)
                for s in range(count)
                for q in range(count_mem)
            ],
        )
        for j, piece in enumerate(blocks_out[:peers])
    ]
    near, far = 1, count_mem // 2
    inner_rows = list(range(RIM, rows - RIM))
    outer_rows = list(range(RIM)) + list(range(rows - RIM, rows))
    early = jax.ShapeDtypeStruct((share, far * members, width), F32)
    owners = owner_map.reshape(1, blocks)

    def work(lines_of):
        return dict(
            compiler_params=PARAMS,
            cost_estimate=cost(
                4 * obs_cells.shape[0] * share * width * len(lines_of) * members * far * cols,
                4 * len(lines_of) * members * cols * far,
            ),
        )

    def split(lines_of):
        return pltpu.VMEM((len(lines_of) * far * members, 2 * cols), BF16)

    inner = {0: inner_heights(state, after(depth, to_above))}
    inner[near] = swap(inner[0], "mem", near)
    (inner[0],) = hold([inner[0]], inner[near])
    inner[far] = swap(inner[0], "mem", far)
    first, owners = pl.pallas_call(
        functools.partial(near_inner_kernel, inner_rows, far),
        out_shape=(early, jax.ShapeDtypeStruct(owners.shape, owners.dtype)),
        in_specs=[VMEM] * (far + 3),
        out_specs=(VMEM, VMEM),
        scratch_shapes=[split(inner_rows)],
        name="near_inner",
        **work(inner_rows),
    )(inner[0], inner[near], obs_cells, obs_weights, owners)

    above, below = (after(x, first) for x in (above, below))
    height, *parts = forecast(ends, state, depth, above, below, held)
    (inner[far],) = hold([inner[far]], height)
    inner[far + near] = swap(inner[far], "mem", near)
    outer = {0: height}
    outer[far] = swap(height, "mem", far)
    direct = []
    for i, piece in enumerate(blocks_out[peers:]):
        shift = far_shift(peers * count_mem + i)
        ring = [(s, (s - shift) % count) for s in range(count)]
        direct.append(lax.ppermute(after(piece, height), "space", ring))
    outer[near] = swap(height, "mem", near)
    outer[far + near] = swap(height, "mem", far + near)
    near_shape = (3 + far * peers, obs_values.shape[2], cols)
    first, second, near_blocks = pl.pallas_call(
        functools.partial(middle_kernel, inner_rows, outer_rows, far),
        out_shape=(early, early, jax.ShapeDtypeStruct(near_shape, F32)),
        in_specs=[VMEM] * (2 * far + 6),
        out_specs=(VMEM,) * 3,
        scratch_shapes=[split(inner_rows + outer_rows)],
        name="middle",
        **work(inner_rows + outer_rows),
    )(
        *[inner[k] for k in range(far, 2 * far)],
        *[outer[k] for k in range(far)],
        obs_cells,
        obs_weights,
        first,
        own,
        above,
        below,
    )
    both = [parts[0], swap(parts[0], "mem", near), swap(parts[0], "mem", far)]
    winds = both + [swap(both[2][i * rows : (i + 1) * rows], "mem", near) for i in range(2)]
    inner, outer = ([x[k] for k in range(count_mem)] for x in (inner, outer))

    half = (total // 4 + 2) // 2
    devices = count * count_mem
    part = jax.ShapeDtypeStruct((half, 1, 2 * total), F32)
    keep, give = pl.pallas_call(
        functools.partial(gram_kernel, outer_rows, scale, far, count_mem, peers),
        out_shape=(part, part),
        in_specs=[VMEM] * (far + 6 + len(direct)),
        out_specs=(VMEM, VMEM),
        scratch_shapes=[
            split(outer_rows),
            pltpu.VMEM((2 * total, share * width), F32),
            pltpu.VMEM((count,) + near_shape[1:], F32),
        ],
        name="gram",
        compiler_params=PARAMS,
        cost_estimate=cost(1000, 1000),
    )(owners, *outer[far:], obs_cells, obs_weights, near_blocks, first, second, *direct)
    sent = jnp.broadcast_to(keep + swap(give, "mem", near), (devices,) + part.shape)
    sums = lax.all_to_all(sent, ("space", "mem"), split_axis=0, concat_axis=0, tiled=True)

    return pl.pallas_call(
        functools.partial(analysis_kernel, count_mem),
        out_shape=jax.ShapeDtypeStruct(state.shape, F32),
        in_specs=[VMEM] * (1 + 2 * count_mem + len(winds)),
        out_specs=VMEM,
        scratch_shapes=[pltpu.VMEM((total, 2 * total), F32)],
        compiler_params=PARAMS,
        name="analysis",
    )(sums, *inner, *outer, *winds)


def solution(mesh):
    return jax.shard_map(
        local,
        mesh=mesh,
        in_specs=(
            P("mem", None, "space", None),
            P("space", None),
            P(None, "space", None),
            P(None, "space", None),
            P("space", None),
            P("space", None, None, None),
            P("space", None, None, None),
        ),
        out_specs=P("mem", None, "space", None),
        check_vma=False,
    )
```

```python
import functools
import math

import jax
import jax.numpy as jnp
from jax import lax
from jax.experimental import pallas as pl
from jax.experimental.pallas import tpu as pltpu
from jax.sharding import PartitionSpec as P

mass_rate = 0.2
wave_rate = 0.2
turn_rate = 0.1

ANY = pl.BlockSpec(memory_space=pl.ANY)
VMEM = pl.BlockSpec(memory_space=pltpu.VMEM)
HBM = pl.BlockSpec(memory_space=pltpu.HBM)
SMEM = pl.BlockSpec(memory_space=pltpu.SMEM)
F32 = jnp.float32
BF16 = jnp.bfloat16
PARAMS = pltpu.CompilerParams(vmem_limit_bytes=12 * 1024 * 1024)
FORECAST_FLOPS = 2 * 10**9
RIM = 3


def hold(arrays, *others):
    return pl.pallas_call(
        lambda *refs: None,
        out_shape=tuple(jax.ShapeDtypeStruct(x.shape, x.dtype) for x in arrays),
        in_specs=[ANY] * (len(arrays) + len(others)),
        out_specs=(ANY,) * len(arrays),
        input_output_aliases={i: i for i in range(len(arrays))},
        compiler_params=PARAMS,
        cost_estimate=cost(1, 1),
        name="hold",
    )(*arrays, *others)


def cost(flops, size):
    return pl.CostEstimate(flops=flops, bytes_accessed=size, transcendentals=0)


def diff_cols(field):
    width = field.shape[-1]
    return pltpu.roll(field, width - 1, 1) - pltpu.roll(field, 1, 1)


def far_shift(index):
    half = 2 + index // 2
    return half - 2 * half * (index % 2)


def edge_kernel(peers, state_in, depth_in, values, precision, above, below, own, *refs):
    held = refs[:-5]
    state, depth, seen, weight, sems = refs[-5:]
    members, _, rows, cols = state.shape
    width = values.shape[-1]
    half = members // 2
    copies = [
        pltpu.make_async_copy(state_in.at[0:half], state.at[0:half], sems.at[0]),
        pltpu.make_async_copy(state_in.at[half:members], state.at[half:members], sems.at[1]),
        pltpu.make_async_copy(depth_in, depth, sems.at[2]),
    ]
    place, count = lax.axis_index("space"), values.shape[1]
    peers_of = [place, lax.rem(place + count - 1, count), lax.rem(place + 1, count)]
    quarters = lax.axis_size("mem")
    for j in range(peers):
        index = j * quarters + lax.axis_index("mem")
        half = 2 + lax.div(index, 2)
        shift = half - 2 * half * lax.rem(index, 2)
        peers_of.append(lax.rem(place + 2 * count - shift, count))
    for index in range(peers * quarters, count - 3):
        peers_of.append(lax.rem(place + 2 * count - far_shift(index), count))
    for j, peer in enumerate(peers_of):
        copies.append(pltpu.make_async_copy(values.at[0, peer], seen.at[j], sems.at[3 + 2 * j]))
        copies.append(pltpu.make_async_copy(precision.at[0, peer], weight.at[j], sems.at[4 + 2 * j]))
    for copy in copies:
        copy.start()
    for copy in copies[:3]:
        copy.wait()
    for out, sign, at in ((above, 1.0, range(4)), (below, -1.0, range(rows - 1, rows - 5, -1))):
        deep = [jnp.broadcast_to(depth[t : t + 1], (members, cols)) for t in at]
        h = [state[:, 0, t, :] for t in at]
        u = [state[:, 1, t, :] for t in at]
        v = [state[:, 2, t, :] for t in at]
        flux = [d * e for d, e in zip(deep, u)]
        first = h[0] - mass_rate * (sign * flux[1] + diff_cols(deep[0] * v[0]))
        second, third = (
            h[i] - mass_rate * (sign * (flux[i + 1] - flux[i - 1]) + diff_cols(deep[i] * v[i]))
            for i in (1, 2)
        )
        east = u[0] - wave_rate * sign * second + turn_rate * v[0]
        east_next = u[1] - wave_rate * sign * third + turn_rate * v[1]
        north = v[0] - turn_rate * u[0] - wave_rate * diff_cols(first)
        twice = first - mass_rate * (
            sign * deep[1] * (east_next + sign * wave_rate * first) + diff_cols(deep[0] * north)
        )
        for i, part in enumerate((flux[0], first, east, twice)):
            out[i * members : (i + 1) * members] = part
        out[4 * members : 4 * members + 8] = jnp.concatenate(
            [deep[0][0:1], deep[1][0:1], jnp.zeros((6, cols), F32)], axis=0
        )
    for copy in copies[3:]:
        copy.wait()
    rim = 4 * members + 8
    slots = seen.shape[1]
    places = [own, above.at[rim : rim + slots], below.at[rim : rim + slots]] + list(held)
    for j, out in enumerate(places):
        out[:, 0:width] = seen[j]
        out[:, width : 2 * width] = weight[j]


def edges(peers, state, depth, values, precision):
    members, _, _, cols = state.shape
    slots = values.shape[2]
    rim = jax.ShapeDtypeStruct((4 * members + 8 + slots, cols), F32)
    held = jax.ShapeDtypeStruct((slots, cols), F32)
    owners = peers + (values.shape[1] - 3) % lax.axis_size("mem")
    return pl.pallas_call(
        functools.partial(edge_kernel, peers),
        out_shape=(rim, rim, held) + (held,) * owners,
        in_specs=[HBM] * 4,
        out_specs=(VMEM,) * (3 + owners),
        scratch_shapes=[
            pltpu.VMEM(state.shape, F32),
            pltpu.VMEM(depth.shape, F32),
            pltpu.VMEM((3 + owners,) + values.shape[2:], F32),
            pltpu.VMEM((3 + owners,) + values.shape[2:], F32),
            pltpu.SemaphoreType.DMA((9 + 2 * owners,)),
        ],
        compiler_params=pltpu.CompilerParams(vmem_limit_bytes=56 * 1024 * 1024),
        name="edges",
    )(state, depth, values, precision)


def inner_kernel(state, depth, out):
    members, _, rows, cols = state.shape
    deep = [jnp.broadcast_to(depth[t : t + 1], (members, cols)) for t in range(rows)]
    h = [state[:, 0, t, :] for t in range(rows)]
    u = [state[:, 1, t, :] for t in range(rows)]
    v = [state[:, 2, t, :] for t in range(rows)]
    for step in range(2):
        edge = 2 * step + 1
        flux = [d * e if e is not None else None for d, e in zip(deep, u)]
        new = [None] * rows
        for t in range(edge, rows - edge):
            new[t] = h[t] - mass_rate * (flux[t + 1] - flux[t - 1] + diff_cols(deep[t] * v[t]))
        h = new
        if step == 1:
            break
        east, north = [None] * rows, [None] * rows
        for t in range(edge + 1, rows - edge - 1):
            east[t] = u[t] - wave_rate * (h[t + 1] - h[t - 1]) + turn_rate * v[t]
            north[t] = v[t] - wave_rate * diff_cols(h[t]) - turn_rate * u[t]
        u, v = east, north
    for t in range(RIM, rows - RIM):
        out[t - RIM] = h[t]


def inner_heights(state, depth):
    members, _, rows, cols = state.shape
    return pl.pallas_call(
        inner_kernel,
        out_shape=jax.ShapeDtypeStruct((rows - 2 * RIM, members, cols), F32),
        in_specs=[VMEM] * 2,
        out_specs=VMEM,
        compiler_params=PARAMS,
        cost_estimate=cost(FORECAST_FLOPS, 4 * state.size),
        name="inner",
    )(state, depth)


def forecast_kernel(last, state, depth, above, below, *refs):
    held = refs[:-6]
    height_out, wind_out, h, u, v, flux = refs[-6:]
    members, _, rows, cols = state.shape
    slots = held[0].shape[0]
    deep = [jnp.broadcast_to(depth[t : t + 1], (members, cols)) for t in range(rows)]
    sides = []
    place = lax.axis_index("space")
    for ref, sign, edge, inside in (
        (above, -1.0, 0, place > 0),
        (below, 1.0, rows - 1, place < last),
    ):
        parts = [ref[i * members : (i + 1) * members] for i in range(4)]
        deeps = [
            jnp.broadcast_to(ref[4 * members + i : 4 * members + i + 1], (members, cols))
            for i in range(2)
        ]
        sides.append((parts, deeps, sign, edge, inside.astype(F32)))

    def outer(edge):
        return 0 if edge == 0 else rows + 1

    for t in range(rows):
        h[t + 1] = state[:, 0, t, :]
        u[t] = state[:, 1, t, :]
        v[t] = state[:, 2, t, :]
        flux[t + 1] = deep[t] * u[t]
    deltas = []
    for (first_flux, _, _, _), _, sign, edge, inside in sides:
        deltas.append(sign * mass_rate * flux[edge + 1])
        flux[outer(edge)] = first_flux * inside

    def new_heights():
        for t in range(rows):
            h[t + 1] = h[t + 1] - mass_rate * (flux[t + 2] - flux[t] + diff_cols(deep[t] * v[t]))

    def new_winds(put):
        for t in range(rows):
            east, north = u[t], v[t]
            put(
                t,
                east - wave_rate * (h[t + 2] - h[t]) + turn_rate * north,
                north - wave_rate * diff_cols(h[t + 1]) - turn_rate * east,
            )

    def keep(t, east, north):
        u[t], v[t] = east, north
        flux[t + 1] = deep[t] * east

    def emit(t, east, north):
        wind_out[t] = east
        wind_out[rows + t] = north

    new_heights()
    for delta, ((_, first, east, _), deeps, sign, edge, inside) in zip(deltas, sides):
        h[outer(edge)] = (first + delta) * inside
        flux[outer(edge)] = inside * deeps[0] * (east + sign * wave_rate * h[edge + 1])
    new_winds(keep)
    rims = []
    for delta, ((_, _, _, twice), deeps, sign, edge, inside) in zip(deltas, sides):
        turned = wave_rate * diff_cols(deeps[0] * diff_cols(delta))
        change = wave_rate * deeps[1] * delta - sign * flux[edge + 1] - turned
        rims.append((edge, (twice + delta - mass_rate * change) * inside))
    new_heights()
    for edge, rim in rims:
        h[outer(edge)] = rim
    new_winds(emit)
    outer_rows = list(range(RIM)) + list(range(rows - RIM, rows))
    for i, t in enumerate(outer_rows):
        height_out[i] = h[t + 1]
    for j, piece in enumerate(held):
        at = j * slots
        height_out[2 * RIM + at // members, at % members : at % members + slots, :] = piece[...]


def forecast(last, state, depth, above, below, held):
    members, _, rows, cols = state.shape
    extra = -(-len(held) * held[0].shape[0] // members)
    return pl.pallas_call(
        functools.partial(forecast_kernel, last),
        out_shape=(
            jax.ShapeDtypeStruct((2 * RIM + extra, members, cols), F32),
            jax.ShapeDtypeStruct((2 * rows, members, cols), F32),
        ),
        in_specs=[VMEM] * (4 + len(held)),
        out_specs=(VMEM, VMEM),
        scratch_shapes=[
            pltpu.VMEM((rows + 2, members, cols), F32),
            pltpu.VMEM((rows, members, cols), F32),
            pltpu.VMEM((rows, members, cols), F32),
            pltpu.VMEM((rows + 2, members, cols), F32),
        ],
        compiler_params=PARAMS,
        cost_estimate=cost(FORECAST_FLOPS, 4 * state.size),
        name="forecast",
    )(state, depth, above, below, *held)


def interpolate(groups, cells, weights, split, put):
    _, members, cols = groups[0][0][0].shape
    total = members * len(groups[0][0])
    points, blocks, width = cells.shape
    quarter = lax.axis_index("mem")
    blocks = blocks // lax.axis_size("mem")
    first = 0
    for pieces, lines_of in groups:
        for k, piece in enumerate(pieces):
            who = lax.bitwise_xor(lax.rem(quarter, len(pieces)), k)
            for r in range(len(lines_of)):
                x = piece[r]
                high = x.astype(BF16)
                low = (x - high.astype(F32)).astype(BF16)
                at = pl.ds(pl.multiple_of((first + r) * total + who * members, members), members)
                split[at, 0:cols] = high
                split[at, cols : 2 * cols] = low
        first += len(lines_of)

    def block(b, carry):
        results = [None] * len(groups)
        line = pl.ds(quarter * blocks + b, 1)
        for half in range(points // 2):
            cell = jnp.concatenate(
                [cells[2 * half, line, :], cells[2 * half + 1, line, :]], axis=1
            )
            share = jnp.concatenate(
                [weights[2 * half, line, :], weights[2 * half + 1, line, :]], axis=1
            )
            row = cell // cols
            col = jnp.broadcast_to(cell - row * cols, (cols, 2 * width))
            here = lax.broadcasted_iota(jnp.int32, (cols, 2 * width), 0) == col
            pick = jnp.where(here, 1.0, 0.0).astype(BF16)
            lines = jnp.dot(
                split[...], jnp.concatenate([pick, pick], axis=0), preferred_element_type=F32
            )
            first = 0
            for g, (_, lines_of) in enumerate(groups):
                for r, at in enumerate(lines_of):
                    term = lines[(first + r) * total : (first + r + 1) * total]
                    term = term * jnp.where(row == at, share, 0.0)
                    term = term[:, :width] + term[:, width:]
                    results[g] = term if results[g] is None else results[g] + term
                first += len(lines_of)
        put(b, *results)
        return carry

    lax.fori_loop(0, blocks, block, 0, unroll=16)


def collect(got, pieces):
    members = pieces[0].shape[1]
    rows = 2 * RIM
    slots = got.shape[1]
    peers = got.shape[0] // len(pieces)
    for k, piece in enumerate(pieces):
        for j in range(peers):
            at = j * slots
            got[k * peers + j] = piece[rows + at // members, at % members : at % members + slots, :]


def block_lines(owners, share, spaces, slots, peers):
    space, quarter = lax.axis_index("space"), lax.axis_index("mem")
    quarters = lax.axis_size("mem")
    shift = quarters.bit_length() - 1
    blocks = owners.shape[1]
    lane = lax.broadcasted_iota(jnp.int32, (share, blocks), 1)
    line = lax.broadcasted_iota(jnp.int32, (share, blocks), 0) + quarter * share
    row = jnp.broadcast_to(owners[...], (share, blocks)).astype(F32)
    mine = jnp.sum(jnp.where(lane == line, row, 0.0), axis=1, keepdims=True)
    slot = jnp.sum(jnp.where((row == mine) & (lane < line), 1.0, 0.0), axis=1, keepdims=True)
    apart = mine.astype(jnp.int32) - space
    apart = jnp.where(apart < 0, apart + spaces, apart)
    index = jnp.where(apart <= spaces // 2, 2 * (apart - 2), 2 * (spaces - apart - 2) + 1)
    who = lax.bitwise_xor(lax.bitwise_and(index, quarters - 1), quarter)
    spot = 3 + who * peers + lax.shift_right_arithmetic(index, shift)
    spot = jnp.where(index >= peers * quarters, 3 + index, spot)
    spot = jnp.where(apart <= 1, apart, spot)
    spot = jnp.where(apart == spaces - 1, 2, spot)
    return spot * slots + slot.astype(jnp.int32)


def near_inner_kernel(lines_of, count, *refs):
    pieces = refs[:count]
    cells, weights, owners, out, owners_out, split = refs[count:]
    owners_out[...] = owners[...]

    def put(b, result):
        out[b] = result

    interpolate([(pieces, lines_of)], cells, weights, split, put)


def middle_kernel(inner_rows, outer_rows, count, *refs):
    far, near = refs[:count], refs[count : 2 * count]
    cells, weights, early, own, above, below, out, out_far, got, split = refs[2 * count :]
    got[0] = own[...]
    rim = below.shape[0] - own.shape[0]
    got[1] = below[rim:]
    got[2] = above[rim:]
    collect(got.at[3:], near)

    def put(b, result_far, result):
        out_far[b] = result_far
        out[b] = result + early[b]

    interpolate([(far, inner_rows), (near, outer_rows)], cells, weights, split, put)


def gram_kernel(lines_of, scale, count, count_mem, peers, owners, *refs):
    pieces = refs[:count]
    cells, weights, near, early, early_far = refs[count : count + 5]
    direct = refs[count + 5 : -5]
    keep, give, split, lined, got = refs[-5:]
    _, members, cols = pieces[0].shape
    total = members * count_mem
    part = members * count
    blocks, width = cells.shape[1] // count_mem, cells.shape[2]
    quarter = lax.axis_index("mem")
    got[0 : near.shape[0]] = near[...]
    later = got.shape[0] - len(direct)
    collect(got.at[near.shape[0] : later], pieces)
    for i, piece in enumerate(direct):
        got[later + i] = piece[...]

    mine = quarter // count
    base = pl.multiple_of(mine * part, part)
    final = pl.multiple_of(lax.bitwise_xor(mine, 1) * part, part)

    def put(b, result):
        at = pl.ds(pl.multiple_of(b * width, width), width)
        lined[pl.ds(final, part), at] = result + early_far[b]
        lined[pl.ds(base, part), at] = early[b]

    interpolate([(pieces, lines_of)], cells, weights, split, put)
    lined[total : 2 * total] = jnp.zeros((total, blocks * width), F32)
    spaces, slots, across = got.shape
    picks = block_lines(owners, blocks, spaces, slots, peers)
    lane = lax.broadcasted_iota(jnp.int32, (blocks, spaces * slots), 1)
    taken = jnp.dot(
        jnp.where(lane == picks, 1.0, 0.0),
        got[...].reshape(spaces * slots, across),
        precision=lax.Precision.HIGHEST,
        preferred_element_type=F32,
    )
    for b in range(blocks):
        line = taken[b : b + 1]
        seen, much = line[:, 0:width], line[:, width : 2 * width] * scale
        at = pl.ds(b * width, width)
        values = lined[0:total, at]
        middle = jnp.sum(values, axis=0, keepdims=True) * (1.0 / total)
        lined[0:total, at] = (values - middle) * much
        lined[total : total + 1, at] = (seen - middle) * much

    x = lined[...]
    high = x.astype(BF16)
    low = (x - high.astype(F32)).astype(BF16)
    turned = (((1,), (1,)), ((), ()))
    gram = lax.dot_general(high, high, turned, preferred_element_type=F32)
    cross = lax.dot_general(high, low, turned, preferred_element_type=F32)
    gram = gram + (cross + cross.T)
    packed = pack_gram(gram, total)
    half = keep.shape[0]
    odd = lax.rem(quarter, 2) == 1
    for r in range(half):
        low, high = packed[r : r + 1], packed[half + r : half + r + 1]
        keep[r] = jnp.where(odd, high, low)
        give[r] = jnp.where(odd, low, high)


def spread_kernel(keep, given, out):
    both = keep[...] + given[...]
    for d in range(out.shape[0]):
        out[d] = both


def pack_gram(gram, total):
    half, quarter = total // 2, total // 4
    span = 2 * total
    top, low = gram[0:half], gram[half:total]
    lane = lax.broadcasted_iota(jnp.int32, (half, span), 1)
    line = lax.broadcasted_iota(jnp.int32, (half, span), 0)
    both = jnp.where(lane <= line, top, pltpu.roll(low, span - half, 1))
    wide = jnp.where(lane < half, both, pltpu.roll(low, half, 1))
    lane_q = lane[0:quarter]
    body = jnp.where(lane_q < total, wide[0:quarter], pltpu.roll(wide[quarter:half], total, 1))
    diag = jnp.sum(jnp.where(lane == line + half, low, 0.0), axis=0, keepdims=True)
    lane_1 = lane[0:8]
    tail = jnp.where(
        lane_1 < total, gram[total : total + 8], pltpu.roll(jnp.broadcast_to(diag, (8, span)), half, 1)
    )
    return jnp.concatenate([body, tail], axis=0)


def unpack_gram(packed, total):
    half, quarter = total // 2, total // 4
    span = 2 * total
    body, tail = packed[0:quarter], packed[quarter : quarter + 1]
    wide = jnp.concatenate([body, pltpu.roll(body, total, 1)], axis=0)
    low = pltpu.roll(wide, span - half, 1)
    lane = lax.broadcasted_iota(jnp.int32, (half, span), 1)
    line = lax.broadcasted_iota(jnp.int32, (half, span), 0)
    first = lane < half
    stacked = jnp.concatenate(
        [jnp.where(first, wide, 0.0), jnp.where(first, low, 0.0), jnp.zeros((total, span), F32)], axis=0
    )
    turned = stacked.T[0:half]
    top = jnp.where(first & (lane <= line), wide, turned)
    diag = pltpu.roll(jnp.broadcast_to(tail, (half, span)), span - half, 1)
    corner = jnp.where(lane > line, wide, turned)
    corner = pltpu.roll(jnp.where(first, corner, 0.0), half, 1)
    corner = jnp.where(lane == line + half, diag, corner)
    bottom = jnp.where(first, low, corner)
    return jnp.concatenate([top, bottom], axis=0), tail


def factor_inverse(system, total):
    span = 2 * total
    lane = lax.broadcasted_iota(jnp.int32, (total, span), 1)
    line = lax.broadcasted_iota(jnp.int32, (total, span), 0)
    work = jnp.where(lane < total, system, jnp.where(lane == line + total, 1.0, 0.0))
    tiles = [work[8 * g : 8 * g + 8] for g in range(total // 8)]
    step = 8
    below = lax.broadcasted_iota(jnp.int32, (8, span), 0)

    def lanes(x, k):
        return jnp.broadcast_to(x[:, k : k + 1], (8, span))

    def lines(x, s):
        return jnp.broadcast_to(x[s : s + 1], (8, span))

    for k in range(0, total, step):
        g, s = k // 8, k % 8
        columns = {t: [lanes(tiles[t], k + i) for i in range(step)] for t in range(g, total // 8)}
        pivots = [lines(tiles[g], s + i) for i in range(step)]
        block = [[lines(columns[g][j], s + i) for j in range(i + 1)] for i in range(step)]
        for j in range(step):
            scale = 1.0 / block[j][j]
            ratio = [None] * step
            for i in range(j + 1, step):
                ratio[i] = block[i][j] * scale
            for i in range(j + 1, step):
                for n in range(j + 1, i + 1):
                    block[i][n] = block[i][n] - ratio[i] * block[n][j]
                pivots[i] = pivots[i] - ratio[i] * pivots[j]
            scaled = pivots[j] * scale
            for t in columns:
                for i in range(j + 1, step):
                    columns[t][i] = columns[t][i] - ratio[i] * columns[t][j]
            for t in columns:
                column = columns[t][j]
                if t == g:
                    if s + j == 7:
                        continue
                    column = jnp.where(below > s + j, column, 0.0)
                tiles[t] = tiles[t] - column * scaled
    work = jnp.concatenate(tiles, axis=0)
    diag = jnp.sum(jnp.where(lane == line, work, 0.0), axis=1, keepdims=True)
    return jnp.where(lane < total, pltpu.roll(work, total, 1), 0.0) / jnp.sqrt(diag)


def mixing_columns(packed, total, members, count_mem, lower):
    span = 2 * total
    quarter = lax.axis_index("mem")
    system, proj = unpack_gram(packed, total)
    lane = lax.broadcasted_iota(jnp.int32, (total, span), 1)
    line = lax.broadcasted_iota(jnp.int32, (total, span), 0)
    inverse = factor_inverse(system + jnp.where(lane == line, float(total - 1), 0.0), total)
    first = jnp.sum(jnp.where(lane < total, inverse * proj, 0.0), axis=1, keepdims=True)
    mean_weights = jnp.sum(inverse * first, axis=0, keepdims=True)
    lower[...] = inverse
    mine = lower[pl.ds(pl.multiple_of(quarter * members, members), members)]
    coef = mean_weights + math.sqrt(total - 1) * mine
    short = lane[0:members]
    coef = jnp.where(short < total, coef, 0.0)
    mixing = coef + (1.0 - jnp.sum(coef, axis=1, keepdims=True)) * (1.0 / total)
    bit = 1
    while bit < count_mem:
        size = bit * members
        turned = jnp.where(
            lax.rem(short // size, 2) == 0, pltpu.roll(mixing, span - size, 1), pltpu.roll(mixing, size, 1)
        )
        swapped = (lax.rem(quarter // bit, 2) == 1).astype(F32)
        mixing = mixing + swapped * (turned - mixing)
        bit *= 2
    return mixing[:, 0:total]


def analysis_kernel(count_mem, sums, *refs):
    inner, outer, *winds = [refs[f * count_mem : (f + 1) * count_mem] for f in range(4)]
    out, lower = refs[4 * count_mem :]
    rows, members, cols = winds[0][0].shape
    total = members * count_mem

    halves = [sums[0], sums[1]]
    for d in range(2, sums.shape[0]):
        halves[d % 2] = halves[d % 2] + sums[d]
    packed = jnp.concatenate([half[r] for half in halves for r in range(half.shape[0])], axis=0)
    mixing = mixing_columns(packed, total, members, count_mem, lower)
    high = mixing.astype(BF16)
    low = (mixing - high.astype(F32)).astype(BF16)
    left = jnp.concatenate([high, high, low], axis=1)
    for field in range(3):
        for r in range(rows):
            if field > 0:
                pieces = [piece[r] for piece in winds[field - 1]]
            elif RIM <= r < rows - RIM:
                pieces = [piece[r - RIM] for piece in inner]
            else:
                pieces = [piece[r if r < RIM else r - rows + 2 * RIM] for piece in outer]
            upper = [x.astype(BF16) for x in pieces]
            rest = [(x - y.astype(F32)).astype(BF16) for x, y in zip(pieces, upper)]
            stack = jnp.concatenate(upper + rest + upper, axis=0)
            out[:, field, r, :] = jnp.dot(left, stack, preferred_element_type=F32)


def swap(x, axis, bit):
    count = lax.axis_size(axis)
    return lax.ppermute(x, axis, [(i, i ^ bit) for i in range(count)])


def after(x, *others):
    return lax.optimization_barrier((x,) + others)[0]


def local(state, depth, obs_cells, obs_weights, owner_map, obs_values, obs_precision):
    members, fields, rows, cols = state.shape
    count = lax.axis_size("space")
    count_mem = lax.axis_size("mem")
    total = members * count_mem
    blocks, width = obs_cells.shape[1:]
    share = blocks // count_mem
    scale = math.sqrt((total - 1) / (count * blocks * width))

    peers = (count - 3) // count_mem

    to_above, to_below, own, *blocks_out = edges(peers, state, depth, obs_values, obs_precision)
    ends = count - 1
    below = lax.ppermute(to_above, "space", [((i + 1) % count, i) for i in range(count)])
    above = lax.ppermute(to_below, "space", [(i, (i + 1) % count) for i in range(count)])
    held = [
        lax.ppermute(
            piece,
            ("space", "mem"),
            [
                (s * count_mem + q, (s - far_shift(j * count_mem + q)) % count * count_mem + q)
                for s in range(count)
                for q in range(count_mem)
            ],
        )
        for j, piece in enumerate(blocks_out[:peers])
    ]
    near, far = 1, count_mem // 2
    inner_rows = list(range(RIM, rows - RIM))
    outer_rows = list(range(RIM)) + list(range(rows - RIM, rows))
    early = jax.ShapeDtypeStruct((share, far * members, width), F32)
    owners = owner_map.reshape(1, blocks)

    def work(lines_of):
        return dict(
            compiler_params=PARAMS,
            cost_estimate=cost(
                4 * obs_cells.shape[0] * share * width * len(lines_of) * members * far * cols,
                4 * len(lines_of) * members * cols * far,
            ),
        )

    def split(lines_of):
        return pltpu.VMEM((len(lines_of) * far * members, 2 * cols), BF16)

    inner = {0: inner_heights(state, after(depth, to_above))}
    inner[near] = swap(inner[0], "mem", near)
    (inner[0],) = hold([inner[0]], inner[near])
    inner[far] = swap(inner[0], "mem", far)
    first, owners = pl.pallas_call(
        functools.partial(near_inner_kernel, inner_rows, far),
        out_shape=(early, jax.ShapeDtypeStruct(owners.shape, owners.dtype)),
        in_specs=[VMEM] * (far + 3),
        out_specs=(VMEM, VMEM),
        scratch_shapes=[split(inner_rows)],
        name="near_inner",
        **work(inner_rows),
    )(inner[0], inner[near], obs_cells, obs_weights, owners)

    above, below = (after(x, first) for x in (above, below))
    height, *parts = forecast(ends, state, depth, above, below, held)
    (inner[far],) = hold([inner[far]], height)
    inner[far + near] = swap(inner[far], "mem", near)
    outer = {0: height}
    outer[far] = swap(height, "mem", far)
    direct = []
    for i, piece in enumerate(blocks_out[peers:]):
        shift = far_shift(peers * count_mem + i)
        ring = [(s, (s - shift) % count) for s in range(count)]
        direct.append(lax.ppermute(after(piece, height), "space", ring))
    outer[near] = swap(height, "mem", near)
    outer[far + near] = swap(height, "mem", far + near)
    near_shape = (3 + far * peers, obs_values.shape[2], cols)
    first, second, near_blocks = pl.pallas_call(
        functools.partial(middle_kernel, inner_rows, outer_rows, far),
        out_shape=(early, early, jax.ShapeDtypeStruct(near_shape, F32)),
        in_specs=[VMEM] * (2 * far + 6),
        out_specs=(VMEM,) * 3,
        scratch_shapes=[split(inner_rows + outer_rows)],
        name="middle",
        **work(inner_rows + outer_rows),
    )(
        *[inner[k] for k in range(far, 2 * far)],
        *[outer[k] for k in range(far)],
        obs_cells,
        obs_weights,
        first,
        own,
        above,
        below,
    )
    both = {0: parts[0], far: swap(parts[0], "mem", far)}
    winds = [{k: x[i * rows : (i + 1) * rows] for k, x in both.items()} for i in range(2)]
    for wind in winds:
        wind[near] = swap(wind[0], "mem", near)
        wind[far + near] = swap(wind[far], "mem", near)
    inner, outer = ([x[k] for k in range(count_mem)] for x in (inner, outer))
    winds = [wind[k] for wind in winds for k in range(count_mem)]

    half = (total // 4 + 2) // 2
    devices = count * count_mem
    part = jax.ShapeDtypeStruct((half, 1, 2 * total), F32)
    keep, give = pl.pallas_call(
        functools.partial(gram_kernel, outer_rows, scale, far, count_mem, peers),
        out_shape=(part, part),
        in_specs=[VMEM] * (far + 6 + len(direct)),
        out_specs=(VMEM, VMEM),
        scratch_shapes=[
            split(outer_rows),
            pltpu.VMEM((2 * total, share * width), F32),
            pltpu.VMEM((count,) + near_shape[1:], F32),
        ],
        name="gram",
        compiler_params=PARAMS,
        cost_estimate=cost(1000, 1000),
    )(owners, *outer[far:], obs_cells, obs_weights, near_blocks, first, second, *direct)
    sent = jnp.broadcast_to(keep + swap(give, "mem", near), (devices,) + part.shape)
    sums = lax.all_to_all(sent, ("space", "mem"), split_axis=0, concat_axis=0, tiled=True)

    return pl.pallas_call(
        functools.partial(analysis_kernel, count_mem),
        out_shape=jax.ShapeDtypeStruct(state.shape, F32),
        in_specs=[VMEM] * (1 + 4 * count_mem),
        out_specs=VMEM,
        scratch_shapes=[pltpu.VMEM((total, 2 * total), F32)],
        compiler_params=PARAMS,
        name="analysis",
    )(sums, *inner, *outer, *winds)


def solution(mesh):
    return jax.shard_map(
        local,
        mesh=mesh,
        in_specs=(
            P("mem", None, "space", None),
            P("space", None),
            P(None, "space", None),
            P(None, "space", None),
            P("space", None),
            P("space", None, None, None),
            P("space", None, None, None),
        ),
        out_specs=P("mem", None, "space", None),
        check_vma=False,
    )
```
